32 devices in a mesh: dp: 8 (over z, x), sp: 4 (over y, core).
Axes of the slice: x: 2, y: 2, z: 4, core: 2. Of those that a mesh axis runs over, the one named last changes fastest.
Arguments:
- inputs: bfloat16 [16, 1024, 512], P('dp', 'sp'), may hold values from -6 to 6
- doc_lengths: int32 [16, 4], P('dp'), may hold values from 0 to 1024, as said below
- gain_attn: bfloat16 [2, 512], P(None, ('dp', 'sp')), may hold values from 0.5 to 1.5
- w_query: bfloat16 [2, 512, 512], P(None, ('dp', 'sp')), may hold values from -0.5 to 0.5
- w_key: bfloat16 [2, 512, 512], P(None, ('dp', 'sp')), may hold values from -0.25 to 0.25
- w_value: bfloat16 [2, 512, 512], P(None, ('dp', 'sp')), may hold values from -0.25 to 0.25
- w_out: bfloat16 [2, 512, 512], P(None, ('dp', 'sp')), may hold values from -1 to 1
- w_gate_attn: bfloat16 [2, 512, 512], P(None, ('dp', 'sp')), may hold values from -0.25 to 0.25
- b_gate_attn: bfloat16 [2, 512], P(None, ('dp', 'sp')), may hold values from -4 to 4
- gain_ffn: bfloat16 [2, 512], P(None, ('dp', 'sp')), may hold values from 0.5 to 1.5
- w_up: bfloat16 [2, 512, 2048], P(None, ('dp', 'sp')), may hold values from -0.25 to 0.25
- w_down: bfloat16 [2, 2048, 512], P(None, ('dp', 'sp')), may hold values from -0.1875 to 0.1875
- w_gate_ffn: bfloat16 [2, 512, 512], P(None, ('dp', 'sp')), may hold values from -0.25 to 0.25
- b_gate_ffn: bfloat16 [2, 512], P(None, ('dp', 'sp')), may hold values from -4 to 4
- cotangent: bfloat16 [16, 1024, 512], P('dp', 'sp'), may hold values from -6 to 6
Outputs:
- layer_out: bfloat16 [16, 1024, 512], P('dp', 'sp')
- input_grad: float32 [16, 1024, 512], P('dp', 'sp')
- grad_gain_attn: float32 [2, 512], P(None, ('dp', 'sp'))
- grad_w_query: float32 [2, 512, 512], P(None, ('dp', 'sp'))
- grad_w_key: float32 [2, 512, 512], P(None, ('dp', 'sp'))
- grad_w_value: float32 [2, 512, 512], P(None, ('dp', 'sp'))
- grad_w_out: float32 [2, 512, 512], P(None, ('dp', 'sp'))
- grad_w_gate_attn: float32 [2, 512, 512], P(None, ('dp', 'sp'))
- grad_b_gate_attn: float32 [2, 512], P(None, ('dp', 'sp'))
- grad_gain_ffn: float32 [2, 512], P(None, ('dp', 'sp'))
- grad_w_up: float32 [2, 512, 2048], P(None, ('dp', 'sp'))
- grad_w_down: float32 [2, 2048, 512], P(None, ('dp', 'sp'))
- grad_w_gate_ffn: float32 [2, 512, 512], P(None, ('dp', 'sp'))
- grad_b_gate_ffn: float32 [2, 512], P(None, ('dp', 'sp'))
The draws below stay inside these ranges and needn't reach their ends.
Inputs may be any that keep to these rules, and one draw needn't show every extreme that they name: `doc_lengths`: each row's lengths sum to 1024 or less; positions past the sum are padding. In every aligned block of 2 rows one row is a single document of 1024 tokens, the others hold 4 documents of one token or more.
All inputs are finite; a program needn't handle non-finite values.
Results may differ from the reference program's by a relative error of at most 0.023.
Values may be sent and summed in bfloat16 or wider, within the bound.
A program may use at most 192 MiB of HBM per device.

```python
import jax
import jax.numpy as jnp
from jax import lax

D = 512
HEADS = 8
HEAD_DIM = 64
FF = 2048
LEN = 1024
DOCS = 4
LAYERS = 2
SEQ_GRP = 2
SEQS = 16


def draw_doc_lengths(key, part):
    key = jax.random.fold_in(key, 7)
    key_weights, key_pad, key_long = jax.random.split(key, 3)
    weights = jax.random.randint(key_weights, (SEQS, DOCS), 1, 65)
    padding = jax.random.randint(key_pad, (SEQS, 1), 0, LEN // 8 + 1)
    used_len = LEN - padding
    shares = 1 + weights * (used_len - DOCS) // jnp.sum(weights, axis=1, keepdims=True)
    head_part = shares[:, :DOCS - 1]
    last_part = used_len - jnp.sum(head_part, axis=1, keepdims=True)
    drawn_rows = jnp.concatenate([head_part, last_part], axis=1)
    chosen = jax.random.randint(key_long, (SEQS // SEQ_GRP, 1), 0, SEQ_GRP)
    row_ids = jnp.arange(SEQS, dtype=jnp.int32).reshape(SEQS // SEQ_GRP, SEQ_GRP)
    long_row = (row_ids == chosen).reshape(SEQS, 1)
    single_doc = jnp.concatenate([jnp.full((SEQS, 1), LEN, jnp.int32), jnp.zeros((SEQS, DOCS - 1), jnp.int32)], axis=1)
    return jnp.where(long_row, single_doc, drawn_rows).astype(jnp.int32)


def with_spikes(drawn, stream_key, source, target, blocks, factor):
    def block_of(axis_at):
        return (jnp.arange(drawn.shape[axis_at]) // (drawn.shape[axis_at] // blocks)).reshape((-1,) + (1,) * (drawn.ndim - 1 - axis_at))

    one_side = jax.random.permutation(stream_key, blocks)[block_of(target)]
    far = (block_of(target) + blocks // 2) % blocks
    return jnp.where((block_of(source) == one_side) | (block_of(source) == far), factor * drawn, drawn)


def levels(stream_key, shape, shards, smallest, largest):
    factor_of = 1.0
    for dim, shards_of in shards:
        draws = jax.random.uniform(jax.random.fold_in(jax.random.fold_in(stream_key, 6), dim), (shards_of,), jnp.float32, smallest / len(shards), largest / len(shards))
        factor_of = factor_of * jnp.repeat(jnp.exp(draws), shape[dim] // shards_of).reshape((-1,) + (1,) * (len(shape) - 1 - dim))
    return factor_of


def centred(rng, dims, deviation, bound, pieces=(), kind=jnp.bfloat16):
    values = deviation * jax.random.normal(rng, dims, jnp.float32)
    if pieces:
        values = values * levels(rng, dims, pieces, -0.22, 0.18)
    return jnp.clip(values, -bound, bound).astype(kind)


def bell_draw_with(rng, extent, deviation, bound, shards, heavy, kind=jnp.bfloat16):
    values = deviation * jax.random.normal(rng, extent, jnp.float32)
    if shards:
        values = values * levels(rng, extent, shards, -0.22, 0.18)
    return jnp.clip(with_spikes(values, jax.random.fold_in(rng, 3), *heavy), -bound, bound).astype(kind)


def setup_inputs(seed: int = 0) -> dict:
    arg_keys = jax.random.split(jax.random.key(seed), 16)
    return {
        "inputs": centred(arg_keys[0], (SEQS, LEN, D), 1.0, 6.0, ((0, 8), (1, 4))),
        "doc_lengths": draw_doc_lengths(jax.random.fold_in(arg_keys[15], 71), 0),
        "gain_attn": jnp.clip(1.0 + 0.1 * jax.random.normal(arg_keys[2], (LAYERS, D), jnp.float32), 0.5, 1.5).astype(jnp.bfloat16),
        "w_query": centred(arg_keys[3], (LAYERS, D, D), (D // 4) ** -0.5, 0.5, ((1, 32),)),
        "w_key": centred(arg_keys[4], (LAYERS, D, D), D ** -0.5, 0.25, ((1, 32),)),
        "w_value": centred(arg_keys[5], (LAYERS, D, D), D ** -0.5, 0.25, ((1, 32),)),
        "w_out": centred(arg_keys[6], (LAYERS, D, D), (D // 16) ** -0.5, 1.0, ((1, 32),)),
        "w_gate_attn": centred(arg_keys[7], (LAYERS, D, D), D ** -0.5, 0.25, ((1, 32),)),
        "b_gate_attn": centred(arg_keys[8], (LAYERS, D), 1.0, 4.0, ((1, 32),)),
        "gain_ffn": jnp.clip(1.0 + 0.1 * jax.random.normal(arg_keys[9], (LAYERS, D), jnp.float32), 0.5, 1.5).astype(jnp.bfloat16),
        "w_up": centred(arg_keys[10], (LAYERS, D, FF), D ** -0.5, 0.25, ((1, 32),)),
        "w_down": centred(arg_keys[11], (LAYERS, FF, D), (FF // 2) ** -0.5, 0.1875, ((1, 32),)),
        "w_gate_ffn": centred(arg_keys[12], (LAYERS, D, D), D ** -0.5, 0.25, ((1, 32),)),
        "b_gate_ffn": centred(arg_keys[13], (LAYERS, D), 1.0, 4.0, ((1, 32),)),
        "cotangent": bell_draw_with(arg_keys[14], (SEQS, LEN, D), 1.0, 6.0, ((0, 8), (1, 4)), (0, 2, 8, 2.0)),
    }


EPSILON = 1e-05
NEG_FILL = -1e+30
PRECISE = lax.Precision.HIGHEST

@jax.custom_vjp
def low(v):
    return lax.optimization_barrier(v.astype(jnp.bfloat16)).astype(jnp.float32)

@jax.custom_vjp
def low_back(v):
    return v

def low_keep(v):
    return (low(v), None)

def low_pass(kept, grad):
    return (grad,)

def back_keep(v):
    return (v, None)

def back_low(kept, grad):
    return (low(grad),)
low.defvjp(low_keep, low_pass)
low_back.defvjp(back_keep, back_low)

def layer_norm(values, gain_vec):
    centre = lax.optimization_barrier(jnp.mean(values, axis=-1, keepdims=True))
    shifted = values - centre
    spread = lax.optimization_barrier(jnp.mean(shifted * shifted, axis=-1, keepdims=True))
    return shifted * lax.rsqrt(spread + EPSILON) * gain_vec

def linear(left_side, right_side):
    return jnp.einsum('bsi,ij->bsj', left_side, right_side, precision=PRECISE)

def allowed_pairs(lengths):
    doc_ends = jnp.cumsum(lengths, axis=1)
    places = jnp.arange(LEN, dtype=jnp.int32)
    segment_ids = lax.optimization_barrier(jnp.sum((places[None, :, None] >= doc_ends[:, None, :]).astype(jnp.int32), axis=2))
    is_live = places[None, :] < doc_ends[:, -1:]
    same_doc = segment_ids[:, :, None] == segment_ids[:, None, :]
    causal = places[:, None] >= places[None, :]
    diagonal = places[:, None] == places[None, :]
    return same_doc & causal[None] & is_live[:, None, :] | diagonal[None]

def one_layer(residual, allowed, layer_params):
    gain_a, w_query, w_key, w_value, w_out, w_gate_a, b_gate_a, gain_f, w_up, w_down, w_gate_f, b_gate_f = layer_params
    num_seqs = residual.shape[0]
    score_scale = HEAD_DIM ** (-0.5)
    hidden_a = low(layer_norm(residual, gain_a))
    queries = low(low_back(linear(hidden_a, w_query)) * score_scale).reshape(num_seqs, LEN, HEADS, HEAD_DIM)
    key_vecs = low(low_back(linear(hidden_a, w_key))).reshape(num_seqs, LEN, HEADS, HEAD_DIM)
    values = low(low_back(linear(hidden_a, w_value))).reshape(num_seqs, LEN, HEADS, HEAD_DIM)
    scores = low_back(jnp.einsum('bqhe,bkhe->bhqk', queries, key_vecs, precision=PRECISE))
    scores = jnp.where(allowed[:, None], scores, NEG_FILL)
    soft_w = low(jax.nn.softmax(scores, axis=-1))
    attn_mixed = jnp.einsum('bhqk,bkhe->bqhe', soft_w, values, precision=PRECISE)
    attn_mixed = low(low_back(attn_mixed)).reshape(num_seqs, LEN, D)
    branch_a = low_back(linear(attn_mixed, w_out))
    gate_a = jax.nn.sigmoid(low_back(linear(hidden_a, w_gate_a) + b_gate_a))
    after_a = residual + gate_a * branch_a
    hidden_f = low(layer_norm(after_a, gain_f))
    up_proj = low_back(linear(hidden_f, w_up))
    active = low(jax.nn.gelu(up_proj, approximate=True))
    branch_f = low_back(linear(active, w_down))
    gate_f = jax.nn.sigmoid(low_back(linear(hidden_f, w_gate_f) + b_gate_f))
    return after_a + gate_f * branch_f

def run_layers(seq_block, weights, allowed):
    for layer_idx in range(LAYERS):
        seq_block = one_layer(seq_block, allowed, tuple((weight_arr[layer_idx] for weight_arr in weights)))
    return seq_block

def reference(inputs, doc_lengths, gain_attn, w_query, w_key, w_value, w_out, w_gate_attn, b_gate_attn, gain_ffn, w_up, w_down, w_gate_ffn, b_gate_ffn, cotangent):
    params = tuple((weight_arr.astype(jnp.float32) for weight_arr in (gain_attn, w_query, w_key, w_value, w_out, w_gate_attn, b_gate_attn, gain_ffn, w_up, w_down, w_gate_ffn, b_gate_ffn)))
    groups = SEQS // 4
    token_blocks = inputs.astype(jnp.float32).reshape(groups, 4, LEN, D)
    length_blocks = doc_lengths.reshape(groups, 4, DOCS)
    cotan_blocks = cotangent.astype(jnp.float32).reshape(groups, 4, LEN, D)

    def accumulate(totals, scan_item):
        seq_block, lens_block, cotan_block = scan_item
        allowed = allowed_pairs(lens_block)

        def forward_pass(block_in, weights):
            return run_layers(block_in, weights, allowed)
        result, pull_back = jax.vjp(forward_pass, seq_block, params)
        grad_in, grad_params = pull_back(cotan_block)
        totals = jax.tree.map(jnp.add, totals, grad_params)
        return (totals, (result, grad_in))
    empty_grads = jax.tree.map(jnp.zeros_like, params)
    totals, (results, grads_in) = lax.scan(accumulate, empty_grads, (token_blocks, length_blocks, cotan_blocks))
    return (results.reshape(SEQS, LEN, D).astype(jnp.bfloat16), grads_in.reshape(SEQS, LEN, D), totals[0], totals[1], totals[2], totals[3], totals[4], totals[5], totals[6], totals[7], totals[8], totals[9], totals[10], totals[11])
```

```python
from functools import partial
from types import SimpleNamespace

import jax
import jax.numpy as jnp
from jax import lax
from jax.experimental import pallas as pl
from jax.experimental.pallas import tpu as pltpu
from jax.sharding import PartitionSpec as P

LEN = 1024
LAYERS = 2
WIDTH = 512
HEAD_DIM = 64
BLOCK = 128
SLOTS = LEN // (2 * BLOCK)
TOKENS = SLOTS * BLOCK
HALF = TOKENS // 2
PAIRS = WIDTH // (2 * HEAD_DIM)
CHUNKS = 4
EPSILON = 1e-05
NEG_FILL = -1e30
F32 = jnp.float32
BF = jnp.bfloat16
MESH = pl.DeviceIdType.MESH
VMEM_BYTES = 56 * 1024 * 1024
BACKWARD_VMEM = 62 * 1024 * 1024

ANY = pl.BlockSpec(memory_space=pl.ANY)
VMEM = pl.BlockSpec(memory_space=pltpu.VMEM)
SMEM = pl.BlockSpec(memory_space=pltpu.SMEM)

SETS = (
    (("k", "v"), (1, 2)),
    (("q", "ga"), (2, 1)),
    (("o", "gf", "up0", "up1", "up2", "up3"), (2, 1)),
    (("down",), (1, 2)),
)
VEC_UNIT = len(SETS[0][0])
UNITS_A = 7
UNITS_B = 3


class Place:
    def __init__(self, dims):
        self.dims = dims
        num_z, num_x, num_y = dims
        self.dp = lax.axis_index("dp")
        self.sp = lax.axis_index("sp")
        self.at = (
            lax.div(self.dp, num_x),
            lax.rem(self.dp, num_x),
            lax.div(self.sp, 2),
            lax.rem(self.sp, 2),
        )
        self.z, self.x, self.y, self.core = self.at

    def device(self, axis=None, position=None):
        z, x, y, core = [position if k == axis else v for k, v in enumerate(self.at)]
        return (z * self.dims[1] + x, y * 2 + core)

    def sibling(self):
        return self.device(3, 1 - self.core)

    def greet(self):
        barrier = pltpu.get_barrier_semaphore()
        count = jnp.int32(0)
        for axis in (0, 1):
            reach = self.dims[0] - 1 if axis == 0 else 1
            for step in [s for s in range(-reach, reach + 1) if s]:
                position = self.at[axis] + step
                there = (position >= 0) & (position < self.dims[axis])

                @pl.when(there)
                def _(axis=axis, position=position):
                    pl.semaphore_signal(
                        barrier, inc=1, device_id=self.device(axis, position), device_id_type=MESH
                    )

                count = count + there.astype(jnp.int32)
        num_sp = self.dims[2] * 2
        for step in range(1, num_sp):
            other = lax.rem(self.sp + step, num_sp)
            pl.semaphore_signal(barrier, inc=1, device_id=(self.dp, other), device_id_type=MESH)
        pl.semaphore_wait(barrier, count + (num_sp - 1))


def remote(src, dst, send_sem, recv_sem, device):
    return pltpu.make_async_remote_copy(
        src_ref=src,
        dst_ref=dst,
        send_sem=send_sem,
        recv_sem=recv_sem,
        device_id=device,
        device_id_type=MESH,
    )


def when(cond, action):
    if cond is True:
        action()
    elif cond is not False:
        pl.when(cond)(action)


def both(*conds):
    out = True
    for cond in conds:
        if cond is False:
            return False
        if cond is not True:
            out = cond if out is True else out & cond
    return out


class GatherSet:
    def __init__(self, place, ref, order, sems):
        self.place, self.ref, self.order = place, ref, order
        self.z_send, self.z_recv, self.s_send, self.s_recv, self.c_send, self.c_recv = sems
        self.sends = []

    def put(self, src, send_sem, recv_sem, device, cond):
        copy = remote(src, src, send_sem, recv_sem, device)
        when(cond, copy.start)
        self.sends.append((cond, copy))

    def got(self, src, send_sem, recv_sem, cond):
        copy = remote(src, src, send_sem, recv_sem, self.place.sibling())
        when(cond, copy.wait_recv)

    def z_block(self, zb):
        return self.ref.at[:, zb, self.place.x, self.place.y, self.place.core]

    def stage_block(self, stage, zb, q):
        axis = self.order[stage]
        index = [zb, self.place.x, self.place.y, self.place.core]
        if stage == 1:
            index[self.order[0]] = slice(None)
        index[axis] = q
        return self.ref.at[(slice(None), *index)]

    def phase_z(self, t, side, zb, valid):
        num = self.place.dims[0]
        z = self.place.z
        if t > 0:
            self.got(self.z_block(zb), self.z_send.at[0, zb], self.z_recv.at[zb], valid)
        if (t == 0 or side == 0) and t <= num - 2:
            self.put(
                self.z_block(zb),
                self.z_send.at[1, zb],
                self.z_recv.at[zb],
                self.place.device(0, z + 1),
                both(valid, z < num - 1),
            )
        if (t == 0 or side == 1) and t <= num - 2:
            self.put(
                self.z_block(zb),
                self.z_send.at[0, zb],
                self.z_recv.at[zb],
                self.place.device(0, z - 1),
                both(valid, z > 0),
            )

    def stage_start(self, stage, zb, valid):
        axis = self.order[stage]
        p, num = self.place.at[axis], self.place.dims[axis]
        for way, cond in ((0, p > 0), (1, p < num - 1)):
            self.put(
                self.stage_block(stage, zb, p),
                self.s_send.at[stage, way, zb, p],
                self.s_recv.at[stage, zb, p],
                self.place.device(axis, p + 2 * way - 1),
                both(valid, cond),
            )

    def stage_finish(self, stage, zb, valid):
        axis = self.order[stage]
        p, num = self.place.at[axis], self.place.dims[axis]
        for u in range(1, num):
            for side in (0, 1):
                q = p - u if side == 0 else p + u
                there = both(valid, q >= 0 if side == 0 else q < num)
                block = self.stage_block(stage, zb, q)
                self.got(
                    block,
                    self.s_send.at[stage, side, zb, q],
                    self.s_recv.at[stage, zb, q],
                    there,
                )
                if u <= num - 2:
                    way = 1 - side
                    self.put(
                        block,
                        self.s_send.at[stage, way, zb, q],
                        self.s_recv.at[stage, zb, q],
                        self.place.device(axis, p + 2 * way - 1),
                        both(there, p < num - 1 if way == 1 else p > 0),
                    )

    def core_start(self, zb, valid):
        block = self.ref.at[:, zb, :, :, self.place.core]
        self.put(block, self.c_send.at[zb], self.c_recv.at[zb], self.place.sibling(), valid)

    def core_finish(self, zb, valid):
        block = self.ref.at[:, zb, :, :, 1 - self.place.core]
        self.got(block, self.c_send.at[zb], self.c_recv.at[zb], valid)

    def finish_sends(self):
        for cond, copy in self.sends:
            when(cond, copy.wait_send)


class PairGather:
    def __init__(self, place, ref, order, sems):
        self.place, self.ref, self.order = place, ref, order
        self.z_send, self.z_recv, self.s_send, self.s_recv, self.c_send, self.c_recv = sems
        self.sends = []

    def put(self, src, send_sem, recv_sem, device):
        copy = remote(src, src, send_sem, recv_sem, device)
        copy.start()
        self.sends.append(copy)

    def got(self, src, send_sem, recv_sem):
        remote(src, src, send_sem, recv_sem, self.place.sibling()).wait_recv()

    def own(self, zb):
        return self.ref.at[:, zb, self.place.x, self.place.y, self.place.core]

    def block(self, stage, zb, near):
        index = [zb, self.place.x, self.place.y, self.place.core]
        if stage == 1:
            index[self.order[0]] = slice(None)
        axis = self.order[stage]
        index[axis] = self.place.at[axis] if near else 1 - self.place.at[axis]
        return self.ref.at[(slice(None), *index)]

    def source(self, t):
        num = self.place.dims[0]
        return lax.rem(self.place.z + (num - t), num)

    def open(self):
        num = self.place.dims[0]
        z = self.place.z
        self.send_stage(0, 0)
        for t in range(1, num):
            target = lax.rem(z + t, num)
            self.put(
                self.own(z),
                self.z_send.at[t - 1],
                self.z_recv.at[t - 1],
                self.place.device(0, target),
            )

    def send_stage(self, stage, t):
        axis = self.order[stage]
        self.put(
            self.block(stage, self.source(t), True),
            self.s_send.at[stage, t],
            self.s_recv.at[stage, t],
            self.place.device(axis, 1 - self.place.at[axis]),
        )

    def got_stage(self, stage, t):
        block = self.block(stage, self.source(t), False)
        self.got(block, self.s_send.at[stage, t], self.s_recv.at[stage, t])

    def stage1(self, *steps):
        for t in steps:
            self.got(self.own(self.source(t)), self.z_send.at[t - 1], self.z_recv.at[t - 1])
            self.send_stage(0, t)

    def stage2(self, *steps):
        for t in steps:
            self.got_stage(0, t)
            self.send_stage(1, t)

    def stage3(self):
        for t in range(self.place.dims[0]):
            self.got_stage(1, t)
        block = self.ref.at[:, :, :, :, self.place.core]
        self.put(block, self.c_send, self.c_recv, self.place.sibling())

    def finish(self):
        block = self.ref.at[:, :, :, :, 1 - self.place.core]
        self.got(block, self.c_send, self.c_recv)

    def finish_sends(self):
        for copy in self.sends:
            copy.wait_send()


def pair_gather_sems(num_sets, num_z):
    dma = pltpu.SemaphoreType.DMA
    return [
        dma((num_sets, num_z - 1)),
        dma((num_sets, num_z - 1)),
        dma((num_sets, 2, num_z)),
        dma((num_sets, 2, num_z)),
        dma((num_sets,)),
        dma((num_sets,)),
    ]


class PairReduce:
    def __init__(self, place, ref, order, bufs, sems, result):
        self.place, self.ref, self.order, self.result = place, ref, order, result
        self.from_core, self.line1, self.line2, self.line_z = bufs
        self.c_send, self.c_recv, self.s_send, self.s_recv, self.z_send, self.z_recv = sems
        self.sends = []

    def put(self, src, dst, send_sem, recv_sem, device):
        copy = remote(src, dst, send_sem, recv_sem, device)
        copy.start()
        return copy

    def cut(self, core, x=slice(None), y=slice(None)):
        return self.ref.at[:, :, x, y, core]

    def axis_cut(self, stage, near):
        at = [slice(None), slice(None), slice(None)]
        if stage == 1:
            at[self.order[0]] = self.place.at[self.order[0]]
        axis = self.order[stage]
        at[axis] = self.place.at[axis] if near else 1 - self.place.at[axis]
        return self.cut(self.place.core, at[1], at[2])

    def wait(self, buf, send_sem, recv_sem):
        remote(buf, buf, send_sem, recv_sem, self.place.sibling()).wait_recv()

    def start(self):
        copy = self.put(
            self.cut(1 - self.place.core),
            self.from_core,
            self.c_send,
            self.c_recv,
            self.place.sibling(),
        )
        self.sends.append(copy)

    def send_stage(self, stage):
        axis = self.order[stage]
        copy = self.put(
            self.axis_cut(stage, False),
            (self.line1, self.line2)[stage],
            self.s_send.at[stage],
            self.s_recv.at[stage],
            self.place.device(axis, 1 - self.place.at[axis]),
        )
        self.sends.append(copy)

    def stage1(self):
        self.wait(self.from_core, self.c_send, self.c_recv)
        add_units(self.cut(self.place.core), self.from_core)
        self.send_stage(0)

    def stage2(self):
        self.wait(self.line1, self.s_send.at[0], self.s_recv.at[0])
        add_units(self.axis_cut(0, True), self.line1)
        self.send_stage(1)

    def stage3(self):
        self.wait(self.line2, self.s_send.at[1], self.s_recv.at[1])
        place = self.place
        num = place.dims[0]
        add_units(self.axis_cut(1, True), self.line2)
        for t in range(num - 1, 0, -1):
            target = lax.rem(place.z + t, num)
            self.put(
                self.ref.at[:, target, place.x, place.y, place.core],
                self.line_z.at[t - 1],
                self.z_send,
                self.z_recv,
                place.device(0, target),
            )
        self.sends.append(
            remote(self.line_z, self.line_z, self.z_send, self.z_recv, place.sibling())
        )

    def finish(self):
        place = self.place
        mine = self.ref.at[:, place.z, place.x, place.y, place.core]
        self.wait(self.line_z, self.z_send, self.z_recv)
        for u in range(mine.shape[0]):
            value = mine[u].astype(F32)
            for slot in range(place.dims[0] - 1):
                value = value + self.line_z[slot, u].astype(F32)
            self.result(u, value)

    def finish_sends(self):
        for copy in self.sends:
            copy.wait_send()


def pair_reduce_sems(num_sets):
    dma = pltpu.SemaphoreType.DMA
    return [
        dma((num_sets,)),
        dma((num_sets,)),
        dma((num_sets, 2)),
        dma((num_sets, 2)),
        dma((num_sets,)),
        dma((num_sets,)),
    ]


def z_items(place, far_first):
    num = place.dims[0]
    order = range(num - 1, -1, -1) if far_first else range(num)
    rounds = []
    for t in order:
        if t == 0:
            rounds.append([(0, 0, place.z, True)])
        else:
            rounds.append(
                [(t, 0, place.z - t, place.z - t >= 0), (t, 1, place.z + t, place.z + t < num)]
            )
    return rounds


def pipeline(rounds, phases):
    for k in range(len(rounds) + len(phases) - 1):
        for lag, phase in enumerate(phases):
            if 0 <= k - lag < len(rounds):
                for item in rounds[k - lag]:
                    phase(*item)


def gather_sems(num_sets, dims):
    num_z, num_x, num_y = dims
    line = max(num_x, num_y)
    dma = pltpu.SemaphoreType.DMA
    return [
        dma((num_sets, 2, num_z)),
        dma((num_sets, num_z)),
        dma((num_sets, 2, 2, num_z, line)),
        dma((num_sets, 2, num_z, line)),
        dma((num_sets, num_z)),
        dma((num_sets, num_z)),
    ]


def set_sems(sems, k):
    return [sem.at[k] for sem in sems]


def run_gather(place, sets):
    def each(method):
        def phase(t, side, zb, valid):
            for one in sets:
                method(one, t, side, zb, valid)

        return phase

    def phase_one(one, t, side, zb, valid):
        one.phase_z(t, side, zb, valid)
        one.stage_start(0, zb, valid)

    def phase_two(one, t, side, zb, valid):
        one.stage_finish(0, zb, valid)
        one.stage_start(1, zb, valid)

    def phase_three(one, t, side, zb, valid):
        one.stage_finish(1, zb, valid)
        one.core_start(zb, valid)

    def phase_four(one, t, side, zb, valid):
        one.core_finish(zb, valid)

    pipeline(
        z_items(place, False), [each(phase_one), each(phase_two), each(phase_three), each(phase_four)]
    )
    for one in sets:
        one.finish_sends()


def own_shards(weights, vecs, layer):
    wq, wk, wv, wo, wga, wgf, wup, wdown = weights
    plain = {"q": wq, "k": wk, "v": wv, "o": wo, "ga": wga, "gf": wgf, "down": wdown}
    out = []
    for which, (names, _) in enumerate(SETS):
        for unit, name in enumerate(names):
            if name in plain:
                out.append((which, unit, plain[name].at[layer]))
            else:
                out.append((which, unit, wup.at[layer, :, pl.ds(int(name[2:]) * WIDTH, WIDTH)]))
    if layer == 0 and vecs is not None:
        out.append((0, VEC_UNIT, vecs))
    return out


OWN_COPIES = LAYERS * sum(len(names) for names, _ in SETS) + 1


def set_shapes(dims, rows):
    shapes = []
    for layer in range(LAYERS):
        for which, (names, _) in enumerate(SETS):
            count = len(names) + (layer == 0 and which == 0)
            depth = 4 * rows if names[0] == "down" else rows
            shapes.append((count, *dims, 2, depth, WIDTH))
    return shapes


def start_own(place, weights, vecs, refs, sem, layers=range(LAYERS), first=0):
    copies = []
    for layer in layers:
        for which, unit, src in own_shards(weights, vecs, layer):
            dst = refs[layer * len(SETS) + which].at[(unit, *place.at)]
            copy = pltpu.make_async_copy(src, dst, sem.at[first + len(copies)])
            copy.start()
            copies.append(copy)
    return copies


def gather_sets(place, refs, sems):
    return [
        GatherSet(place, ref, SETS[k % len(SETS)][1], set_sems(sems, k)) for k, ref in enumerate(refs)
    ]


class TokenMove:
    def __init__(self, place, num_seqs, src, dst_slot, sems, which):
        self.place, self.num_seqs, self.src, self.dst_slot = place, num_seqs, src, dst_slot
        self.send_sem, self.recv_sem, self.local_sem = (s.at[which] for s in sems)
        self.per_dev = LEN // (place.dims[2] * 2) // BLOCK
        self.sends = []

    def start(self):
        for seq in range(self.num_seqs):
            for i in range(self.per_dev):
                g = self.place.sp * self.per_dev + i
                target = seq * 2 + lax.rem(g, 2)
                here = target == self.place.sp
                block = self.src.at[seq, pl.ds(i * BLOCK, BLOCK)]
                slot = self.dst_slot(lax.div(g, 2))
                copy = remote(
                    block,
                    slot,
                    self.send_sem.at[seq, i],
                    self.recv_sem.at[lax.div(g, 2)],
                    (self.place.dp, target),
                )
                local = pltpu.make_async_copy(block, slot, self.local_sem.at[seq, i])
                when(jnp.logical_not(here), copy.start)
                when(here, local.start)
                self.sends.append((here, copy, local))

    def finish(self):
        for here, copy, local in self.sends:
            when(jnp.logical_not(here), copy.wait_send)
            when(here, local.wait)
        for slot in range(SLOTS):
            source = lax.div(2 * slot + self.place.core, self.per_dev)
            goal = self.dst_slot(slot)
            arrived = remote(
                goal, goal, self.send_sem.at[0, 0], self.recv_sem.at[slot], self.place.sibling()
            )
            when(source != self.place.sp, arrived.wait_recv)


def collect_kernel(dims, num_seqs, *refs):
    inputs, cotangent = refs[:2]
    weights, vecs = refs[2:10], refs[10]
    x_out, cot_out = refs[11:13]
    count = LAYERS * len(SETS)
    sets = refs[13 : 13 + count]
    sems = refs[13 + count : 19 + count]
    own_sem, *tok_sems = refs[19 + count :]
    place = Place(dims)
    own = start_own(place, weights, vecs, sets, own_sem)
    place.greet()
    moves = []
    for which, (src, dst) in enumerate(((inputs, x_out), (cotangent, cot_out))):
        moves.append(TokenMove(place, num_seqs, src, lambda s, dst=dst: dst.at[s], tok_sems, which))
        moves[-1].start()
    for copy in own:
        copy.wait()
    run_gather(place, gather_sets(place, sets, sems))
    for move in moves:
        move.finish()


def token_sems(num_seqs, per_dev):
    dma = pltpu.SemaphoreType.DMA
    return [dma((2, num_seqs, per_dev)), dma((2, SLOTS)), dma((2, num_seqs, per_dev))]


def collect(dims, inputs, cotangent, weights, vecs):
    rows = weights[0].shape[1]
    num_seqs = inputs.shape[0]
    tok = jax.ShapeDtypeStruct((SLOTS, BLOCK, WIDTH), BF)
    outs = [tok, tok] + [jax.ShapeDtypeStruct(s, BF) for s in set_shapes(dims, rows)]
    return pl.pallas_call(
        partial(collect_kernel, dims, num_seqs),
        out_shape=outs,
        in_specs=[ANY] * 11,
        out_specs=[ANY] * len(outs),
        scratch_shapes=gather_sems(len(SETS) * LAYERS, dims)
        + [pltpu.SemaphoreType.DMA((OWN_COPIES,))]
        + token_sems(num_seqs, inputs.shape[1] // BLOCK),
        compiler_params=pltpu.CompilerParams(
            collective_id=0, has_side_effects=True, vmem_limit_bytes=VMEM_BYTES
        ),
        name="collect",
    )(inputs, cotangent, *weights, vecs)


def add_units(total, part):
    count = total.shape[0]

    def body(u, carry):
        total[u] = total[u] + part[u]
        return carry

    lax.fori_loop(0, count, body, 0)


class ReduceSet:
    def __init__(self, place, total, other, mine, order, bufs, sems, result):
        self.place, self.total, self.other, self.mine, self.order = place, total, other, mine, order
        self.from_core, self.line1, self.line2, self.line_z = bufs
        self.c_send, self.c_recv, self.s_send, self.s_recv, self.z_send, self.z_recv = sems
        self.result = result
        self.sends = []

    def put(self, src, dst, send_sem, recv_sem, device, cond):
        copy = remote(src, dst, send_sem, recv_sem, device)
        when(cond, copy.start)
        self.sends.append((cond, copy))

    def core_copy(self, zb):
        return remote(
            self.other(zb),
            self.from_core.at[:, zb],
            self.c_send.at[zb],
            self.c_recv.at[zb],
            self.place.sibling(),
        )

    def start(self, zb, valid):
        copy = self.core_copy(zb)
        when(valid, copy.start)
        if self.mine is not None:
            when(valid, self.mine(zb).start)
        self.sends.append((valid, copy))

    def core_finish(self, zb, valid):
        def go():
            if self.mine is not None:
                self.mine(zb).wait()
            self.core_copy(zb).wait_recv()
            add_units(self.total(zb, slice(None), slice(None)), self.from_core.at[:, zb])

        when(valid, go)

    def block(self, stage, zb, q):
        index = [zb, self.place.x, self.place.y]
        if stage == 0:
            index[self.order[1]] = slice(None)
        index[self.order[stage]] = q
        return self.total(*index)

    def line(self, stage, way, zb, slot):
        if self.place.dims[self.order[stage]] == 2:
            way = 0
        return (self.line1, self.line2)[stage].at[way, slot, :, zb]

    def take(self, stage, way, zb, q, cond):
        slot = q - 1 if way == 0 else q
        buf = self.line(stage, way, zb, slot)
        copy = remote(
            buf,
            buf,
            self.s_send.at[stage, way, zb, slot],
            self.s_recv.at[stage, way, zb, slot],
            self.place.sibling(),
        )

        def go():
            copy.wait_recv()
            add_units(self.block(stage, zb, q), buf)

        when(cond, go)

    def stage_send(self, stage, zb, valid):
        axis = self.order[stage]
        p, num = self.place.at[axis], self.place.dims[axis]
        for u in range(num - 1, 0, -1):
            for side in (0, 1):
                q = p - u if side == 0 else p + u
                there = both(valid, q >= 0 if side == 0 else q < num)
                way = 1 - side
                if u <= num - 2:
                    self.take(stage, way, zb, q, both(there, p > 0 if side == 1 else p < num - 1))
                slot = q - 1 if side == 1 else q
                self.put(
                    self.block(stage, zb, q),
                    self.line(stage, way, zb, slot),
                    self.s_send.at[stage, way, zb, slot],
                    self.s_recv.at[stage, way, zb, slot],
                    self.place.device(axis, p + 1 if side == 1 else p - 1),
                    there,
                )

    def stage_keep(self, stage, zb, valid):
        axis = self.order[stage]
        p, num = self.place.at[axis], self.place.dims[axis]
        self.take(stage, 0, zb, p, both(valid, p > 0))
        self.take(stage, 1, zb, p, both(valid, p < num - 1))

    def z_slot(self, source, target):
        return jnp.where(source < target, source, source - 1)

    def z_step(self, t, zb, valid):
        place = self.place
        if t > 0:
            slot = self.z_slot(place.z, zb)
            self.put(
                self.total(zb, place.x, place.y),
                self.line_z.at[slot],
                self.z_send.at[self.z_slot(zb, place.z)],
                self.z_recv.at[slot],
                place.device(0, zb),
                valid,
            )

    def finish(self):
        place = self.place
        mine = self.total(place.z, place.x, place.y)
        num = place.dims[0] - 1
        for slot in range(num):
            buf = self.line_z.at[slot]
            remote(
                buf, buf, self.z_send.at[slot], self.z_recv.at[slot], place.sibling()
            ).wait_recv()
        for u in range(mine.shape[0]):
            value = mine[u].astype(F32)
            for slot in range(num):
                value = value + self.line_z[slot, u].astype(F32)
            self.result(u, value)

    def finish_sends(self):
        for cond, copy in self.sends:
            when(cond, copy.wait_send)

    def steps(self, rounds):
        def round_of(k):
            def act():
                for lag in (2, 1, 0):
                    if not 0 <= k - lag < len(rounds):
                        continue
                    for t, side, zb, valid in rounds[k - lag]:
                        if lag == 0:
                            self.core_finish(zb, valid)
                            self.stage_send(0, zb, valid)
                        elif lag == 1:
                            self.stage_keep(0, zb, valid)
                            self.stage_send(1, zb, valid)
                        else:
                            self.stage_keep(1, zb, valid)
                            self.z_step(t, zb, valid)

            return act

        return [round_of(k) for k in range(len(rounds) + 2)]


def reduce_sems(num_sets, dims):
    num_z, num_x, num_y = dims
    line = max(num_x, num_y)
    dma = pltpu.SemaphoreType.DMA
    return [
        dma((num_sets, num_z)),
        dma((num_sets, num_z)),
        dma((num_sets, 2, 2, num_z, line - 1)),
        dma((num_sets, 2, 2, num_z, line - 1)),
        dma((num_sets, num_z - 1)),
        dma((num_sets, num_z - 1)),
    ]


def reduce_bufs(count, depth, columns, dims, order, dtype):
    one, two = dims[order[0]], dims[order[1]]

    def ways(num):
        return 1 if num == 2 else 2

    return [
        pltpu.VMEM((count, *dims, depth, columns), dtype),
        pltpu.VMEM((ways(one), one - 1, count, dims[0], two, depth, columns), dtype),
        pltpu.VMEM((ways(two), two - 1, count, dims[0], depth, columns), dtype),
        pltpu.VMEM((dims[0] - 1, count, depth, columns), dtype),
    ]


ORDER_A = (2, 1)
ORDER_B = (1, 2)


class TokenReturn:
    def __init__(self, place, num_seqs, src_slot, dst, sems, which):
        self.place, self.num_seqs, self.src_slot, self.dst = place, num_seqs, src_slot, dst
        self.send_sem, self.recv_sem, self.local_sem = (s.at[which] for s in sems)
        self.per_dev = LEN // (place.dims[2] * 2) // BLOCK
        self.sends = []

    def start(self, slots=range(SLOTS)):
        for slot in slots:
            g = 2 * slot + self.place.core
            target = lax.div(g, self.per_dev)
            row = lax.rem(g, self.per_dev)
            here = target == self.place.sp
            block = self.src_slot(slot)
            goal = self.dst.at[self.place.y, pl.ds(pl.multiple_of(row * BLOCK, BLOCK), BLOCK)]
            copy = remote(
                block,
                goal,
                self.send_sem.at[slot],
                self.recv_sem.at[self.place.y, row],
                (self.place.dp, target),
            )
            local = pltpu.make_async_copy(block, goal, self.local_sem.at[slot])
            when(jnp.logical_not(here), copy.start)
            when(here, local.start)
            self.sends.append((here, copy, local))

    def finish(self):
        for here, copy, local in self.sends:
            when(jnp.logical_not(here), copy.wait_send)
            when(here, local.wait)
        for seq in range(self.num_seqs):
            for i in range(self.per_dev):
                g = self.place.sp * self.per_dev + i
                source = seq * 2 + lax.rem(g, 2)
                goal = self.dst.at[seq, pl.ds(i * BLOCK, BLOCK)]
                arrived = remote(
                    goal, goal, self.send_sem.at[0], self.recv_sem.at[seq, i], self.place.sibling()
                )
                when(source != self.place.sp, arrived.wait_recv)


def return_sems(num, num_seqs, per_dev):
    dma = pltpu.SemaphoreType.DMA
    return [dma((num, SLOTS)), dma((num, num_seqs, per_dev)), dma((num, SLOTS))]


def spread_kernel(dims, num_seqs, num_tok, *refs):
    refs = list(refs)

    def pop(count):
        out = refs[:count]
        del refs[:count]
        return out

    grads, toks, outs, tok_outs = pop(7), pop(num_tok), pop(7), pop(num_tok)
    totals, bufs, sems, own, tok_sems = pop(7), pop(28), pop(6), pop(1)[0], pop(3)
    place = Place(dims)
    core = place.core
    place.greet()
    sets = []
    for k in range(7):
        grad, total = grads[k], totals[k]

        def result(u, value, k=k):
            outs[k][u] = value

        sets.append(
            ReduceSet(
                place,
                lambda z, x, y, total=total: total.at[:, z, x, y],
                lambda z, grad=grad: grad.at[:, z, :, :, 1 - core],
                lambda z, grad=grad, total=total, k=k: pltpu.make_async_copy(
                    grad.at[:, z, :, :, core], total.at[:, z], own.at[k, z]
                ),
                ORDER_A if k in (0, 3, 6) else ORDER_B,
                bufs[4 * k : 4 * k + 4],
                set_sems(sems, k),
                result,
            )
        )
    rounds = z_items(place, True)
    for items in rounds:
        for t, side, zb, valid in items:
            for one in sets:
                one.start(zb, valid)
    moves = []
    for which, (src, dst) in enumerate(zip(toks, tok_outs)):
        moves.append(
            TokenReturn(place, num_seqs, lambda s, src=src: src.at[s], dst, tok_sems, which)
        )
        moves[-1].start()
    lists = [one.steps(rounds) for one in sets]
    for acts in zip(*lists):
        for act in acts:
            act()
    for one in sets:
        one.finish()
        one.finish_sends()
    for move in moves:
        move.finish()


def spread(dims, num_seqs, grads, toks):
    num_z, num_x, num_y = dims
    per_dev = LEN // (num_y * 2) // BLOCK
    rows = WIDTH // (num_z * num_x * num_y * 2)
    dma = pltpu.SemaphoreType.DMA
    set_sizes = [(UNITS_A, rows), (UNITS_B, rows), (1, 4 * rows)] * LAYERS + [(1, rows)]
    outs, bufs, totals = [], [], []
    for k, (count, depth) in enumerate(set_sizes):
        columns = WIDTH if k < 6 else BLOCK
        dtype = BF if k < 6 else F32
        outs.append(jax.ShapeDtypeStruct((count, depth, columns), F32))
        order = ORDER_A if k in (0, 3, 6) else ORDER_B
        totals.append(pltpu.VMEM((count, *dims, depth, columns), dtype))
        bufs += reduce_bufs(count, depth, columns, dims, order, dtype)
    outs += [jax.ShapeDtypeStruct((num_seqs, per_dev * BLOCK, WIDTH), t.dtype) for t in toks]
    shaped = [
        g.reshape(count, num_z, num_x, num_y, 2, depth, g.shape[-1])
        for g, (count, depth) in zip(grads, set_sizes)
    ]
    return pl.pallas_call(
        partial(spread_kernel, dims, num_seqs, len(toks)),
        out_shape=outs,
        in_specs=[ANY] * (7 + len(toks)),
        out_specs=[VMEM] * 7 + [ANY] * len(toks),
        scratch_shapes=totals
        + bufs
        + reduce_sems(7, dims)
        + [dma((7, num_z))]
        + return_sems(len(toks), num_seqs, per_dev),
        compiler_params=pltpu.CompilerParams(
            collective_id=1, has_side_effects=True, vmem_limit_bytes=VMEM_BYTES
        ),
        name="spread",
    )(*shaped, *toks)


def dot(left, right):
    return lax.dot_general(left, right, (((1,), (0,)), ((), ())), preferred_element_type=F32)


def dot_nt(left, right):
    return lax.dot_general(left, right, (((1,), (1,)), ((), ())), preferred_element_type=F32)


def dot_tn(left, right):
    return lax.dot_general(left, right, (((0,), (0,)), ((), ())), preferred_element_type=F32)


def normalize(values):
    centre = jnp.mean(values, axis=-1, keepdims=True)
    shifted = values - centre
    inv_std = lax.rsqrt(jnp.mean(shifted * shifted, axis=-1, keepdims=True) + EPSILON)
    return shifted * inv_std, inv_std


def norm_back(grad_normed, normed, inv_std, gain):
    grad_hat = grad_normed * gain
    mean_one = jnp.mean(grad_hat, axis=-1, keepdims=True)
    mean_two = jnp.mean(grad_hat * normed, axis=-1, keepdims=True)
    return inv_std * (grad_hat - mean_one - normed * mean_two)


def halves(body, tick=None):
    if tick is not None:
        for i in range(2):
            body(pl.ds(i * HALF, HALF))
            tick()
        return

    def step(i, carry):
        body(pl.ds(pl.multiple_of(i * HALF, HALF), HALF))
        return carry

    lax.fori_loop(0, 2, step, 0)


def column_sums(values):
    return jnp.sum(values, axis=0, keepdims=True)


GELU_A = 0.7978845608028654
GELU_B = 0.044715


def gelu(t):
    return 0.5 * t * (1.0 + jnp.tanh(GELU_A * (t + GELU_B * t * t * t)))


def gelu_both(t):
    square = t * t
    wave = jnp.tanh(GELU_A * (t + GELU_B * t * square))
    up = 0.5 * (1.0 + wave)
    slope = up + 0.5 * t * (1.0 - wave * wave) * (GELU_A * (1.0 + 3.0 * GELU_B * square))
    return t * up, slope


class Weights:
    def __init__(self, r, layer, names):
        self.r, self.layer = r, layer
        self.copies = {}
        sets = r.g[layer]
        place_of = {}
        for which, (units, _) in enumerate(SETS):
            for unit, name in enumerate(units):
                src = sets[which].at[unit]
                if name == "down":
                    place_of["down"] = [
                        (src.at[pl.ds(k * WIDTH, WIDTH)], r.w_scratch, ("down", k))
                        for k in range(CHUNKS)
                    ]
                elif name[:2] == "up":
                    place_of.setdefault("up", []).append((src, r.w_scratch, ("up", int(name[2:]))))
                else:
                    place_of[name] = [(src, r.w_scratch, name)]
        for name in names:
            group = []
            for src, pool, key in place_of[name]:
                index = r.w_index[(layer, key)]
                copy = pltpu.make_async_copy(src, pool.at[index], r.w_sem.at[index])
                copy.start()
                group.append(copy)
            self.copies[name] = group
        self.waited = set()

    def need(self, *names):
        for name in names:
            if name in self.copies and name not in self.waited:
                self.waited.add(name)
                for copy in self.copies[name]:
                    copy.wait()

    def get(self, name):
        return self.r.w_scratch[self.r.w_index[(self.layer, name)]]

    def chunk(self, name, n):
        return self.r.w_scratch[self.r.w_index[(self.layer, (name, 0))] + n]


def vec_row(r, layer, which):
    row = layer * 4 + which
    return r.vec[row : row + 1, :]


def load_vectors(r):
    r.vec[...] = jnp.transpose(r.vec_in[...].astype(F32))[0:8, :]


def mask_setup(r, flipped):
    core = lax.rem(lax.axis_index("sp"), 2)
    seq = lax.div(lax.axis_index("sp"), 2)
    ends = []
    total = jnp.int32(0)
    for d in range(4):
        total = total + r.lengths[seq, d]
        ends.append(total)

    def segment(position):
        out = jnp.zeros(position.shape, jnp.int32)
        for end in ends:
            out = out + (position >= end).astype(jnp.int32)
        return out

    for j in range(SLOTS):
        for which in range(2):
            count = (j + 1) * BLOCK
            other = core if which == 0 else 1 - core
            q_shape, k_shape = ((1, BLOCK), (count, 1)) if flipped else ((BLOCK, 1), (1, count))
            q_in = lax.broadcasted_iota(jnp.int32, q_shape, 1 if flipped else 0)
            k_in = lax.broadcasted_iota(jnp.int32, k_shape, 0 if flipped else 1)
            q_pos = (2 * j + core) * BLOCK + q_in
            k_pos = k_in + BLOCK * lax.div(k_in, BLOCK) + other * BLOCK
            q_seg = segment(q_pos)
            k_seg = segment(k_pos)
            k_seg = jnp.where(k_seg >= 4, -1, k_seg)
            allowed = ((q_seg == k_seg) & (k_pos <= q_pos)) | (q_pos == k_pos)
            bias = jnp.where(allowed, 0.0, NEG_FILL).astype(F32)
            if flipped:
                r.bias[j, which * TOKENS : which * TOKENS + count, :] = bias
            else:
                r.bias[j, :, which * TOKENS : which * TOKENS + count] = bias


def two_heads(block):
    lane = lax.broadcasted_iota(jnp.int32, block.shape, 1)
    zero = jnp.zeros_like(block)
    first = jnp.where(lane < HEAD_DIM, block, zero)
    second = jnp.where(lane < HEAD_DIM, zero, block)
    return jnp.concatenate([first, second], axis=0)


def join_heads(stacked):
    first, second = stacked[:BLOCK], stacked[BLOCK:]
    lane = lax.broadcasted_iota(jnp.int32, first.shape, 1)
    return jnp.where(lane < HEAD_DIM, first, second)


def layer_front(
    r, w, layer, x_ref, h_ref, q_ref, k_ref, v_ref, gate_ref, tick=None, exchange=lambda: None
):
    w.need("q", "k", "v", "ga")

    def first(rows):
        normed, _ = normalize(x_ref[rows, :].astype(F32))
        hidden = (normed * vec_row(r, layer, 0)).astype(BF)
        h_ref[rows, :] = hidden
        k_ref[rows, :] = dot(hidden, w.get("k")).astype(BF)
        v_ref[rows, :] = dot(hidden, w.get("v")).astype(BF)

    halves(first)
    exchange()
    if tick is not None:
        tick()

    def second(rows):
        hidden = h_ref[rows, :]
        q_ref[rows, :] = (dot(hidden, w.get("q")) * (HEAD_DIM**-0.5)).astype(BF)
        gate_ref[rows, :] = jax.nn.sigmoid(dot(hidden, w.get("ga")) + vec_row(r, layer, 1))

    halves(second)
    if tick is not None:
        tick()


def attention(r, q_ref, k_refs, v_refs, out_ref, lse_ref, tick=None):
    lse_ref[...] = jnp.zeros_like(lse_ref)

    def pair_step(pair, carry):
        cols = pl.ds(pl.multiple_of(pair * BLOCK, BLOCK), BLOCK)
        for j in range(SLOTS):
            rows = slice(j * BLOCK, (j + 1) * BLOCK)
            count = (j + 1) * BLOCK
            queries = two_heads(q_ref[rows, cols])
            scores = []
            for which in range(2):
                bias = r.bias[j, :, which * TOKENS : which * TOKENS + count]
                score = dot_nt(queries, k_refs[which][0:count, cols])
                scores.append(score + jnp.concatenate([bias, bias], axis=0))
            top = jnp.maximum(
                jnp.max(scores[0], axis=1, keepdims=True), jnp.max(scores[1], axis=1, keepdims=True)
            )
            expo = [jnp.exp(score - top) for score in scores]
            total = jnp.sum(expo[0], axis=1, keepdims=True) + jnp.sum(expo[1], axis=1, keepdims=True)
            mixed = dot(expo[0].astype(BF), v_refs[0][0:count, cols])
            mixed = mixed + dot(expo[1].astype(BF), v_refs[1][0:count, cols])
            out_ref[rows, cols] = join_heads(mixed / total).astype(BF)
            lse = top + jnp.log(total)
            lane = lax.broadcasted_iota(jnp.int32, (BLOCK, BLOCK), 1)
            kept = lse_ref[rows, :]
            kept = jnp.where(lane == 2 * pair, lse[:BLOCK], kept)
            lse_ref[rows, :] = jnp.where(lane == 2 * pair + 1, lse[BLOCK:], kept)
        return carry

    if tick is None:
        lax.fori_loop(0, PAIRS, pair_step, 0)
        return
    for part in range(2):
        lax.fori_loop(part * PAIRS // 2, (part + 1) * PAIRS // 2, pair_step, 0)
        tick()


def layer_back_half(
    r, w, layer, x_ref, attn_ref, gate_ref, a_ref, x2_ref, y_ref, gf_ref, x3_ref, tick=None, more=None
):
    w.need("o", "gf", "up", "down")

    def body(rows):
        branch = dot(attn_ref[rows, :], w.get("o"))
        a_ref[rows, :] = branch.astype(a_ref.dtype)
        after = x_ref[rows, :].astype(F32) + gate_ref[rows, :] * branch
        x2_ref[rows, :] = after
        normed, _ = normalize(after)
        hidden = (normed * vec_row(r, layer, 2)).astype(BF)
        if more is not None:
            more.hid_t[:, rows] = jnp.transpose(hidden)
        out = None
        for n in range(CHUNKS):
            up = dot(hidden, w.chunk("up", n))
            if more is None:
                active = gelu(up).astype(BF)
            else:
                value, slope = gelu_both(up)
                active = value.astype(BF)
                more.slope[n, rows, :] = slope.astype(BF)
                more.act_t[n, :, rows] = jnp.transpose(active)
            part = dot(active, w.chunk("down", n))
            out = part if out is None else out + part
        y_ref[rows, :] = out.astype(y_ref.dtype)
        gate = jax.nn.sigmoid(dot(hidden, w.get("gf")) + vec_row(r, layer, 3))
        gf_ref[rows, :] = gate
        x3_ref[rows, :] = after + gate * out

    halves(body, tick)


def nothing(*args):
    pass


def ffn_backward(r, w, layer, dx_ref, s, out, tick=nothing, ready=nothing, kept=None):
    w.need("o", "gf", "up", "down")
    hid_t = r.hid_t if kept is None else kept.hid_t

    def start(rows):
        grad = dx_ref[rows, :].astype(F32)
        gate = s.gf[rows, :]
        r.dy[rows, :] = (grad * gate).astype(BF)
        dz = (grad * s.y[rows, :].astype(F32) * gate * (1.0 - gate)).astype(BF)
        r.dz[rows, :] = dz
        if kept is None:
            normed, _ = normalize(s.x2[rows, :])
            r.hid[rows, :] = (normed * vec_row(r, layer, 2)).astype(BF)
        r.dh[rows, :] = dot_nt(dz, w.get("gf"))

    halves(start)
    if kept is None:
        r.hid_t[...] = jnp.transpose(r.hid[...])
    out.unit("gf", dot(hid_t[...], r.dz[...]))
    r.vg[layer * 4 + 3 : layer * 4 + 4, :] = column_sums(r.dz[...].astype(F32))
    tick()

    for n in range(CHUNKS):
        if kept is not None:
            kept.take(n)

        def body(rows, n=n):
            if kept is None:
                act, slope = gelu_both(dot(r.hid[rows, :], w.chunk("up", n)))
                r.act[rows, :] = act.astype(BF)
            else:
                slope = kept.slope(n)[rows, :].astype(F32)
            du = (dot_nt(r.dy[rows, :], w.chunk("down", n)) * slope).astype(BF)
            r.du[rows, :] = du
            r.dh[rows, :] += dot_nt(du, w.chunk("up", n))

        halves(body)
        if kept is None:
            out.down(n, dot_tn(r.act[...], r.dy[...]))
        else:
            out.down(n, dot(kept.act_t(n)[...], r.dy[...]))
        out.unit("up" + str(n), dot(hid_t[...], r.du[...]))
        if kept is not None:
            kept.drop(n)
        if n == 1:
            ready("up_a")
        elif n == 3:
            ready("up_b", "down")
        tick()

    r.sums[...] = jnp.zeros_like(r.sums)

    def finish(rows):
        normed, inv_std = normalize(s.x2[rows, :])
        grad_hidden = r.dh[rows, :]
        r.sums[0:1, :] += column_sums(grad_hidden * normed)
        mid = dx_ref[rows, :].astype(F32) + norm_back(
            grad_hidden, normed, inv_std, vec_row(r, layer, 2)
        )
        out.dx2[rows, :] = mid
        gate = s.gate[rows, :]
        da = (mid * gate).astype(BF)
        r.dy[rows, :] = da
        dza = (mid * s.a[rows, :].astype(F32) * gate * (1.0 - gate)).astype(BF)
        out.dza[rows, :] = dza
        r.sums[1:2, :] += column_sums(dza.astype(F32))
        r.dattn[rows, :] = dot_nt(da, w.get("o")).astype(BF)

    halves(finish)
    tick()
    r.vg[layer * 4 + 2 : layer * 4 + 3, :] = r.sums[0:1, :]
    r.vg[layer * 4 + 1 : layer * 4 + 2, :] = r.sums[1:2, :]
    if kept is None:
        out.unit("o", dot_tn(s.attn[...], r.dy[...]))
        out.unit("ga", dot_tn(s.h[...], out.dza[...]))
    else:
        out.unit("o", dot(kept.attn_t[...], r.dy[...]))
        out.unit("ga", dot(kept.h_t[...], out.dza[...]))
    ready("mix")
    tick()


def attention_backward(r, s, out, tick=None):
    for j in range(SLOTS):
        r.lse_t[j] = jnp.transpose(s.lse[j * BLOCK : (j + 1) * BLOCK, :])[0:8, :]

    def slot_step(pair, cols, j):
        rows = slice(j * BLOCK, (j + 1) * BLOCK)
        count = (j + 1) * BLOCK
        queries = two_heads(s.q[rows, cols])
        grads = two_heads(r.dattn[rows, cols])
        lse = jnp.concatenate(
            [r.lse_t[j, pl.ds(2 * pair, 1), :], r.lse_t[j, pl.ds(2 * pair + 1, 1), :]], axis=1
        )
        probs, slopes = [], []
        delta = None
        for which in range(2):
            bias = r.bias[j, which * TOKENS : which * TOKENS + count, :]
            score = dot_nt(s.k[which][0:count, cols], queries)
            prob = jnp.exp(score + jnp.concatenate([bias, bias], axis=1) - lse)
            slope = dot_nt(s.v[which][0:count, cols], grads)
            part = column_sums(prob * slope)
            delta = part if delta is None else delta + part
            probs.append(prob)
            slopes.append(slope)
        grad_q = None
        for which in range(2):
            ds = (probs[which] * (slopes[which] - delta)).astype(BF)
            dv = dot(probs[which].astype(BF), grads)
            dk = dot(ds, queries)
            dk_ref, dv_ref = (out.dk, out.dv) if which == 0 else (r.dk_other, r.dv_other)
            where = cols if which == 0 else slice(None)
            if j == SLOTS - 1:
                dk_ref[:, where] = dk
                dv_ref[:, where] = dv
            else:
                dk_ref[0:count, where] += dk
                dv_ref[0:count, where] += dv
            part = dot_tn(s.k[which][0:count, cols], ds)
            grad_q = part if grad_q is None else grad_q + part
        grad_q = join_heads(jnp.transpose(grad_q)) * (HEAD_DIM**-0.5)
        out.dq[rows, cols] = grad_q.astype(BF)

    def pair_step(pair, carry):
        cols = pl.ds(pl.multiple_of(pair * BLOCK, BLOCK), BLOCK)
        for j in range(SLOTS - 1, -1, -1):
            slot_step(pair, cols, j)
        if tick is not None:
            tick()
        out.dk_out[:, cols] = r.dk_other[...].astype(BF)
        out.dv_out[:, cols] = r.dv_other[...].astype(BF)
        return carry

    if tick is None:
        lax.fori_loop(0, PAIRS, pair_step, 0)
    else:
        for pair in range(PAIRS):
            pair_step(pair, 0)


def layer_front_backward(
    r, w, layer, s, g, out, dx_ref, arrived=nothing, tick=nothing, ready=nothing, h_t=None
):
    w.need("q", "k", "v", "ga")
    if h_t is None:
        h_t = r.hid_t
        h_t[...] = jnp.transpose(s.h[...])
    out.unit("q", dot(h_t[...], g.dq[...]))
    ready("q")

    def before(rows):
        grad_hidden = dot_nt(g.dq[rows, :], w.get("q"))
        r.dh[rows, :] = grad_hidden + dot_nt(g.dza[rows, :], w.get("ga"))

    halves(before)
    arrived()

    def start(rows):
        r.dk[rows, :] = (g.dk[rows, :] + g.dk_in[rows, :].astype(F32)).astype(BF)
        r.dv[rows, :] = (g.dv[rows, :] + g.dv_in[rows, :].astype(F32)).astype(BF)

    halves(start)
    out.unit("k", dot(h_t[...], r.dk[...]))
    out.unit("v", dot(h_t[...], r.dv[...]))
    ready("kv")
    tick()
    r.sums[...] = jnp.zeros_like(r.sums)

    def body(rows):
        grad_hidden = r.dh[rows, :] + dot_nt(r.dk[rows, :], w.get("k"))
        grad_hidden += dot_nt(r.dv[rows, :], w.get("v"))
        normed, inv_std = normalize(s.x[rows, :].astype(F32))
        r.sums[0:1, :] += column_sums(grad_hidden * normed)
        dx_ref[rows, :] = g.dx2[rows, :] + norm_back(
            grad_hidden, normed, inv_std, vec_row(r, layer, 0)
        )

    halves(body)
    tick()
    r.vg[layer * 4 : layer * 4 + 1, :] = r.sums[0:1, :]


FRONT = ("q", "k", "v", "ga")
BACK = ("o", "gf", "up", "down")


def weight_index(wanted):
    index, count = {}, 0
    for layer, names in wanted:
        for name in names:
            if name in ("up", "down"):
                for k in range(CHUNKS):
                    index[(layer, (name, k))] = count
                    count += 1
            else:
                index[(layer, name)] = count
                count += 1
    return index, count


def compute_call(body, name, wanted, gathered, ins, outs, scratch):
    in_names, out_names, scratch_names = list(ins), list(outs), list(scratch)
    layers = sorted({layer for layer, _ in wanted})
    index, count = weight_index(wanted)
    weight_refs = [arr for layer in layers for arr in gathered[layer]]

    def kernel(*refs):
        refs = list(refs)
        r = SimpleNamespace()
        r.g = {}
        for layer in layers:
            r.g[layer] = [refs.pop(0) for _ in SETS]
        for field in in_names + out_names + scratch_names:
            setattr(r, field, refs.pop(0))
        r.w_scratch, r.w_sem, r.vec = refs
        r.w_index = index
        r.w = {}
        for layer, names in wanted:
            r.w[layer] = Weights(r, layer, names)
        load_vectors(r)
        body(r)

    return pl.pallas_call(
        kernel,
        out_shape=[outs[n] for n in out_names],
        in_specs=[ANY] * len(weight_refs) + [SMEM if n == "lengths" else VMEM for n in in_names],
        out_specs=[VMEM] * len(out_names),
        scratch_shapes=[scratch[n] for n in scratch_names]
        + [
            pltpu.VMEM((count, WIDTH, WIDTH), BF),
            pltpu.SemaphoreType.DMA((count,)),
            pltpu.VMEM((8, WIDTH), F32),
        ],
        compiler_params=pltpu.CompilerParams(vmem_limit_bytes=VMEM_BYTES),
        name=name,
    )(*weight_refs, *[ins[n] for n in in_names])


def tok(dtype):
    return jax.ShapeDtypeStruct((TOKENS, WIDTH), dtype)


def vm(*shape, dtype=BF):
    return pltpu.VMEM(shape, dtype)


def front_outs(prefix):
    return {
        prefix + "h": tok(BF),
        prefix + "q": tok(BF),
        prefix + "k": tok(BF),
        prefix + "v": tok(BF),
        prefix + "gate": tok(F32),
    }


def back_outs():
    return {
        "attn": tok(BF),
        "lse": jax.ShapeDtypeStruct((TOKENS, BLOCK), F32),
        "a": tok(F32),
        "x2": tok(F32),
        "y": tok(F32),
        "gf": tok(F32),
        "x3": tok(F32),
    }


BIAS = vm(SLOTS, BLOCK, 2 * TOKENS, dtype=F32)
BIAS_T = vm(SLOTS, 2 * TOKENS, BLOCK, dtype=F32)


def grad_outs():
    return {
        "a": jax.ShapeDtypeStruct((UNITS_A, WIDTH, WIDTH), BF),
        "b": jax.ShapeDtypeStruct((UNITS_B, WIDTH, WIDTH), BF),
        "d": jax.ShapeDtypeStruct((1, CHUNKS * WIDTH, WIDTH), BF),
    }


BACKWARD_SCRATCH = {
    "bias": BIAS_T,
    "dy": vm(TOKENS, WIDTH),
    "dz": vm(TOKENS, WIDTH),
    "hid": vm(TOKENS, WIDTH),
    "hid_t": vm(WIDTH, TOKENS),
    "dh": vm(TOKENS, WIDTH, dtype=F32),
    "act": vm(TOKENS, WIDTH),
    "du": vm(TOKENS, WIDTH),
    "sums": vm(8, WIDTH, dtype=F32),
    "dattn": vm(TOKENS, WIDTH),
    "lse_t": vm(SLOTS, 8, BLOCK, dtype=F32),
    "dk_other": vm(TOKENS, BLOCK, dtype=F32),
    "dv_other": vm(TOKENS, BLOCK, dtype=F32),
}


def front_call(gathered, vec_in, layer, x):
    def body(r):
        layer_front(r, r.w[layer], layer, r.x, r.h, r.q, r.k, r.v, r.gate)

    outs = front_outs("")
    got = compute_call(
        body, "front", [(layer, FRONT)], gathered, {"vec_in": vec_in, "x": x}, outs, {}
    )
    return dict(zip(outs, got))


def middle_call(gathered, vec_in, lengths, layer, x, s):
    ins = {
        "vec_in": vec_in,
        "lengths": lengths,
        "x": x,
        "q": s["q"],
        "k0": s["k"],
        "v0": s["v"],
        "k1": s["k1"],
        "v1": s["v1"],
        "gate": s["gate"],
    }
    last = layer == LAYERS - 1
    outs = back_outs()
    wanted = [(layer, BACK)]
    if not last:
        outs.update(front_outs("n"))
        wanted.append((layer + 1, FRONT))

    def body(r):
        mask_setup(r, False)
        attention(r, r.q, (r.k0, r.k1), (r.v0, r.v1), r.attn, r.lse)
        layer_back_half(
            r, r.w[layer], layer, r.x, r.attn, r.gate, r.a, r.x2, r.y, r.gf, r.x3
        )
        if not last:
            layer_front(
                r, r.w[layer + 1], layer + 1, r.x3, r.nh, r.nq, r.nk, r.nv, r.ngate
            )

    got = compute_call(body, "middle", wanted, gathered, ins, outs, {"bias": BIAS})
    return dict(zip(outs, got))


class Gathered:
    def __init__(self, refs):
        self.place = {
            name: refs[which].at[unit]
            for which, (names, _) in enumerate(SETS)
            for unit, name in enumerate(names)
        }

    def need(self, *names):
        pass

    def get(self, name):
        return self.place[name][...].reshape(WIDTH, WIDTH)

    def chunk(self, name, n):
        if name == "up":
            return self.get("up" + str(n))
        ref = self.place["down"]
        part = ref.shape[0] // CHUNKS
        return ref[n * part : (n + 1) * part].reshape(WIDTH, WIDTH)


LAYER_ARRAYS = {
    "h": BF,
    "q": BF,
    "k": BF,
    "v": BF,
    "k1": BF,
    "v1": BF,
    "gate": F32,
    "attn": BF,
    "lse": F32,
    "a": BF,
    "x2": F32,
    "y": BF,
    "gf": F32,
    "x3": F32,
    "h_t": BF,
    "attn_t": BF,
    "hid_t": BF,
    "act_t": BF,
    "slope": BF,
}
NOT_SAVED = ("h", "attn")


def layer_shape(name):
    if name in ("act_t", "slope"):
        return (CHUNKS, WIDTH, TOKENS)
    return (TOKENS, BLOCK if name == "lse" else WIDTH)


def saved_names(layer):
    return [n for n in LAYER_ARRAYS if n not in NOT_SAVED and (n != "x3" or layer < LAYERS - 1)]


def forward_kernel(dims, num_seqs, *refs):
    refs = list(refs)

    def pop(count):
        out = refs[:count]
        del refs[:count]
        return out

    num_sets = LAYERS * len(SETS)
    inputs, cotangent = pop(2)
    weights = pop(8)
    vectors = pop(4)
    (lengths,) = pop(1)
    cot_out, result, x0_out = pop(3)
    set_outs = pop(num_sets)
    saved_outs = [{n: pop(1)[0] for n in saved_names(layer)} for layer in range(LAYERS)]
    sets = pop(num_sets)
    arrays = [dict(zip(LAYER_ARRAYS, pop(len(LAYER_ARRAYS)))) for _ in range(LAYERS)]
    x0, cot, last, bias, vec, square = pop(6)
    sems = pop(6)
    (own_sem,) = pop(1)
    tok_sems = pop(3)
    kv_send, kv_recv, out_sem = pop(3)

    place = Place(dims)
    own = [start_own(place, weights, None, sets, own_sem, (0,))]
    own.append(start_own(place, weights, None, sets, own_sem, (1,), len(own[0])))
    rows = vectors[0].shape[1]
    square[...] = jnp.zeros_like(square)
    for layer in range(LAYERS):
        for which, ref in enumerate(vectors):
            row = layer * 4 + which
            square[row : row + 1, 0:rows] = ref[layer : layer + 1, :].astype(F32)
    vec_unit = sets[0].at[VEC_UNIT, place.z, place.x, place.y, place.core]
    vec_unit[...] = jnp.zeros(vec_unit.shape, BF)
    vec_unit[:, 0:BLOCK] = jnp.transpose(square[...])[0:rows, :].astype(BF)
    place.greet()

    def rows_of(ref):
        return lambda slot: ref.at[pl.ds(pl.multiple_of(slot * BLOCK, BLOCK), BLOCK)]

    move_x = TokenMove(place, num_seqs, inputs, rows_of(x0), tok_sems, 0)
    move_cot = TokenMove(place, num_seqs, cotangent, rows_of(cot), tok_sems, 1)
    outgoing = []

    def save(src, dst):
        copy = pltpu.make_async_copy(src, dst, out_sem.at[len(outgoing)])
        copy.start()
        outgoing.append(copy)

    gathers = [
        PairGather(place, ref, SETS[k % len(SETS)][1], set_sems(sems, k))
        for k, ref in enumerate(sets)
    ]
    far = range(1, dims[0])

    def event(method, group, *args):
        for one in gathers[2 * group : 2 * group + 2]:
            getattr(one, method)(*args)

    for copy in own[0]:
        copy.wait()
    event("open", 0)
    move_x.start()
    for copy in own[1]:
        copy.wait()

    def finish_group(group):
        event("finish", group)
        for which in (2 * group, 2 * group + 1):
            save(sets[which], set_outs[which])

    after = (
        {
            "front0": (("stage2", 1, 1),),
            "front1": (("stage2", 1, 2),),
            "attend0": (("stage2", 1, 3), ("stage1", 2, *far), ("open", 3), ("stage2", 2, 0)),
            "attend1": (("stage2", 2, *far), ("stage3", 1), ("done", 1)),
            "feed0": (("stage1", 3, *far), ("stage2", 3, 0, 1)),
            "feed1": (("stage3", 2), ("stage2", 3, 2, 3), ("done", 2)),
        },
        {"attend1": (("stage3", 3), ("done", 3))},
    )

    def ticker(layer, name):
        count = [0]

        def tick():
            for method, group, *args in after[layer].get(name + str(count[0]), ()):
                if method == "done":
                    finish_group(group)
                else:
                    event(method, group, *args)
            count[0] += 1

        return tick

    r = SimpleNamespace(bias=bias, lengths=lengths, vec=vec)
    event("open", 1)
    event("stage2", 0, 0)
    for t in far:
        event("stage1", 0, t)
        event("stage2", 0, t)
    event("stage1", 1, *far)
    event("open", 2)
    event("stage3", 0)
    mask_setup(r, False)
    event("stage2", 1, 0)
    finish_group(0)
    move_x.finish()
    vec_block = sets[0][VEC_UNIT].reshape(WIDTH, WIDTH)[:, :BLOCK]
    vec[...] = jnp.transpose(vec_block.astype(F32))[0:8, :]
    save(x0, x0_out)

    exchanges = []
    x = x0
    for layer in range(LAYERS):
        s = SimpleNamespace(**arrays[layer])
        w = Gathered(sets[layer * len(SETS) : (layer + 1) * len(SETS)])
        def exchange(s=s, layer=layer):
            for k, (src, dst) in enumerate(((s.k, s.k1), (s.v, s.v1))):
                copy = remote(src, dst, kv_send.at[layer, k], kv_recv.at[layer, k], place.sibling())
                copy.start()
                exchanges.append(copy)

        tick = ticker(layer, "front")
        layer_front(r, w, layer, x, s.h, s.q, s.k, s.v, s.gate, tick, exchange)
        if layer == 0:
            move_cot.start()
        s.h_t[...] = jnp.transpose(s.h[...])
        for name in ("h_t", "q", "k", "v", "gate"):
            save(arrays[layer][name], saved_outs[layer][name])
        exchanges[-2].wait_recv()
        exchanges[-1].wait_recv()
        attention(r, s.q, (s.k, s.k1), (s.v, s.v1), s.attn, s.lse, ticker(layer, "attend"))
        s.attn_t[...] = jnp.transpose(s.attn[...])
        for name in ("k1", "v1", "attn_t", "lse"):
            save(arrays[layer][name], saved_outs[layer][name])
        layer_back_half(
            r,
            w,
            layer,
            x,
            s.attn,
            s.gate,
            s.a,
            s.x2,
            s.y,
            s.gf,
            s.x3,
            ticker(layer, "feed"),
            s,
        )
        for name in ("a", "x2", "y", "gf", "x3", "hid_t", "act_t", "slope"):
            if layer < LAYERS - 1 or name != "x3":
                save(arrays[layer][name], saved_outs[layer][name])
        x = s.x3

    last[...] = x[...].astype(BF)
    save(last, result)
    move_cot.finish()
    save(cot, cot_out)
    for copy in exchanges:
        copy.wait_send()
    for one in gathers:
        one.finish_sends()
    for copy in outgoing:
        copy.wait()


def forward(dims, inputs, cotangent, weights, vectors, lengths):
    rows = weights[0].shape[1]
    num_seqs, positions, _ = inputs.shape
    shapes = set_shapes(dims, rows)
    dma = pltpu.SemaphoreType.DMA
    layer_types = list(LAYER_ARRAYS.items()) * LAYERS
    outs = [tok(BF), tok(BF), tok(BF)]
    outs += [jax.ShapeDtypeStruct(s, BF) for s in shapes]
    for layer in range(LAYERS):
        for name in saved_names(layer):
            outs.append(jax.ShapeDtypeStruct(layer_shape(name), LAYER_ARRAYS[name]))
    num_saves = len(outs)
    scratch = [vm(*s) for s in shapes]
    scratch += [vm(*layer_shape(n), dtype=t) for n, t in layer_types]
    scratch += [vm(TOKENS, WIDTH), vm(TOKENS, WIDTH), vm(TOKENS, WIDTH), BIAS]
    scratch += [vm(8, WIDTH, dtype=F32), vm(BLOCK, BLOCK, dtype=F32)]
    scratch += pair_gather_sems(len(shapes), dims[0])
    scratch += [dma((OWN_COPIES,))]
    scratch += token_sems(num_seqs, positions // BLOCK)
    scratch += [dma((LAYERS, 2)), dma((LAYERS, 2)), dma((num_saves,))]
    cot, result, x0, *rest = pl.pallas_call(
        partial(forward_kernel, dims, num_seqs),
        out_shape=outs,
        in_specs=[ANY] * 10 + [VMEM] * 4 + [SMEM],
        out_specs=[ANY] * len(outs),
        scratch_shapes=scratch,
        compiler_params=pltpu.CompilerParams(
            collective_id=0, has_side_effects=True, vmem_limit_bytes=VMEM_BYTES
        ),
        name="forward",
    )(inputs, cotangent, *weights, *vectors, lengths)
    units, arrays = rest[: len(shapes)], rest[len(shapes) :]
    saved = []
    for layer in range(LAYERS):
        saved.append({name: arrays.pop(0) for name in saved_names(layer)})
    return cot, result, x0, units, saved


SAVED = ("h", "q", "k", "v", "k1", "v1", "gate", "attn", "lse", "a", "x2", "y", "gf")


def backward_outs():
    outs = {"g" + n: shape for n, shape in grad_outs().items()}
    outs["dx2"] = tok(F32)
    outs["dza"] = tok(BF)
    outs["dq"] = tok(BF)
    outs["dk"] = tok(F32)
    outs["dv"] = tok(F32)
    outs["dk_out"] = tok(BF)
    outs["dv_out"] = tok(BF)
    outs["vg"] = jax.ShapeDtypeStruct((8, WIDTH), F32)
    return outs


UNIT_PLACE = {"q": 0, "k": 1, "v": 2, "o": 3, "ga": 4, "gf": 5, "up0": 6}


class PlainGrads:
    def __init__(self, a, b=None, d=None):
        self.a, self.b, self.d = a, b, d

    def unit(self, name, value):
        if name in UNIT_PLACE:
            self.a[UNIT_PLACE[name]] = value.astype(BF)
        else:
            self.b[int(name[2:]) - 1] = value.astype(BF)

    def down(self, n, value):
        self.d[0, n * WIDTH : (n + 1) * WIDTH, :] = value.astype(BF)


def run_backward(r, layer, dx_ref):
    s = SimpleNamespace(**{n: getattr(r, "s" + n) for n in SAVED})
    s.k = (r.sk, r.sk1)
    s.v = (r.sv, r.sv1)
    out = PlainGrads(r.ga, r.gb, r.gd)
    for name in ("dx2", "dza", "dq", "dk", "dv", "dk_out", "dv_out"):
        setattr(out, name, getattr(r, name))
    mask_setup(r, True)
    ffn_backward(r, r.w[layer], layer, dx_ref, s, out)
    attention_backward(r, s, out)


def backward_call(gathered, vec_in, lengths, layer, dx, saved):
    ins = {"vec_in": vec_in, "lengths": lengths, "dx": dx}
    ins.update({"s" + n: saved[n] for n in SAVED})

    def body(r):
        r.vg[...] = jnp.zeros_like(r.vg)
        run_backward(r, layer, r.dx)

    outs = backward_outs()
    got = compute_call(
        body, "backward", [(layer, BACK)], gathered, ins, outs, BACKWARD_SCRATCH
    )
    return dict(zip(outs, got))


def front_backward_call(gathered, vec_in, layer, saved, g, vec_grads, final):
    ins = {"vec_in": vec_in, "sx": saved["x"], "sh": saved["h"], "vg_in": vec_grads}
    ins.update({"g" + n: g[n] for n in ("dq", "dk", "dv", "dk_in", "dv_in", "dza", "dx2")})
    outs = {
        "qkv": jax.ShapeDtypeStruct((3, WIDTH, WIDTH), BF),
        "dx": tok(F32),
    }
    if final:
        outs["vg_t"] = jax.ShapeDtypeStruct((1, WIDTH, BLOCK), F32)
    else:
        outs["vg"] = jax.ShapeDtypeStruct((8, WIDTH), F32)
    scratch = {
        "dk": vm(TOKENS, WIDTH),
        "dv": vm(TOKENS, WIDTH),
        "hid_t": vm(WIDTH, TOKENS),
        "sums": vm(8, WIDTH, dtype=F32),
        "dh": vm(TOKENS, WIDTH, dtype=F32),
    }
    if final:
        scratch["vg"] = vm(8, WIDTH, dtype=F32)

    def body(r):
        r.vg[...] = r.vg_in[...]
        s = SimpleNamespace(x=r.sx, h=r.sh)
        gg = SimpleNamespace(
            dq=r.gdq, dk=r.gdk, dv=r.gdv, dk_in=r.gdk_in, dv_in=r.gdv_in, dza=r.gdza, dx2=r.gdx2
        )
        layer_front_backward(r, r.w[layer], layer, s, gg, PlainGrads(r.qkv), r.dx)
        if final:
            tall = jnp.concatenate(
                [r.vg[...], jnp.zeros((BLOCK - 8, WIDTH), F32)], axis=0
            )
            r.vg_t[0] = jnp.transpose(tall)

    got = compute_call(
        body, "front_backward", [(layer, FRONT)], gathered, ins, outs, scratch
    )
    return dict(zip(outs, got))


GRAD_SETS = (
    ("up_a", ("up0", "up1"), (2, 1)),
    ("up_b", ("up2", "up3"), (2, 1)),
    ("down", ("down",), (1, 2)),
    ("mix", ("gf", "o", "ga"), (1, 2)),
    ("q", ("q",), (2, 1)),
    ("kv", ("k", "v"), (1, 2)),
)
LATE_SETS = ("q", "kv")
RESULT_UNITS = ("q", "k", "v", "o", "ga", "gf", "up0", "up1", "up2", "up3")

EARLY_ARRAYS = ("x2", "y", "gf", "gate", "a", "attn_t", "hid_t")
STREAMED = ("act_t", "slope")
ATTENTION_ARRAYS = ("q", "k", "v", "k1", "v1", "lse")


TICKS = ("gf", "c0", "c1", "c2", "c3", "norm", "mix", "p0", "p1", "p2", "p3", "kv", "end")
SCHEDULE = {
    "gf": ((1, 1, "q"), (1, 1, "kv")),
    "c0": ((1, 3, "down"),),
    "c1": ((1, 2, "mix"), (1, 3, "up_b")),
    "c2": ((0, 1, "up_a"), (1, 2, "q")),
    "norm": ((0, 1, "up_b"), (0, 1, "down"), (1, 3, "mix"), (1, 2, "kv")),
    "mix": ((1, 3, "q"),),
    "p0": ((0, 2, "up_a"), (0, 1, "mix")),
    "p1": ((1, 4, "up_a"), (1, 4, "up_b"), (1, 4, "down"), (1, 4, "mix")),
    "p2": ((0, 2, "up_b"), (1, 3, "kv"), (1, 4, "q")),
    "p3": ((0, 2, "down"), (0, 3, "up_a")),
}
LAST = (
    (0, 1, "q"),
    (0, 1, "kv"),
    (0, 3, "down"),
    (0, 1, "vec"),
    (0, 2, "mix"),
    (0, 2, "q"),
    (0, 3, "up_b"),
    (0, 2, "kv"),
    (0, 2, "vec"),
    (1, 4, "kv"),
    (0, 3, "mix"),
    (0, 3, "q"),
    (0, 4, "up_a"),
    (0, 4, "down"),
    (0, 4, "up_b"),
    (0, 3, "kv"),
    (0, 3, "vec"),
    (0, 4, "mix"),
    (0, 4, "q"),
    (0, 4, "kv"),
    (0, 4, "vec"),
)


def grad_set_list(dims, rows):
    out = []
    for layer in range(LAYERS):
        for name, units, order in GRAD_SETS:
            depth = 4 * rows if name == "down" else rows
            out.append((name, layer, units, order, (len(units), *dims, 2, depth, WIDTH), BF))
    out.append(("vec", 0, None, (1, 2), (1, *dims, 2, rows, BLOCK), F32))
    return out


class FusedGrads:
    def __init__(self, refs):
        self.refs = dict(zip((name for name, _, _ in GRAD_SETS), refs))
        self.place = {
            unit: (name, k) for name, units, _ in GRAD_SETS for k, unit in enumerate(units)
        }

    def unit(self, name, value):
        which, k = self.place[name]
        ref = self.refs[which]
        ref[k] = value.astype(BF).reshape(ref.shape[1:])

    def down(self, n, value):
        ref = self.refs["down"]
        part = ref.shape[1] // CHUNKS
        ref[0, n * part : (n + 1) * part] = value.astype(BF).reshape((part, *ref.shape[2:]))


BACKWARD_ARRAYS = {
    "x2": F32,
    "y": BF,
    "gf": F32,
    "gate": F32,
    "a": BF,
    "attn_t": BF,
    "hid_t": BF,
    "h_t": BF,
    "q": BF,
    "k": BF,
    "v": BF,
    "k1": BF,
    "v1": BF,
    "lse": F32,
}

FUSED_WORK = {
    "bias": BIAS_T,
    "dy": vm(TOKENS, WIDTH),
    "dz": vm(TOKENS, WIDTH),
    "act_t": vm(2, WIDTH, TOKENS),
    "slope": vm(2, TOKENS, WIDTH),
    "dh": vm(TOKENS, WIDTH, dtype=F32),
    "act": vm(TOKENS, WIDTH),
    "du": vm(TOKENS, WIDTH),
    "sums": vm(8, WIDTH, dtype=F32),
    "dattn": vm(TOKENS, WIDTH),
    "lse_t": vm(SLOTS, 8, BLOCK, dtype=F32),
    "dk_other": vm(TOKENS, BLOCK, dtype=F32),
    "dv_other": vm(TOKENS, BLOCK, dtype=F32),
    "vg": vm(8, WIDTH, dtype=F32),
    "vec": vm(8, WIDTH, dtype=F32),
    "dx": vm(TOKENS, WIDTH, dtype=F32),
    "dx2": vm(TOKENS, WIDTH, dtype=F32),
    "dza": vm(TOKENS, WIDTH),
    "dq": vm(TOKENS, WIDTH),
    "own_dk": vm(TOKENS, WIDTH, dtype=F32),
    "own_dv": vm(TOKENS, WIDTH, dtype=F32),
    "send_dk": vm(TOKENS, WIDTH),
    "send_dv": vm(TOKENS, WIDTH),
    "got_dk": vm(TOKENS, WIDTH),
    "got_dv": vm(TOKENS, WIDTH),
}


def backward_kernel(dims, num_seqs, *refs):
    refs = list(refs)

    def pop(count):
        out = refs[:count]
        del refs[:count]
        return out

    num_w = LAYERS * len(SETS)
    cot_in, x0_in, last_in = pop(3)
    weight_in = pop(num_w)
    saved_in = [{n: pop(1)[0] for n in saved_names(layer)} for layer in range(LAYERS)]
    (lengths,) = pop(1)
    res, res_down, res_vec, g_out, x_out = pop(5)
    weight_bufs = pop(len(SETS))
    (vec_buf,) = pop(1)
    bufs = dict(zip(BACKWARD_ARRAYS, pop(len(BACKWARD_ARRAYS))))
    r = SimpleNamespace(**dict(zip(FUSED_WORK, pop(len(FUSED_WORK)))))
    set_list = grad_set_list(dims, res_vec.shape[0])
    totals = pop(len(set_list))
    landings = pop(len(GRAD_SETS) + len(LATE_SETS) + 1)
    lines = pop(3 * len(set_list))
    sems = pop(6)
    weight_sem, array_sem, other_sem, stream_sem, dkv_send, dkv_recv = pop(6)
    back_sems = pop(3)
    r.lengths = lengths
    r.dk, r.dv, r.out = r.act, r.du, r.dattn

    place = Place(dims)
    core = place.core
    copies = {}

    def load(key, src, dst, sem):
        copy = pltpu.make_async_copy(src, dst, sem)
        copy.start()
        copies[key] = copy

    def need(*keys):
        for key in keys:
            copy = copies.pop(key, None)
            if copy is not None:
                copy.wait()

    unit_place = {
        name: (which, unit) for which, (names, _) in enumerate(SETS) for unit, name in enumerate(names)
    }
    flat_names = list(unit_place)

    def load_weights(layer, *names):
        for name in names:
            which, unit = unit_place[name]
            load(
                (layer, "w", name),
                weight_in[layer * len(SETS) + which].at[unit],
                weight_bufs[which].at[unit],
                weight_sem.at[layer, flat_names.index(name)],
            )

    array_names = list(BACKWARD_ARRAYS)

    def load_arrays(layer, *names):
        for name in names:
            src = saved_in[layer][name]
            load((layer, name), src, bufs[name], array_sem.at[layer, array_names.index(name)])

    def stream(layer, n):
        for k, name in enumerate(STREAMED):
            load(
                (layer, name, n),
                saved_in[layer][name].at[n],
                (r.act_t, r.slope)[k].at[n % 2],
                stream_sem.at[layer, k, n],
            )

    ffn_weights = ("gf", "o", "up0", "up1", "up2", "up3", "down")
    front_weights = ("q", "k", "v", "ga")
    last = LAYERS - 1
    load((last, "cot"), cot_in, r.dq, other_sem.at[0])
    load_arrays(last, "gf", "y", "x2", "hid_t")
    vec_src = weight_in[0].at[VEC_UNIT, :, :, :, :, :, pl.ds(0, BLOCK)]
    load("vec", vec_src, vec_buf, weight_sem.at[0, len(flat_names)])
    load_weights(last, *ffn_weights)
    stream(last, 0)
    stream(last, 1)
    load_arrays(last, "gate", "a", "attn_t", "h_t", *ATTENTION_ARRAYS)
    load_weights(last, *front_weights)
    load((last, "x"), saved_in[last - 1]["x3"], r.dx, other_sem.at[1])
    place.greet()

    def rows_of(ref):
        return lambda slot: ref.at[pl.ds(pl.multiple_of(slot * BLOCK, BLOCK), BLOCK)]

    back_x = TokenReturn(place, num_seqs, rows_of(last_in), x_out, back_sems, 1)
    back_x.start()

    sets = {}
    for k, (name, layer, units, order, _, _) in enumerate(set_list):

        def result(u, value, name=name, layer=layer, units=units):
            if name == "vec":
                res_vec[...] = value
            elif name == "down":
                res_down[layer] = value
            else:
                res[layer, RESULT_UNITS.index(units[u])] = value

        sets[(layer, name)] = PairReduce(
            place,
            totals[k],
            order,
            [landings[landing_index(name, layer)], *lines[3 * k : 3 * k + 3]],
            set_sems(sems, k),
            result,
        )
    stages = (None, "stage1", "stage2", "stage3", "finish")

    def act(layer, *events):
        for before, stage, name in events:
            if layer + before < LAYERS:
                getattr(sets[(layer + before, name)], stages[stage])()

    def ticker(layer):
        names = iter(TICKS)
        return lambda: act(layer, *SCHEDULE.get(next(names), ()))

    def ready_for(layer):
        def ready(*names):
            for name in names:
                sets[(layer, name)].start()

        return ready

    mask_setup(r, True)
    need("vec")
    r.vec[...] = jnp.transpose(vec_buf[...].reshape(WIDTH, BLOCK).astype(F32))[0:8, :]

    w = Gathered(weight_bufs)
    exchanges = []
    for layer in range(last, -1, -1):
        s = SimpleNamespace(**bufs)
        s.k = (bufs["k"], bufs["k1"])
        s.v = (bufs["v"], bufs["v1"])
        out = FusedGrads(totals[layer * len(GRAD_SETS) : (layer + 1) * len(GRAD_SETS)])
        out.dx2, out.dza, out.dq = r.dx2, r.dza, r.dq
        out.dk, out.dv, out.dk_out, out.dv_out = r.own_dk, r.own_dv, r.send_dk, r.send_dv
        dx_in = r.dq if layer == last else r.dx
        need((layer, "cot"), *((layer, n) for n in EARLY_ARRAYS), (layer, "h_t"))
        need(*((layer, "w", n) for n in ffn_weights))
        ready = ready_for(layer)
        tick = ticker(layer)

        def take(n, layer=layer):
            need((layer, "act_t", n), (layer, "slope", n))

        def drop(n, layer=layer):
            if n + 2 < CHUNKS:
                stream(layer, n + 2)
            elif layer:
                stream(layer - 1, n + 2 - CHUNKS)

        kept = SimpleNamespace(
            hid_t=bufs["hid_t"],
            attn_t=bufs["attn_t"],
            h_t=bufs["h_t"],
            act_t=lambda n: r.act_t.at[n % 2],
            slope=lambda n: r.slope.at[n % 2],
            take=take,
            drop=drop,
        )
        ffn_backward(r, w, layer, dx_in, s, out, tick, ready, kept)
        if layer:
            load_arrays(layer - 1, *EARLY_ARRAYS)
            load_weights(layer - 1, *ffn_weights)
        else:
            load((0, "x"), x0_in, r.dz, other_sem.at[2])
        need(*((layer, n) for n in ATTENTION_ARRAYS))
        for copy in exchanges:
            copy.wait_send()
        attention_backward(r, s, out, tick)
        if layer:
            load_arrays(layer - 1, *ATTENTION_ARRAYS)
        exchanges = []
        for k, (src, dst) in enumerate(((r.send_dk, r.got_dk), (r.send_dv, r.got_dv))):
            copy = remote(
                src,
                dst,
                dkv_send.at[layer, k],
                dkv_recv.at[layer, k],
                place.sibling(),
            )
            copy.start()
            exchanges.append(copy)
        need(*((layer, "w", n) for n in front_weights), (layer, "x"))
        g = SimpleNamespace(
            dq=r.dq,
            dk=r.own_dk,
            dv=r.own_dv,
            dk_in=r.got_dk,
            dv_in=r.got_dv,
            dza=r.dza,
            dx2=r.dx2,
        )

        def arrived(pair=tuple(exchanges)):
            for copy in pair:
                copy.wait_recv()

        s.x = r.dx if layer else r.dz
        layer_front_backward(r, w, layer, s, g, out, r.dx, arrived, tick, ready, bufs["h_t"])
        if layer:
            load_arrays(layer - 1, "h_t")
            load_weights(layer - 1, *front_weights)

    r.out[...] = r.dx[...].astype(BF)
    back = TokenReturn(place, num_seqs, rows_of(r.out), g_out, back_sems, 0)
    back.start()
    tall = jnp.concatenate([r.vg[...], jnp.zeros((BLOCK - 8, WIDTH), F32)], axis=0)
    totals[-1][0] = jnp.transpose(tall).reshape(totals[-1].shape[1:])
    ready_for(0)("vec")
    act(0, *LAST)
    for one in sets.values():
        one.finish_sends()
    for copy in exchanges:
        copy.wait_send()
    back.finish()
    back_x.finish()


def landing_index(name, layer):
    names = [one[0] for one in GRAD_SETS]
    if name == "vec":
        return len(names) + len(LATE_SETS)
    if name in LATE_SETS and layer:
        return len(names) + LATE_SETS.index(name)
    return names.index(name)


def backward(dims, rows, lengths, positions, cot, x0, result, units, saved):
    num_seqs = lengths.shape[0]
    per_dev = positions // BLOCK
    dma = pltpu.SemaphoreType.DMA
    scratch = [
        vm(len(names), *dims, 2, 4 * rows if names[0] == "down" else rows, WIDTH) for names, _ in SETS
    ]
    scratch += [vm(*dims, 2, rows, BLOCK)]
    scratch += [vm(*layer_shape(n), dtype=t) for n, t in BACKWARD_ARRAYS.items()]
    scratch += list(FUSED_WORK.values())
    set_list = grad_set_list(dims, rows)
    scratch += [vm(*s, dtype=t) for *_, s, t in set_list]
    landings, lines = {}, []
    for name, layer, _, order, (count, num_z, num_x, num_y, _, *block), dtype in set_list:
        landings[landing_index(name, layer)] = vm(count, num_z, num_x, num_y, *block, dtype=dtype)
        lines.append(vm(count, num_z, 2, *block, dtype=dtype))
        lines.append(vm(count, num_z, *block, dtype=dtype))
        lines.append(vm(num_z - 1, count, *block, dtype=dtype))
    scratch += [landings[k] for k in sorted(landings)] + lines
    scratch += pair_reduce_sems(len(set_list))
    scratch += [
        dma((LAYERS, 16)),
        dma((LAYERS, len(BACKWARD_ARRAYS))),
        dma((3,)),
        dma((LAYERS, 2, CHUNKS)),
        dma((LAYERS, 2)),
        dma((LAYERS, 2)),
    ]
    scratch += return_sems(2, num_seqs, per_dev)
    arrays = [saved[layer][n] for layer in range(LAYERS) for n in saved_names(layer)]
    return pl.pallas_call(
        partial(backward_kernel, dims, num_seqs),
        out_shape=[
            jax.ShapeDtypeStruct((LAYERS, len(RESULT_UNITS), rows, WIDTH), F32),
            jax.ShapeDtypeStruct((LAYERS, 4 * rows, WIDTH), F32),
            jax.ShapeDtypeStruct((rows, BLOCK), F32),
            jax.ShapeDtypeStruct((num_seqs, positions, WIDTH), BF),
            jax.ShapeDtypeStruct((num_seqs, positions, WIDTH), BF),
        ],
        in_specs=[ANY] * (3 + len(units) + len(arrays)) + [SMEM],
        out_specs=[VMEM] * 3 + [ANY] * 2,
        scratch_shapes=scratch,
        compiler_params=pltpu.CompilerParams(
            collective_id=1, has_side_effects=True, vmem_limit_bytes=BACKWARD_VMEM
        ),
        name="backward",
    )(cot, x0, result, *units, *arrays, lengths)


def unpack_kernel(*refs):
    res, res_down, res_vec, x_in, g_in = refs[:5]
    x_out, g_out = refs[5:7]
    ga, wq, wk, wv, wo, wga, ba, gf, wup, wdown, wgf, bf = refs[7:19]
    square = refs[19]
    x_out[...] = x_in[...]
    g_out[...] = g_in[...].astype(F32)
    plain = {"q": wq, "k": wk, "v": wv, "o": wo, "ga": wga, "gf": wgf}
    for layer in range(LAYERS):
        for k, name in enumerate(RESULT_UNITS):
            if name in plain:
                plain[name][layer] = res[layer, k]
            else:
                n = int(name[2:])
                wup[layer, :, n * WIDTH : (n + 1) * WIDTH] = res[layer, k]
        wdown[layer] = res_down[layer]
    rows = res_vec.shape[0]
    square[...] = jnp.zeros_like(square)
    square[0:rows, :] = res_vec[...]
    turned = jnp.transpose(square[...])
    for layer in range(LAYERS):
        for which, ref in enumerate((ga, ba, gf, bf)):
            row = layer * 4 + which
            ref[layer : layer + 1, :] = turned[row : row + 1, 0:rows]


def unpack(res, res_down, res_vec, x_out, g_out):
    rows = res_vec.shape[0]
    vector = jax.ShapeDtypeStruct((LAYERS, rows), F32)
    matrix = jax.ShapeDtypeStruct((LAYERS, rows, WIDTH), F32)
    outs = [
        jax.ShapeDtypeStruct(x_out.shape, x_out.dtype),
        jax.ShapeDtypeStruct(g_out.shape, F32),
        vector,
        matrix,
        matrix,
        matrix,
        matrix,
        matrix,
        vector,
        vector,
        jax.ShapeDtypeStruct((LAYERS, rows, CHUNKS * WIDTH), F32),
        jax.ShapeDtypeStruct((LAYERS, CHUNKS * rows, WIDTH), F32),
        matrix,
        vector,
    ]
    return pl.pallas_call(
        unpack_kernel,
        out_shape=outs,
        in_specs=[VMEM] * 5,
        out_specs=[VMEM] * 14,
        scratch_shapes=[vm(BLOCK, BLOCK, dtype=F32)],
        name="unpack",
    )(res, res_down, res_vec, x_out, g_out)


def plain_forward(gathered, vec_in, lengths, x_tok, exchange):
    x = x_tok.reshape(TOKENS, WIDTH)
    front = front_call(gathered, vec_in, 0, x)
    saved = []
    for layer in range(LAYERS):
        front["k1"], front["v1"] = exchange(front["k"], front["v"])
        got = middle_call(gathered, vec_in, lengths, layer, x, front)
        keep = dict(front)
        keep.update({n: got[n] for n in ("attn", "lse", "a", "x2", "y", "gf")})
        keep["x"] = x
        saved.append(keep)
        x = got["x3"]
        front = {n[1:]: got[n] for n in ("nh", "nq", "nk", "nv", "ngate") if n in got}
    return saved, x.astype(BF).reshape(SLOTS, BLOCK, WIDTH)


def per_device(num_dp, num_sp, *args):
    inputs, lengths, gain_a, wq, wk, wv, wo, wga, ba, gain_f, wup, wdown, wgf, bf, cotangent = args
    num_y = num_sp // 2
    num_x = num_y
    dims = (num_dp // num_x, num_x, num_y)
    rows = wq.shape[1]
    weights = (wq, wk, wv, wo, wga, wgf, wup, wdown)
    if rows % 16 == 0 and dims[0] % CHUNKS == 0 and num_x == num_y == 2:
        cot, last, x0, units, saved = forward(
            dims, inputs, cotangent, weights, (gain_a, ba, gain_f, bf), lengths
        )
        *summed, g_out, x_out = backward(
            dims, rows, lengths, inputs.shape[1], cot, x0, last, units, saved
        )
        return tuple(unpack(*summed, x_out, g_out))
    vectors = jnp.stack(
        [v[layer] for layer in range(LAYERS) for v in (gain_a, ba, gain_f, bf)], axis=1
    )
    vecs = jnp.pad(vectors, ((0, 0), (0, WIDTH - vectors.shape[1])))
    x_tok, cot_tok, *units = collect(dims, inputs, cotangent, weights, vecs)
    gathered = {}
    for layer in range(LAYERS):
        gathered[layer] = [
            u.reshape(u.shape[0], -1, WIDTH)
            for u in units[len(SETS) * layer : len(SETS) * (layer + 1)]
        ]
    vec_in = gathered[0][0][VEC_UNIT, :, :BLOCK]

    swap = [(i, i ^ 1) for i in range(num_sp)]

    def exchange(*arrays):
        return [lax.ppermute(a, "sp", swap) for a in arrays]

    saved, layer_out = plain_forward(gathered, vec_in, lengths, x_tok, exchange)

    dx = cot_tok.reshape(TOKENS, WIDTH)
    vec_grads = None
    grads = [None] * LAYERS
    for layer in reversed(range(LAYERS)):
        g = backward_call(gathered, vec_in, lengths, layer, dx, saved[layer])
        g["dk_in"], g["dv_in"] = exchange(g["dk_out"], g["dv_out"])
        vec_grads = g["vg"] if vec_grads is None else vec_grads + g["vg"]
        got = front_backward_call(gathered, vec_in, layer, saved[layer], g, vec_grads, layer == 0)
        dx = got["dx"]
        grads[layer] = (
            jnp.concatenate([got["qkv"], g["ga"][3:]], axis=0),
            g["gb"],
            g["gd"],
        )
        vec_grads = got["vg"] if layer else got["vg_t"]

    flat = [arr for layer in range(LAYERS) for arr in grads[layer]] + [vec_grads]
    toks = [dx.reshape(SLOTS, BLOCK, WIDTH), layer_out]
    *summed, g_out, x_out = spread(dims, inputs.shape[0], flat, toks)
    a, b, d = ([summed[3 * layer + k] for layer in range(LAYERS)] for k in range(3))

    def unit(k):
        return jnp.stack([a[layer][k] for layer in range(LAYERS)])

    def vector(which):
        return jnp.stack([summed[6][0, :, layer * 4 + which] for layer in range(LAYERS)])

    grad_up = jnp.stack(
        [
            jnp.concatenate([a[layer][6], b[layer][0], b[layer][1], b[layer][2]], axis=1)
            for layer in range(LAYERS)
        ]
    )
    grad_down = jnp.stack([d[layer][0] for layer in range(LAYERS)])
    return (
        x_out,
        g_out,
        vector(0),
        unit(0),
        unit(1),
        unit(2),
        unit(3),
        unit(4),
        vector(1),
        vector(2),
        grad_up,
        grad_down,
        unit(5),
        vector(3),
    )


def solution(mesh):
    tokens = P("dp", "sp", None)
    vector = P(None, ("dp", "sp"))
    matrix = P(None, ("dp", "sp"), None)
    return jax.shard_map(
        partial(per_device, mesh.shape["dp"], mesh.shape["sp"]),
        mesh=mesh,
        in_specs=(
            tokens,
            P("dp", None),
            vector,
            matrix,
            matrix,
            matrix,
            matrix,
            matrix,
            vector,
            vector,
            matrix,
            matrix,
            matrix,
            vector,
            tokens,
        ),
        out_specs=(
            tokens,
            tokens,
            vector,
            matrix,
            matrix,
            matrix,
            matrix,
            matrix,
            vector,
            vector,
            matrix,
            matrix,
            matrix,
            vector,
        ),
        check_vma=False,
    )
```

```python
from functools import partial
from types import SimpleNamespace

import jax
import jax.numpy as jnp
from jax import lax
from jax.experimental import pallas as pl
from jax.experimental.pallas import tpu as pltpu
from jax.sharding import PartitionSpec as P

LEN = 1024
LAYERS = 2
WIDTH = 512
HEAD_DIM = 64
BLOCK = 128
SLOTS = LEN // (2 * BLOCK)
TOKENS = SLOTS * BLOCK
HALF = TOKENS // 2
PAIRS = WIDTH // (2 * HEAD_DIM)
CHUNKS = 4
EPSILON = 1e-05
NEG_FILL = -1e30
F32 = jnp.float32
BF = jnp.bfloat16
MESH = pl.DeviceIdType.MESH
VMEM_BYTES = 56 * 1024 * 1024
BACKWARD_VMEM = 62 * 1024 * 1024

ANY = pl.BlockSpec(memory_space=pl.ANY)
VMEM = pl.BlockSpec(memory_space=pltpu.VMEM)
SMEM = pl.BlockSpec(memory_space=pltpu.SMEM)

SETS = (
    (("k", "v"), (2, 1)),
    (("q", "ga"), (2, 1)),
    (("up0", "up1", "up2", "up3"), (2, 1)),
    (("o", "gf"), (1, 2)),
    (("down",), (1, 2)),
)
VEC_UNIT = len(SETS[0][0])
UNITS_A = 7
UNITS_B = 3


class Place:
    def __init__(self, dims):
        self.dims = dims
        num_z, num_x, num_y = dims
        self.dp = lax.axis_index("dp")
        self.sp = lax.axis_index("sp")
        self.at = (
            lax.div(self.dp, num_x),
            lax.rem(self.dp, num_x),
            lax.div(self.sp, 2),
            lax.rem(self.sp, 2),
        )
        self.z, self.x, self.y, self.core = self.at

    def device(self, axis=None, position=None):
        z, x, y, core = [position if k == axis else v for k, v in enumerate(self.at)]
        return (z * self.dims[1] + x, y * 2 + core)

    def sibling(self):
        return self.device(3, 1 - self.core)

    def greet(self):
        barrier = pltpu.get_barrier_semaphore()
        count = jnp.int32(0)
        for axis in (0, 1):
            reach = self.dims[0] - 1 if axis == 0 else 1
            for step in [s for s in range(-reach, reach + 1) if s]:
                position = self.at[axis] + step
                there = (position >= 0) & (position < self.dims[axis])

                @pl.when(there)
                def _(axis=axis, position=position):
                    pl.semaphore_signal(
                        barrier, inc=1, device_id=self.device(axis, position), device_id_type=MESH
                    )

                count = count + there.astype(jnp.int32)
        num_sp = self.dims[2] * 2
        for step in range(1, num_sp):
            other = lax.rem(self.sp + step, num_sp)
            pl.semaphore_signal(barrier, inc=1, device_id=(self.dp, other), device_id_type=MESH)
        pl.semaphore_wait(barrier, count + (num_sp - 1))


def remote(src, dst, send_sem, recv_sem, device):
    return pltpu.make_async_remote_copy(
        src_ref=src,
        dst_ref=dst,
        send_sem=send_sem,
        recv_sem=recv_sem,
        device_id=device,
        device_id_type=MESH,
    )


def when(cond, action):
    if cond is True:
        action()
    elif cond is not False:
        pl.when(cond)(action)


def both(*conds):
    out = True
    for cond in conds:
        if cond is False:
            return False
        if cond is not True:
            out = cond if out is True else out & cond
    return out


class GatherSet:
    def __init__(self, place, ref, order, sems):
        self.place, self.ref, self.order = place, ref, order
        self.z_send, self.z_recv, self.s_send, self.s_recv, self.c_send, self.c_recv = sems
        self.sends = []

    def put(self, src, send_sem, recv_sem, device, cond):
        copy = remote(src, src, send_sem, recv_sem, device)
        when(cond, copy.start)
        self.sends.append((cond, copy))

    def got(self, src, send_sem, recv_sem, cond):
        copy = remote(src, src, send_sem, recv_sem, self.place.sibling())
        when(cond, copy.wait_recv)

    def z_block(self, zb):
        return self.ref.at[:, zb, self.place.x, self.place.y, self.place.core]

    def stage_block(self, stage, zb, q):
        axis = self.order[stage]
        index = [zb, self.place.x, self.place.y, self.place.core]
        if stage == 1:
            index[self.order[0]] = slice(None)
        index[axis] = q
        return self.ref.at[(slice(None), *index)]

    def phase_z(self, t, side, zb, valid):
        num = self.place.dims[0]
        z = self.place.z
        if t > 0:
            self.got(self.z_block(zb), self.z_send.at[0, zb], self.z_recv.at[zb], valid)
        if (t == 0 or side == 0) and t <= num - 2:
            self.put(
                self.z_block(zb),
                self.z_send.at[1, zb],
                self.z_recv.at[zb],
                self.place.device(0, z + 1),
                both(valid, z < num - 1),
            )
        if (t == 0 or side == 1) and t <= num - 2:
            self.put(
                self.z_block(zb),
                self.z_send.at[0, zb],
                self.z_recv.at[zb],
                self.place.device(0, z - 1),
                both(valid, z > 0),
            )

    def stage_start(self, stage, zb, valid):
        axis = self.order[stage]
        p, num = self.place.at[axis], self.place.dims[axis]
        for way, cond in ((0, p > 0), (1, p < num - 1)):
            self.put(
                self.stage_block(stage, zb, p),
                self.s_send.at[stage, way, zb, p],
                self.s_recv.at[stage, zb, p],
                self.place.device(axis, p + 2 * way - 1),
                both(valid, cond),
            )

    def stage_finish(self, stage, zb, valid):
        axis = self.order[stage]
        p, num = self.place.at[axis], self.place.dims[axis]
        for u in range(1, num):
            for side in (0, 1):
                q = p - u if side == 0 else p + u
                there = both(valid, q >= 0 if side == 0 else q < num)
                block = self.stage_block(stage, zb, q)
                self.got(
                    block,
                    self.s_send.at[stage, side, zb, q],
                    self.s_recv.at[stage, zb, q],
                    there,
                )
                if u <= num - 2:
                    way = 1 - side
                    self.put(
                        block,
                        self.s_send.at[stage, way, zb, q],
                        self.s_recv.at[stage, zb, q],
                        self.place.device(axis, p + 2 * way - 1),
                        both(there, p < num - 1 if way == 1 else p > 0),
                    )

    def core_start(self, zb, valid):
        block = self.ref.at[:, zb, :, :, self.place.core]
        self.put(block, self.c_send.at[zb], self.c_recv.at[zb], self.place.sibling(), valid)

    def core_finish(self, zb, valid):
        block = self.ref.at[:, zb, :, :, 1 - self.place.core]
        self.got(block, self.c_send.at[zb], self.c_recv.at[zb], valid)

    def finish_sends(self):
        for cond, copy in self.sends:
            when(cond, copy.wait_send)


class PairGather:
    def __init__(self, place, ref, order, sems):
        self.place, self.ref, self.order = place, ref, order
        self.z_send, self.z_recv, self.s_send, self.s_recv, self.c_send, self.c_recv = sems
        self.sends = []

    def put(self, src, send_sem, recv_sem, device):
        copy = remote(src, src, send_sem, recv_sem, device)
        copy.start()
        self.sends.append(copy)

    def got(self, src, send_sem, recv_sem):
        remote(src, src, send_sem, recv_sem, self.place.sibling()).wait_recv()

    def own(self, zb):
        return self.ref.at[:, zb, self.place.x, self.place.y, self.place.core]

    def block(self, stage, zb, near):
        index = [zb, self.place.x, self.place.y, self.place.core]
        if stage == 1:
            index[self.order[0]] = slice(None)
        axis = self.order[stage]
        index[axis] = self.place.at[axis] if near else 1 - self.place.at[axis]
        return self.ref.at[(slice(None), *index)]

    def source(self, t):
        num = self.place.dims[0]
        return lax.rem(self.place.z + (num - t), num)

    def open(self):
        num = self.place.dims[0]
        z = self.place.z
        self.send_stage(0, 0)
        for t in range(1, num):
            target = lax.rem(z + t, num)
            self.put(
                self.own(z),
                self.z_send.at[t - 1],
                self.z_recv.at[t - 1],
                self.place.device(0, target),
            )

    def send_stage(self, stage, t):
        axis = self.order[stage]
        self.put(
            self.block(stage, self.source(t), True),
            self.s_send.at[stage, t],
            self.s_recv.at[stage, t],
            self.place.device(axis, 1 - self.place.at[axis]),
        )

    def got_stage(self, stage, t):
        block = self.block(stage, self.source(t), False)
        self.got(block, self.s_send.at[stage, t], self.s_recv.at[stage, t])

    def stage1(self, *steps):
        for t in steps:
            self.got(self.own(self.source(t)), self.z_send.at[t - 1], self.z_recv.at[t - 1])
            self.send_stage(0, t)

    def stage2(self, *steps):
        for t in steps:
            self.got_stage(0, t)
            self.send_stage(1, t)

    def stage3(self, *steps):
        for t in steps:
            self.got_stage(1, t)
            block = self.ref.at[:, self.source(t), :, :, self.place.core]
            self.put(block, self.c_send.at[t], self.c_recv.at[t], self.place.sibling())

    def finish(self):
        for t in range(self.place.dims[0]):
            block = self.ref.at[:, self.source(t), :, :, 1 - self.place.core]
            self.got(block, self.c_send.at[t], self.c_recv.at[t])

    def finish_sends(self):
        for copy in self.sends:
            copy.wait_send()


def pair_gather_sems(num_sets, num_z):
    dma = pltpu.SemaphoreType.DMA
    return [
        dma((num_sets, num_z - 1)),
        dma((num_sets, num_z - 1)),
        dma((num_sets, 2, num_z)),
        dma((num_sets, 2, num_z)),
        dma((num_sets, num_z)),
        dma((num_sets, num_z)),
    ]


class PairReduce:
    def __init__(self, place, ref, order, bufs, sems, result):
        self.place, self.ref, self.order, self.result = place, ref, order, result
        self.from_core, self.line1, self.line2, self.line_z = bufs
        self.c_send, self.c_recv, self.s_send, self.s_recv, self.z_send, self.z_recv = sems
        self.sends = []

    def put(self, src, dst, send_sem, recv_sem, device):
        copy = remote(src, dst, send_sem, recv_sem, device)
        copy.start()
        return copy

    def cut(self, core, x=slice(None), y=slice(None)):
        return self.ref.at[:, :, x, y, core]

    def axis_cut(self, stage, near):
        at = [slice(None), slice(None), slice(None)]
        if stage == 1:
            at[self.order[0]] = self.place.at[self.order[0]]
        axis = self.order[stage]
        at[axis] = self.place.at[axis] if near else 1 - self.place.at[axis]
        return self.cut(self.place.core, at[1], at[2])

    def wait(self, buf, send_sem, recv_sem):
        remote(buf, buf, send_sem, recv_sem, self.place.sibling()).wait_recv()

    def start(self):
        copy = self.put(
            self.cut(1 - self.place.core),
            self.from_core,
            self.c_send,
            self.c_recv,
            self.place.sibling(),
        )
        self.sends.append(copy)

    def send_stage(self, stage):
        axis = self.order[stage]
        copy = self.put(
            self.axis_cut(stage, False),
            (self.line1, self.line2)[stage],
            self.s_send.at[stage],
            self.s_recv.at[stage],
            self.place.device(axis, 1 - self.place.at[axis]),
        )
        self.sends.append(copy)

    def stage1(self):
        self.wait(self.from_core, self.c_send, self.c_recv)
        add_units(self.cut(self.place.core), self.from_core)
        self.send_stage(0)

    def stage2(self):
        self.wait(self.line1, self.s_send.at[0], self.s_recv.at[0])
        add_units(self.axis_cut(0, True), self.line1)
        self.send_stage(1)

    def stage3(self):
        self.wait(self.line2, self.s_send.at[1], self.s_recv.at[1])
        place = self.place
        num = place.dims[0]
        add_units(self.axis_cut(1, True), self.line2)
        for t in range(num - 1, 0, -1):
            target = lax.rem(place.z + t, num)
            self.put(
                self.ref.at[:, target, place.x, place.y, place.core],
                self.line_z.at[t - 1],
                self.z_send,
                self.z_recv,
                place.device(0, target),
            )
        self.sends.append(
            remote(self.line_z, self.line_z, self.z_send, self.z_recv, place.sibling())
        )

    def finish(self):
        place = self.place
        mine = self.ref.at[:, place.z, place.x, place.y, place.core]
        self.wait(self.line_z, self.z_send, self.z_recv)
        for u in range(mine.shape[0]):
            value = mine[u].astype(F32)
            for slot in range(place.dims[0] - 1):
                value = value + self.line_z[slot, u].astype(F32)
            self.result(u, value)

    def finish_sends(self):
        for copy in self.sends:
            copy.wait_send()


def pair_reduce_sems(num_sets):
    dma = pltpu.SemaphoreType.DMA
    return [
        dma((num_sets,)),
        dma((num_sets,)),
        dma((num_sets, 2)),
        dma((num_sets, 2)),
        dma((num_sets,)),
        dma((num_sets,)),
    ]


def z_items(place, far_first):
    num = place.dims[0]
    order = range(num - 1, -1, -1) if far_first else range(num)
    rounds = []
    for t in order:
        if t == 0:
            rounds.append([(0, 0, place.z, True)])
        else:
            rounds.append(
                [(t, 0, place.z - t, place.z - t >= 0), (t, 1, place.z + t, place.z + t < num)]
            )
    return rounds


def pipeline(rounds, phases):
    for k in range(len(rounds) + len(phases) - 1):
        for lag, phase in enumerate(phases):
            if 0 <= k - lag < len(rounds):
                for item in rounds[k - lag]:
                    phase(*item)


def gather_sems(num_sets, dims):
    num_z, num_x, num_y = dims
    line = max(num_x, num_y)
    dma = pltpu.SemaphoreType.DMA
    return [
        dma((num_sets, 2, num_z)),
        dma((num_sets, num_z)),
        dma((num_sets, 2, 2, num_z, line)),
        dma((num_sets, 2, num_z, line)),
        dma((num_sets, num_z)),
        dma((num_sets, num_z)),
    ]


def set_sems(sems, k):
    return [sem.at[k] for sem in sems]


def run_gather(place, sets):
    def each(method):
        def phase(t, side, zb, valid):
            for one in sets:
                method(one, t, side, zb, valid)

        return phase

    def phase_one(one, t, side, zb, valid):
        one.phase_z(t, side, zb, valid)
        one.stage_start(0, zb, valid)

    def phase_two(one, t, side, zb, valid):
        one.stage_finish(0, zb, valid)
        one.stage_start(1, zb, valid)

    def phase_three(one, t, side, zb, valid):
        one.stage_finish(1, zb, valid)
        one.core_start(zb, valid)

    def phase_four(one, t, side, zb, valid):
        one.core_finish(zb, valid)

    pipeline(
        z_items(place, False), [each(phase_one), each(phase_two), each(phase_three), each(phase_four)]
    )
    for one in sets:
        one.finish_sends()


def own_shards(weights, vecs, layer):
    wq, wk, wv, wo, wga, wgf, wup, wdown = weights
    plain = {"q": wq, "k": wk, "v": wv, "o": wo, "ga": wga, "gf": wgf, "down": wdown}
    out = []
    for which, (names, _) in enumerate(SETS):
        for unit, name in enumerate(names):
            if name in plain:
                out.append((which, unit, plain[name].at[layer]))
            else:
                out.append((which, unit, wup.at[layer, :, pl.ds(int(name[2:]) * WIDTH, WIDTH)]))
    if layer == 0 and vecs is not None:
        out.append((0, VEC_UNIT, vecs))
    return out


OWN_COPIES = LAYERS * sum(len(names) for names, _ in SETS) + 1


def set_shapes(dims, rows):
    shapes = []
    for layer in range(LAYERS):
        for which, (names, _) in enumerate(SETS):
            count = len(names) + (layer == 0 and which == 0)
            depth = 4 * rows if names[0] == "down" else rows
            shapes.append((count, *dims, 2, depth, WIDTH))
    return shapes


def start_own(place, weights, vecs, refs, sem, layers=range(LAYERS), first=0):
    copies = []
    for layer in layers:
        for which, unit, src in own_shards(weights, vecs, layer):
            dst = refs[layer * len(SETS) + which].at[(unit, *place.at)]
            copy = pltpu.make_async_copy(src, dst, sem.at[first + len(copies)])
            copy.start()
            copies.append(copy)
    return copies


def gather_sets(place, refs, sems):
    return [
        GatherSet(place, ref, SETS[k % len(SETS)][1], set_sems(sems, k)) for k, ref in enumerate(refs)
    ]


class TokenMove:
    def __init__(self, place, num_seqs, src, dst_slot, sems, which):
        self.place, self.num_seqs, self.src, self.dst_slot = place, num_seqs, src, dst_slot
        self.send_sem, self.recv_sem, self.local_sem = (s.at[which] for s in sems)
        self.per_dev = LEN // (place.dims[2] * 2) // BLOCK
        self.sends = []

    def start(self):
        for seq in range(self.num_seqs):
            for i in range(self.per_dev):
                g = self.place.sp * self.per_dev + i
                target = seq * 2 + lax.rem(g, 2)
                here = target == self.place.sp
                block = self.src.at[seq, pl.ds(i * BLOCK, BLOCK)]
                slot = self.dst_slot(lax.div(g, 2))
                copy = remote(
                    block,
                    slot,
                    self.send_sem.at[seq, i],
                    self.recv_sem.at[lax.div(g, 2)],
                    (self.place.dp, target),
                )
                local = pltpu.make_async_copy(block, slot, self.local_sem.at[seq, i])
                when(jnp.logical_not(here), copy.start)
                when(here, local.start)
                self.sends.append((here, copy, local))

    def finish(self):
        for here, copy, local in self.sends:
            when(jnp.logical_not(here), copy.wait_send)
            when(here, local.wait)
        for slot in range(SLOTS):
            source = lax.div(2 * slot + self.place.core, self.per_dev)
            goal = self.dst_slot(slot)
            arrived = remote(
                goal, goal, self.send_sem.at[0, 0], self.recv_sem.at[slot], self.place.sibling()
            )
            when(source != self.place.sp, arrived.wait_recv)


def collect_kernel(dims, num_seqs, *refs):
    inputs, cotangent = refs[:2]
    weights, vecs = refs[2:10], refs[10]
    x_out, cot_out = refs[11:13]
    count = LAYERS * len(SETS)
    sets = refs[13 : 13 + count]
    sems = refs[13 + count : 19 + count]
    own_sem, *tok_sems = refs[19 + count :]
    place = Place(dims)
    own = start_own(place, weights, vecs, sets, own_sem)
    place.greet()
    moves = []
    for which, (src, dst) in enumerate(((inputs, x_out), (cotangent, cot_out))):
        moves.append(TokenMove(place, num_seqs, src, lambda s, dst=dst: dst.at[s], tok_sems, which))
        moves[-1].start()
    for copy in own:
        copy.wait()
    run_gather(place, gather_sets(place, sets, sems))
    for move in moves:
        move.finish()


def token_sems(num_seqs, per_dev):
    dma = pltpu.SemaphoreType.DMA
    return [dma((2, num_seqs, per_dev)), dma((2, SLOTS)), dma((2, num_seqs, per_dev))]


def collect(dims, inputs, cotangent, weights, vecs):
    rows = weights[0].shape[1]
    num_seqs = inputs.shape[0]
    tok = jax.ShapeDtypeStruct((SLOTS, BLOCK, WIDTH), BF)
    outs = [tok, tok] + [jax.ShapeDtypeStruct(s, BF) for s in set_shapes(dims, rows)]
    return pl.pallas_call(
        partial(collect_kernel, dims, num_seqs),
        out_shape=outs,
        in_specs=[ANY] * 11,
        out_specs=[ANY] * len(outs),
        scratch_shapes=gather_sems(len(SETS) * LAYERS, dims)
        + [pltpu.SemaphoreType.DMA((OWN_COPIES,))]
        + token_sems(num_seqs, inputs.shape[1] // BLOCK),
        compiler_params=pltpu.CompilerParams(
            collective_id=0, has_side_effects=True, vmem_limit_bytes=VMEM_BYTES
        ),
        name="collect",
    )(inputs, cotangent, *weights, vecs)


def add_units(total, part):
    count = total.shape[0]

    def body(u, carry):
        total[u] = total[u] + part[u]
        return carry

    lax.fori_loop(0, count, body, 0)


class ReduceSet:
    def __init__(self, place, total, other, mine, order, bufs, sems, result):
        self.place, self.total, self.other, self.mine, self.order = place, total, other, mine, order
        self.from_core, self.line1, self.line2, self.line_z = bufs
        self.c_send, self.c_recv, self.s_send, self.s_recv, self.z_send, self.z_recv = sems
        self.result = result
        self.sends = []

    def put(self, src, dst, send_sem, recv_sem, device, cond):
        copy = remote(src, dst, send_sem, recv_sem, device)
        when(cond, copy.start)
        self.sends.append((cond, copy))

    def core_copy(self, zb):
        return remote(
            self.other(zb),
            self.from_core.at[:, zb],
            self.c_send.at[zb],
            self.c_recv.at[zb],
            self.place.sibling(),
        )

    def start(self, zb, valid):
        copy = self.core_copy(zb)
        when(valid, copy.start)
        if self.mine is not None:
            when(valid, self.mine(zb).start)
        self.sends.append((valid, copy))

    def core_finish(self, zb, valid):
        def go():
            if self.mine is not None:
                self.mine(zb).wait()
            self.core_copy(zb).wait_recv()
            add_units(self.total(zb, slice(None), slice(None)), self.from_core.at[:, zb])

        when(valid, go)

    def block(self, stage, zb, q):
        index = [zb, self.place.x, self.place.y]
        if stage == 0:
            index[self.order[1]] = slice(None)
        index[self.order[stage]] = q
        return self.total(*index)

    def line(self, stage, way, zb, slot):
        if self.place.dims[self.order[stage]] == 2:
            way = 0
        return (self.line1, self.line2)[stage].at[way, slot, :, zb]

    def take(self, stage, way, zb, q, cond):
        slot = q - 1 if way == 0 else q
        buf = self.line(stage, way, zb, slot)
        copy = remote(
            buf,
            buf,
            self.s_send.at[stage, way, zb, slot],
            self.s_recv.at[stage, way, zb, slot],
            self.place.sibling(),
        )

        def go():
            copy.wait_recv()
            add_units(self.block(stage, zb, q), buf)

        when(cond, go)

    def stage_send(self, stage, zb, valid):
        axis = self.order[stage]
        p, num = self.place.at[axis], self.place.dims[axis]
        for u in range(num - 1, 0, -1):
            for side in (0, 1):
                q = p - u if side == 0 else p + u
                there = both(valid, q >= 0 if side == 0 else q < num)
                way = 1 - side
                if u <= num - 2:
                    self.take(stage, way, zb, q, both(there, p > 0 if side == 1 else p < num - 1))
                slot = q - 1 if side == 1 else q
                self.put(
                    self.block(stage, zb, q),
                    self.line(stage, way, zb, slot),
                    self.s_send.at[stage, way, zb, slot],
                    self.s_recv.at[stage, way, zb, slot],
                    self.place.device(axis, p + 1 if side == 1 else p - 1),
                    there,
                )

    def stage_keep(self, stage, zb, valid):
        axis = self.order[stage]
        p, num = self.place.at[axis], self.place.dims[axis]
        self.take(stage, 0, zb, p, both(valid, p > 0))
        self.take(stage, 1, zb, p, both(valid, p < num - 1))

    def z_slot(self, source, target):
        return jnp.where(source < target, source, source - 1)

    def z_step(self, t, zb, valid):
        place = self.place
        if t > 0:
            slot = self.z_slot(place.z, zb)
            self.put(
                self.total(zb, place.x, place.y),
                self.line_z.at[slot],
                self.z_send.at[self.z_slot(zb, place.z)],
                self.z_recv.at[slot],
                place.device(0, zb),
                valid,
            )

    def finish(self):
        place = self.place
        mine = self.total(place.z, place.x, place.y)
        num = place.dims[0] - 1
        for slot in range(num):
            buf = self.line_z.at[slot]
            remote(
                buf, buf, self.z_send.at[slot], self.z_recv.at[slot], place.sibling()
            ).wait_recv()
        for u in range(mine.shape[0]):
            value = mine[u].astype(F32)
            for slot in range(num):
                value = value + self.line_z[slot, u].astype(F32)
            self.result(u, value)

    def finish_sends(self):
        for cond, copy in self.sends:
            when(cond, copy.wait_send)

    def steps(self, rounds):
        def round_of(k):
            def act():
                for lag in (2, 1, 0):
                    if not 0 <= k - lag < len(rounds):
                        continue
                    for t, side, zb, valid in rounds[k - lag]:
                        if lag == 0:
                            self.core_finish(zb, valid)
                            self.stage_send(0, zb, valid)
                        elif lag == 1:
                            self.stage_keep(0, zb, valid)
                            self.stage_send(1, zb, valid)
                        else:
                            self.stage_keep(1, zb, valid)
                            self.z_step(t, zb, valid)

            return act

        return [round_of(k) for k in range(len(rounds) + 2)]


def reduce_sems(num_sets, dims):
    num_z, num_x, num_y = dims
    line = max(num_x, num_y)
    dma = pltpu.SemaphoreType.DMA
    return [
        dma((num_sets, num_z)),
        dma((num_sets, num_z)),
        dma((num_sets, 2, 2, num_z, line - 1)),
        dma((num_sets, 2, 2, num_z, line - 1)),
        dma((num_sets, num_z - 1)),
        dma((num_sets, num_z - 1)),
    ]


def reduce_bufs(count, depth, columns, dims, order, dtype):
    one, two = dims[order[0]], dims[order[1]]

    def ways(num):
        return 1 if num == 2 else 2

    return [
        pltpu.VMEM((count, *dims, depth, columns), dtype),
        pltpu.VMEM((ways(one), one - 1, count, dims[0], two, depth, columns), dtype),
        pltpu.VMEM((ways(two), two - 1, count, dims[0], depth, columns), dtype),
        pltpu.VMEM((dims[0] - 1, count, depth, columns), dtype),
    ]


ORDER_A = (2, 1)
ORDER_B = (1, 2)


class TokenReturn:
    def __init__(self, place, num_seqs, src_slot, dst, sems, which):
        self.place, self.num_seqs, self.src_slot, self.dst = place, num_seqs, src_slot, dst
        self.send_sem, self.recv_sem, self.local_sem = (s.at[which] for s in sems)
        self.per_dev = LEN // (place.dims[2] * 2) // BLOCK
        self.sends = []

    def start(self, slots=range(SLOTS)):
        for slot in slots:
            g = 2 * slot + self.place.core
            target = lax.div(g, self.per_dev)
            row = lax.rem(g, self.per_dev)
            here = target == self.place.sp
            block = self.src_slot(slot)
            goal = self.dst.at[self.place.y, pl.ds(pl.multiple_of(row * BLOCK, BLOCK), BLOCK)]
            copy = remote(
                block,
                goal,
                self.send_sem.at[slot],
                self.recv_sem.at[self.place.y, row],
                (self.place.dp, target),
            )
            local = pltpu.make_async_copy(block, goal, self.local_sem.at[slot])
            when(jnp.logical_not(here), copy.start)
            when(here, local.start)
            self.sends.append((here, copy, local))

    def finish(self):
        for here, copy, local in self.sends:
            when(jnp.logical_not(here), copy.wait_send)
            when(here, local.wait)
        for seq in range(self.num_seqs):
            for i in range(self.per_dev):
                g = self.place.sp * self.per_dev + i
                source = seq * 2 + lax.rem(g, 2)
                goal = self.dst.at[seq, pl.ds(i * BLOCK, BLOCK)]
                arrived = remote(
                    goal, goal, self.send_sem.at[0], self.recv_sem.at[seq, i], self.place.sibling()
                )
                when(source != self.place.sp, arrived.wait_recv)


def return_sems(num, num_seqs, per_dev):
    dma = pltpu.SemaphoreType.DMA
    return [dma((num, SLOTS)), dma((num, num_seqs, per_dev)), dma((num, SLOTS))]


def spread_kernel(dims, num_seqs, num_tok, *refs):
    refs = list(refs)

    def pop(count):
        out = refs[:count]
        del refs[:count]
        return out

    grads, toks, outs, tok_outs = pop(7), pop(num_tok), pop(7), pop(num_tok)
    totals, bufs, sems, own, tok_sems = pop(7), pop(28), pop(6), pop(1)[0], pop(3)
    place = Place(dims)
    core = place.core
    place.greet()
    sets = []
    for k in range(7):
        grad, total = grads[k], totals[k]

        def result(u, value, k=k):
            outs[k][u] = value

        sets.append(
            ReduceSet(
                place,
                lambda z, x, y, total=total: total.at[:, z, x, y],
                lambda z, grad=grad: grad.at[:, z, :, :, 1 - core],
                lambda z, grad=grad, total=total, k=k: pltpu.make_async_copy(
                    grad.at[:, z, :, :, core], total.at[:, z], own.at[k, z]
                ),
                ORDER_A if k in (0, 3, 6) else ORDER_B,
                bufs[4 * k : 4 * k + 4],
                set_sems(sems, k),
                result,
            )
        )
    rounds = z_items(place, True)
    for items in rounds:
        for t, side, zb, valid in items:
            for one in sets:
                one.start(zb, valid)
    moves = []
    for which, (src, dst) in enumerate(zip(toks, tok_outs)):
        moves.append(
            TokenReturn(place, num_seqs, lambda s, src=src: src.at[s], dst, tok_sems, which)
        )
        moves[-1].start()
    lists = [one.steps(rounds) for one in sets]
    for acts in zip(*lists):
        for act in acts:
            act()
    for one in sets:
        one.finish()
        one.finish_sends()
    for move in moves:
        move.finish()


def spread(dims, num_seqs, grads, toks):
    num_z, num_x, num_y = dims
    per_dev = LEN // (num_y * 2) // BLOCK
    rows = WIDTH // (num_z * num_x * num_y * 2)
    dma = pltpu.SemaphoreType.DMA
    set_sizes = [(UNITS_A, rows), (UNITS_B, rows), (1, 4 * rows)] * LAYERS + [(1, rows)]
    outs, bufs, totals = [], [], []
    for k, (count, depth) in enumerate(set_sizes):
        columns = WIDTH if k < 6 else BLOCK
        dtype = BF if k < 6 else F32
        outs.append(jax.ShapeDtypeStruct((count, depth, columns), F32))
        order = ORDER_A if k in (0, 3, 6) else ORDER_B
        totals.append(pltpu.VMEM((count, *dims, depth, columns), dtype))
        bufs += reduce_bufs(count, depth, columns, dims, order, dtype)
    outs += [jax.ShapeDtypeStruct((num_seqs, per_dev * BLOCK, WIDTH), t.dtype) for t in toks]
    shaped = [
        g.reshape(count, num_z, num_x, num_y, 2, depth, g.shape[-1])
        for g, (count, depth) in zip(grads, set_sizes)
    ]
    return pl.pallas_call(
        partial(spread_kernel, dims, num_seqs, len(toks)),
        out_shape=outs,
        in_specs=[ANY] * (7 + len(toks)),
        out_specs=[VMEM] * 7 + [ANY] * len(toks),
        scratch_shapes=totals
        + bufs
        + reduce_sems(7, dims)
        + [dma((7, num_z))]
        + return_sems(len(toks), num_seqs, per_dev),
        compiler_params=pltpu.CompilerParams(
            collective_id=1, has_side_effects=True, vmem_limit_bytes=VMEM_BYTES
        ),
        name="spread",
    )(*shaped, *toks)


def dot(left, right):
    return lax.dot_general(left, right, (((1,), (0,)), ((), ())), preferred_element_type=F32)


def dot_nt(left, right):
    return lax.dot_general(left, right, (((1,), (1,)), ((), ())), preferred_element_type=F32)


def dot_tn(left, right):
    return lax.dot_general(left, right, (((0,), (0,)), ((), ())), preferred_element_type=F32)


def normalize(values):
    centre = jnp.mean(values, axis=-1, keepdims=True)
    shifted = values - centre
    inv_std = lax.rsqrt(jnp.mean(shifted * shifted, axis=-1, keepdims=True) + EPSILON)
    return shifted * inv_std, inv_std


def norm_back(grad_normed, normed, inv_std, gain):
    grad_hat = grad_normed * gain
    mean_one = jnp.mean(grad_hat, axis=-1, keepdims=True)
    mean_two = jnp.mean(grad_hat * normed, axis=-1, keepdims=True)
    return inv_std * (grad_hat - mean_one - normed * mean_two)


def halves(body, tick=None):
    if tick is not None:
        for i in range(2):
            body(pl.ds(i * HALF, HALF))
            tick()
        return

    def step(i, carry):
        body(pl.ds(pl.multiple_of(i * HALF, HALF), HALF))
        return carry

    lax.fori_loop(0, 2, step, 0)


def column_sums(values):
    return jnp.sum(values, axis=0, keepdims=True)


GELU_A = 0.7978845608028654
GELU_B = 0.044715


def gelu(t):
    return 0.5 * t * (1.0 + jnp.tanh(GELU_A * (t + GELU_B * t * t * t)))


def gelu_both(t):
    square = t * t
    wave = jnp.tanh(GELU_A * (t + GELU_B * t * square))
    up = 0.5 * (1.0 + wave)
    slope = up + 0.5 * t * (1.0 - wave * wave) * (GELU_A * (1.0 + 3.0 * GELU_B * square))
    return t * up, slope


class Weights:
    def __init__(self, r, layer, names):
        self.r, self.layer = r, layer
        self.copies = {}
        sets = r.g[layer]
        place_of = {}
        for which, (units, _) in enumerate(SETS):
            for unit, name in enumerate(units):
                src = sets[which].at[unit]
                if name == "down":
                    place_of["down"] = [
                        (src.at[pl.ds(k * WIDTH, WIDTH)], r.w_scratch, ("down", k))
                        for k in range(CHUNKS)
                    ]
                elif name[:2] == "up":
                    place_of.setdefault("up", []).append((src, r.w_scratch, ("up", int(name[2:]))))
                else:
                    place_of[name] = [(src, r.w_scratch, name)]
        for name in names:
            group = []
            for src, pool, key in place_of[name]:
                index = r.w_index[(layer, key)]
                copy = pltpu.make_async_copy(src, pool.at[index], r.w_sem.at[index])
                copy.start()
                group.append(copy)
            self.copies[name] = group
        self.waited = set()

    def need(self, *names):
        for name in names:
            if name in self.copies and name not in self.waited:
                self.waited.add(name)
                for copy in self.copies[name]:
                    copy.wait()

    def get(self, name):
        return self.r.w_scratch[self.r.w_index[(self.layer, name)]]

    def chunk(self, name, n):
        return self.r.w_scratch[self.r.w_index[(self.layer, (name, 0))] + n]


def vec_row(r, layer, which):
    row = layer * 4 + which
    return r.vec[row : row + 1, :]


def load_vectors(r):
    r.vec[...] = jnp.transpose(r.vec_in[...].astype(F32))[0:8, :]


def mask_setup(r, flipped):
    core = lax.rem(lax.axis_index("sp"), 2)
    seq = lax.div(lax.axis_index("sp"), 2)
    ends = []
    total = jnp.int32(0)
    for d in range(4):
        total = total + r.lengths[seq, d]
        ends.append(total)

    def segment(position):
        out = jnp.zeros(position.shape, jnp.int32)
        for end in ends:
            out = out + (position >= end).astype(jnp.int32)
        return out

    for j in range(SLOTS):
        for which in range(2):
            count = (j + 1) * BLOCK
            other = core if which == 0 else 1 - core
            q_shape, k_shape = ((1, BLOCK), (count, 1)) if flipped else ((BLOCK, 1), (1, count))
            q_in = lax.broadcasted_iota(jnp.int32, q_shape, 1 if flipped else 0)
            k_in = lax.broadcasted_iota(jnp.int32, k_shape, 0 if flipped else 1)
            q_pos = (2 * j + core) * BLOCK + q_in
            k_pos = k_in + BLOCK * lax.div(k_in, BLOCK) + other * BLOCK
            q_seg = segment(q_pos)
            k_seg = segment(k_pos)
            k_seg = jnp.where(k_seg >= 4, -1, k_seg)
            allowed = ((q_seg == k_seg) & (k_pos <= q_pos)) | (q_pos == k_pos)
            bias = jnp.where(allowed, 0.0, NEG_FILL).astype(F32)
            if flipped:
                r.bias[j, which * TOKENS : which * TOKENS + count, :] = bias
            else:
                r.bias[j, :, which * TOKENS : which * TOKENS + count] = bias


def two_heads(block):
    lane = lax.broadcasted_iota(jnp.int32, block.shape, 1)
    zero = jnp.zeros_like(block)
    first = jnp.where(lane < HEAD_DIM, block, zero)
    second = jnp.where(lane < HEAD_DIM, zero, block)
    return jnp.concatenate([first, second], axis=0)


def join_heads(stacked):
    first, second = stacked[:BLOCK], stacked[BLOCK:]
    lane = lax.broadcasted_iota(jnp.int32, first.shape, 1)
    return jnp.where(lane < HEAD_DIM, first, second)


def layer_front(
    r, w, layer, x_ref, h_ref, q_ref, k_ref, v_ref, gate_ref, tick=None, exchange=lambda: None
):
    w.need("q", "k", "v", "ga")

    def first(rows):
        normed, _ = normalize(x_ref[rows, :].astype(F32))
        hidden = (normed * vec_row(r, layer, 0)).astype(BF)
        h_ref[rows, :] = hidden
        k_ref[rows, :] = dot(hidden, w.get("k")).astype(BF)
        v_ref[rows, :] = dot(hidden, w.get("v")).astype(BF)

    halves(first)
    exchange()
    if tick is not None:
        tick()

    def second(rows):
        hidden = h_ref[rows, :]
        q_ref[rows, :] = (dot(hidden, w.get("q")) * (HEAD_DIM**-0.5)).astype(BF)
        gate_ref[rows, :] = jax.nn.sigmoid(dot(hidden, w.get("ga")) + vec_row(r, layer, 1))

    halves(second)
    if tick is not None:
        tick()


def attention(r, q_ref, k_refs, v_refs, out_ref, lse_ref, tick=None):
    lse_ref[...] = jnp.zeros_like(lse_ref)

    def pair_step(pair, carry):
        cols = pl.ds(pl.multiple_of(pair * BLOCK, BLOCK), BLOCK)
        for j in range(SLOTS):
            rows = slice(j * BLOCK, (j + 1) * BLOCK)
            count = (j + 1) * BLOCK
            queries = two_heads(q_ref[rows, cols])
            scores = []
            for which in range(2):
                bias = r.bias[j, :, which * TOKENS : which * TOKENS + count]
                score = dot_nt(queries, k_refs[which][0:count, cols])
                scores.append(score + jnp.concatenate([bias, bias], axis=0))
            top = jnp.maximum(
                jnp.max(scores[0], axis=1, keepdims=True), jnp.max(scores[1], axis=1, keepdims=True)
            )
            expo = [jnp.exp(score - top) for score in scores]
            total = jnp.sum(expo[0], axis=1, keepdims=True) + jnp.sum(expo[1], axis=1, keepdims=True)
            mixed = dot(expo[0].astype(BF), v_refs[0][0:count, cols])
            mixed = mixed + dot(expo[1].astype(BF), v_refs[1][0:count, cols])
            out_ref[rows, cols] = join_heads(mixed / total).astype(BF)
            lse = top + jnp.log(total)
            lane = lax.broadcasted_iota(jnp.int32, (BLOCK, BLOCK), 1)
            kept = lse_ref[rows, :]
            kept = jnp.where(lane == 2 * pair, lse[:BLOCK], kept)
            lse_ref[rows, :] = jnp.where(lane == 2 * pair + 1, lse[BLOCK:], kept)
        return carry

    if tick is None:
        lax.fori_loop(0, PAIRS, pair_step, 0)
        return
    for part in range(2):
        lax.fori_loop(part * PAIRS // 2, (part + 1) * PAIRS // 2, pair_step, 0)
        tick()


def layer_back_half(
    r, w, layer, x_ref, attn_ref, gate_ref, a_ref, x2_ref, y_ref, gf_ref, x3_ref, tick=None, more=None
):
    w.need("o", "gf", "up", "down")

    def first(rows):
        branch = dot(attn_ref[rows, :], w.get("o"))
        a_ref[rows, :] = branch.astype(a_ref.dtype)
        after = x_ref[rows, :].astype(F32) + gate_ref[rows, :] * branch
        x2_ref[rows, :] = after
        normed, _ = normalize(after)
        hidden = (normed * vec_row(r, layer, 2)).astype(BF)
        gf_ref[rows, :] = jax.nn.sigmoid(dot(hidden, w.get("gf")) + vec_row(r, layer, 3))
        if more is not None:
            more.hid_t[:, rows] = jnp.transpose(hidden)
        for n in range(CHUNKS):
            up = dot(hidden, w.chunk("up", n))
            if more is None:
                r.act[n, rows, :] = gelu(up).astype(BF)
            else:
                value, slope = gelu_both(up)
                active = value.astype(BF)
                r.act[n, rows, :] = active
                more.slope[n, rows, :] = slope.astype(BF)
                more.act_t[n, :, rows] = jnp.transpose(active)

    halves(first, tick)

    def second(rows):
        out = None
        for n in range(CHUNKS):
            part = dot(r.act[n, rows, :], w.chunk("down", n))
            out = part if out is None else out + part
        y_ref[rows, :] = out.astype(y_ref.dtype)
        x3_ref[rows, :] = x2_ref[rows, :] + gf_ref[rows, :] * out

    halves(second)
    if tick is not None:
        tick()


def nothing(*args):
    pass


def ffn_backward(r, w, layer, dx_ref, s, out, tick=nothing, ready=nothing, kept=None):
    w.need("o", "gf", "up", "down")
    hid_t = r.hid_t if kept is None else kept.hid_t

    def start(rows):
        grad = dx_ref[rows, :].astype(F32)
        gate = s.gf[rows, :]
        r.dy[rows, :] = (grad * gate).astype(BF)
        dz = (grad * s.y[rows, :].astype(F32) * gate * (1.0 - gate)).astype(BF)
        r.dz[rows, :] = dz
        if kept is None:
            normed, _ = normalize(s.x2[rows, :])
            r.hid[rows, :] = (normed * vec_row(r, layer, 2)).astype(BF)
        r.dh[rows, :] = dot_nt(dz, w.get("gf"))

    halves(start)
    if kept is None:
        r.hid_t[...] = jnp.transpose(r.hid[...])
    out.unit("gf", dot(hid_t[...], r.dz[...]))
    r.vg[layer * 4 + 3 : layer * 4 + 4, :] = column_sums(r.dz[...].astype(F32))
    tick()

    for n in range(CHUNKS):
        if kept is not None:
            kept.take(n)

        def body(rows, n=n):
            if kept is None:
                act, slope = gelu_both(dot(r.hid[rows, :], w.chunk("up", n)))
                r.act[rows, :] = act.astype(BF)
            else:
                slope = kept.slope(n)[rows, :].astype(F32)
            du = (dot_nt(r.dy[rows, :], w.chunk("down", n)) * slope).astype(BF)
            r.du[rows, :] = du
            r.dh[rows, :] += dot_nt(du, w.chunk("up", n))

        halves(body)
        if kept is None:
            out.down(n, dot_tn(r.act[...], r.dy[...]))
        else:
            out.down(n, dot(kept.act_t(n)[...], r.dy[...]))
        out.unit("up" + str(n), dot(hid_t[...], r.du[...]))
        if kept is not None:
            kept.drop(n)
        if n == 1:
            ready("up_a")
        elif n == 3:
            ready("up_b", "down")
        tick()

    r.sums[...] = jnp.zeros_like(r.sums)

    def finish(rows):
        normed, inv_std = normalize(s.x2[rows, :])
        grad_hidden = r.dh[rows, :]
        r.sums[0:1, :] += column_sums(grad_hidden * normed)
        mid = dx_ref[rows, :].astype(F32) + norm_back(
            grad_hidden, normed, inv_std, vec_row(r, layer, 2)
        )
        out.dx2[rows, :] = mid
        gate = s.gate[rows, :]
        da = (mid * gate).astype(BF)
        r.dy[rows, :] = da
        dza = (mid * s.a[rows, :].astype(F32) * gate * (1.0 - gate)).astype(BF)
        out.dza[rows, :] = dza
        r.sums[1:2, :] += column_sums(dza.astype(F32))
        r.dattn[rows, :] = dot_nt(da, w.get("o")).astype(BF)

    halves(finish)
    tick()
    r.vg[layer * 4 + 2 : layer * 4 + 3, :] = r.sums[0:1, :]
    r.vg[layer * 4 + 1 : layer * 4 + 2, :] = r.sums[1:2, :]
    if kept is None:
        out.unit("o", dot_tn(s.attn[...], r.dy[...]))
        out.unit("ga", dot_tn(s.h[...], out.dza[...]))
    else:
        out.unit("o", dot(kept.attn_t[...], r.dy[...]))
        out.unit("ga", dot(kept.h_t[...], out.dza[...]))
    ready("mix")
    tick()


def attention_backward(r, s, out, tick=None):
    for j in range(SLOTS):
        r.lse_t[j] = jnp.transpose(s.lse[j * BLOCK : (j + 1) * BLOCK, :])[0:8, :]

    def slot_step(pair, cols, j):
        rows = slice(j * BLOCK, (j + 1) * BLOCK)
        count = (j + 1) * BLOCK
        queries = two_heads(s.q[rows, cols])
        grads = two_heads(r.dattn[rows, cols])
        lse = jnp.concatenate(
            [r.lse_t[j, pl.ds(2 * pair, 1), :], r.lse_t[j, pl.ds(2 * pair + 1, 1), :]], axis=1
        )
        probs, slopes = [], []
        delta = None
        for which in range(2):
            bias = r.bias[j, which * TOKENS : which * TOKENS + count, :]
            score = dot_nt(s.k[which][0:count, cols], queries)
            prob = jnp.exp(score + jnp.concatenate([bias, bias], axis=1) - lse)
            slope = dot_nt(s.v[which][0:count, cols], grads)
            part = column_sums(prob * slope)
            delta = part if delta is None else delta + part
            probs.append(prob)
            slopes.append(slope)
        grad_q = None
        for which in range(2):
            ds = (probs[which] * (slopes[which] - delta)).astype(BF)
            dv = dot(probs[which].astype(BF), grads)
            dk = dot(ds, queries)
            dk_ref, dv_ref = (out.dk, out.dv) if which == 0 else (r.dk_other, r.dv_other)
            where = cols if which == 0 else slice(None)
            if j == SLOTS - 1:
                dk_ref[:, where] = dk
                dv_ref[:, where] = dv
            else:
                dk_ref[0:count, where] += dk
                dv_ref[0:count, where] += dv
            part = dot_tn(s.k[which][0:count, cols], ds)
            grad_q = part if grad_q is None else grad_q + part
        grad_q = join_heads(jnp.transpose(grad_q)) * (HEAD_DIM**-0.5)
        out.dq[rows, cols] = grad_q.astype(BF)

    def pair_step(pair, carry):
        cols = pl.ds(pl.multiple_of(pair * BLOCK, BLOCK), BLOCK)
        for j in range(SLOTS - 1, -1, -1):
            slot_step(pair, cols, j)
        if tick is not None:
            tick()
        out.dk_out[:, cols] = r.dk_other[...].astype(BF)
        out.dv_out[:, cols] = r.dv_other[...].astype(BF)
        return carry

    if tick is None:
        lax.fori_loop(0, PAIRS, pair_step, 0)
    else:
        for pair in range(PAIRS):
            pair_step(pair, 0)


def layer_front_backward(
    r, w, layer, s, g, out, dx_ref, arrived=nothing, tick=nothing, ready=nothing, h_t=None
):
    w.need("q", "k", "v", "ga")
    if h_t is None:
        h_t = r.hid_t
        h_t[...] = jnp.transpose(s.h[...])
    out.unit("q", dot(h_t[...], g.dq[...]))
    ready("q")

    def before(rows):
        grad_hidden = dot_nt(g.dq[rows, :], w.get("q"))
        r.dh[rows, :] = grad_hidden + dot_nt(g.dza[rows, :], w.get("ga"))

    halves(before)
    arrived()

    def start(rows):
        r.dk[rows, :] = (g.dk[rows, :] + g.dk_in[rows, :].astype(F32)).astype(BF)
        r.dv[rows, :] = (g.dv[rows, :] + g.dv_in[rows, :].astype(F32)).astype(BF)

    halves(start)
    out.unit("k", dot(h_t[...], r.dk[...]))
    out.unit("v", dot(h_t[...], r.dv[...]))
    ready("kv")
    tick()
    r.sums[...] = jnp.zeros_like(r.sums)

    def body(rows):
        grad_hidden = r.dh[rows, :] + dot_nt(r.dk[rows, :], w.get("k"))
        grad_hidden += dot_nt(r.dv[rows, :], w.get("v"))
        normed, inv_std = normalize(s.x[rows, :].astype(F32))
        r.sums[0:1, :] += column_sums(grad_hidden * normed)
        dx_ref[rows, :] = g.dx2[rows, :] + norm_back(
            grad_hidden, normed, inv_std, vec_row(r, layer, 0)
        )

    halves(body)
    tick()
    r.vg[layer * 4 : layer * 4 + 1, :] = r.sums[0:1, :]


FRONT = ("q", "k", "v", "ga")
BACK = ("o", "gf", "up", "down")


def weight_index(wanted):
    index, count = {}, 0
    for layer, names in wanted:
        for name in names:
            if name in ("up", "down"):
                for k in range(CHUNKS):
                    index[(layer, (name, k))] = count
                    count += 1
            else:
                index[(layer, name)] = count
                count += 1
    return index, count


def compute_call(body, name, wanted, gathered, ins, outs, scratch):
    in_names, out_names, scratch_names = list(ins), list(outs), list(scratch)
    layers = sorted({layer for layer, _ in wanted})
    index, count = weight_index(wanted)
    weight_refs = [arr for layer in layers for arr in gathered[layer]]

    def kernel(*refs):
        refs = list(refs)
        r = SimpleNamespace()
        r.g = {}
        for layer in layers:
            r.g[layer] = [refs.pop(0) for _ in SETS]
        for field in in_names + out_names + scratch_names:
            setattr(r, field, refs.pop(0))
        r.w_scratch, r.w_sem, r.vec = refs
        r.w_index = index
        r.w = {}
        for layer, names in wanted:
            r.w[layer] = Weights(r, layer, names)
        load_vectors(r)
        body(r)

    return pl.pallas_call(
        kernel,
        out_shape=[outs[n] for n in out_names],
        in_specs=[ANY] * len(weight_refs) + [SMEM if n == "lengths" else VMEM for n in in_names],
        out_specs=[VMEM] * len(out_names),
        scratch_shapes=[scratch[n] for n in scratch_names]
        + [
            pltpu.VMEM((count, WIDTH, WIDTH), BF),
            pltpu.SemaphoreType.DMA((count,)),
            pltpu.VMEM((8, WIDTH), F32),
        ],
        compiler_params=pltpu.CompilerParams(vmem_limit_bytes=VMEM_BYTES),
        name=name,
    )(*weight_refs, *[ins[n] for n in in_names])


def tok(dtype):
    return jax.ShapeDtypeStruct((TOKENS, WIDTH), dtype)


def vm(*shape, dtype=BF):
    return pltpu.VMEM(shape, dtype)


def front_outs(prefix):
    return {
        prefix + "h": tok(BF),
        prefix + "q": tok(BF),
        prefix + "k": tok(BF),
        prefix + "v": tok(BF),
        prefix + "gate": tok(F32),
    }


def back_outs():
    return {
        "attn": tok(BF),
        "lse": jax.ShapeDtypeStruct((TOKENS, BLOCK), F32),
        "a": tok(F32),
        "x2": tok(F32),
        "y": tok(F32),
        "gf": tok(F32),
        "x3": tok(F32),
    }


BIAS = vm(SLOTS, BLOCK, 2 * TOKENS, dtype=F32)
BIAS_T = vm(SLOTS, 2 * TOKENS, BLOCK, dtype=F32)


def grad_outs():
    return {
        "a": jax.ShapeDtypeStruct((UNITS_A, WIDTH, WIDTH), BF),
        "b": jax.ShapeDtypeStruct((UNITS_B, WIDTH, WIDTH), BF),
        "d": jax.ShapeDtypeStruct((1, CHUNKS * WIDTH, WIDTH), BF),
    }


BACKWARD_SCRATCH = {
    "bias": BIAS_T,
    "dy": vm(TOKENS, WIDTH),
    "dz": vm(TOKENS, WIDTH),
    "hid": vm(TOKENS, WIDTH),
    "hid_t": vm(WIDTH, TOKENS),
    "dh": vm(TOKENS, WIDTH, dtype=F32),
    "act": vm(TOKENS, WIDTH),
    "du": vm(TOKENS, WIDTH),
    "sums": vm(8, WIDTH, dtype=F32),
    "dattn": vm(TOKENS, WIDTH),
    "lse_t": vm(SLOTS, 8, BLOCK, dtype=F32),
    "dk_other": vm(TOKENS, BLOCK, dtype=F32),
    "dv_other": vm(TOKENS, BLOCK, dtype=F32),
}


def front_call(gathered, vec_in, layer, x):
    def body(r):
        layer_front(r, r.w[layer], layer, r.x, r.h, r.q, r.k, r.v, r.gate)

    outs = front_outs("")
    got = compute_call(
        body, "front", [(layer, FRONT)], gathered, {"vec_in": vec_in, "x": x}, outs, {}
    )
    return dict(zip(outs, got))


def middle_call(gathered, vec_in, lengths, layer, x, s):
    ins = {
        "vec_in": vec_in,
        "lengths": lengths,
        "x": x,
        "q": s["q"],
        "k0": s["k"],
        "v0": s["v"],
        "k1": s["k1"],
        "v1": s["v1"],
        "gate": s["gate"],
    }
    last = layer == LAYERS - 1
    outs = back_outs()
    wanted = [(layer, BACK)]
    if not last:
        outs.update(front_outs("n"))
        wanted.append((layer + 1, FRONT))

    def body(r):
        mask_setup(r, False)
        attention(r, r.q, (r.k0, r.k1), (r.v0, r.v1), r.attn, r.lse)
        layer_back_half(
            r, r.w[layer], layer, r.x, r.attn, r.gate, r.a, r.x2, r.y, r.gf, r.x3
        )
        if not last:
            layer_front(
                r, r.w[layer + 1], layer + 1, r.x3, r.nh, r.nq, r.nk, r.nv, r.ngate
            )

    scratch = {"bias": BIAS, "act": vm(CHUNKS, TOKENS, WIDTH)}
    got = compute_call(body, "middle", wanted, gathered, ins, outs, scratch)
    return dict(zip(outs, got))


class Gathered:
    def __init__(self, refs):
        self.place = {
            name: refs[which].at[unit]
            for which, (names, _) in enumerate(SETS)
            for unit, name in enumerate(names)
        }

    def need(self, *names):
        pass

    def get(self, name):
        return self.place[name][...].reshape(WIDTH, WIDTH)

    def chunk(self, name, n):
        if name == "up":
            return self.get("up" + str(n))
        ref = self.place["down"]
        part = ref.shape[0] // CHUNKS
        return ref[n * part : (n + 1) * part].reshape(WIDTH, WIDTH)


LAYER_ARRAYS = {
    "h": BF,
    "q": BF,
    "k": BF,
    "v": BF,
    "k1": BF,
    "v1": BF,
    "gate": F32,
    "attn": BF,
    "lse": F32,
    "a": BF,
    "x2": F32,
    "y": BF,
    "gf": F32,
    "x3": F32,
    "h_t": BF,
    "attn_t": BF,
    "hid_t": BF,
    "act_t": BF,
    "slope": BF,
}
NOT_SAVED = ("h", "attn")


def layer_shape(name):
    if name in ("act_t", "slope"):
        return (CHUNKS, WIDTH, TOKENS)
    return (TOKENS, BLOCK if name == "lse" else WIDTH)


def saved_names(layer):
    return [n for n in LAYER_ARRAYS if n not in NOT_SAVED and (n != "x3" or layer < LAYERS - 1)]


def forward_kernel(dims, num_seqs, *refs):
    refs = list(refs)

    def pop(count):
        out = refs[:count]
        del refs[:count]
        return out

    num_sets = LAYERS * len(SETS)
    inputs, cotangent = pop(2)
    weights = pop(8)
    vectors = pop(4)
    (lengths,) = pop(1)
    cot_out, result, x0_out = pop(3)
    set_outs = pop(num_sets)
    saved_outs = [{n: pop(1)[0] for n in saved_names(layer)} for layer in range(LAYERS)]
    sets = pop(num_sets)
    arrays = [dict(zip(LAYER_ARRAYS, pop(len(LAYER_ARRAYS)))) for _ in range(LAYERS)]
    x0, cot, last, bias, vec, square, act = pop(7)
    sems = pop(6)
    (own_sem,) = pop(1)
    tok_sems = pop(3)
    kv_send, kv_recv, out_sem = pop(3)

    place = Place(dims)
    own = [start_own(place, weights, None, sets, own_sem, (0,))]
    own.append(start_own(place, weights, None, sets, own_sem, (1,), len(own[0])))
    rows = vectors[0].shape[1]
    square[...] = jnp.zeros_like(square)
    for layer in range(LAYERS):
        for which, ref in enumerate(vectors):
            row = layer * 4 + which
            square[row : row + 1, 0:rows] = ref[layer : layer + 1, :].astype(F32)
    vec_unit = sets[0].at[VEC_UNIT, place.z, place.x, place.y, place.core]
    vec_unit[...] = jnp.zeros(vec_unit.shape, BF)
    vec_unit[:, 0:BLOCK] = jnp.transpose(square[...])[0:rows, :].astype(BF)
    place.greet()

    def rows_of(ref):
        return lambda slot: ref.at[pl.ds(pl.multiple_of(slot * BLOCK, BLOCK), BLOCK)]

    move_x = TokenMove(place, num_seqs, inputs, rows_of(x0), tok_sems, 0)
    move_cot = TokenMove(place, num_seqs, cotangent, rows_of(cot), tok_sems, 1)
    outgoing = []

    def save(src, dst):
        copy = pltpu.make_async_copy(src, dst, out_sem.at[len(outgoing)])
        copy.start()
        outgoing.append(copy)

    gathers = [
        PairGather(place, ref, SETS[k % len(SETS)][1], set_sems(sems, k)) for k, ref in enumerate(sets)
    ]
    groups = [
        [layer * len(SETS) + k for k in part]
        for layer in range(LAYERS)
        for part in ((0, 1), (2, 3), (4,))
    ]
    far = range(1, dims[0])
    every = range(dims[0])

    def event(method, group, *args):
        members = [gathers[k] for k in groups[group]]
        if not args:
            for one in members:
                getattr(one, method)()
        for t in args:
            for one in members:
                getattr(one, method)(t)

    for copy in own[0]:
        copy.wait()
    event("open", 0)
    move_x.start()
    for copy in own[1]:
        copy.wait()

    def finish_group(group):
        event("finish", group)
        for k in groups[group]:
            save(sets[k], set_outs[k])

    after = (
        {
            "front0": (("stage2", 1, 1),),
            "front1": (("stage2", 1, 2, 3), ("stage1", 2, *far), ("stage2", 2, 0), ("open", 3)),
            "attend0": (("stage2", 2, *far), ("stage1", 3, *far)),
            "attend1": (("stage3", 1, *every), ("open", 4), ("stage2", 3, *every), ("done", 1)),
            "feed0": (("stage3", 2, *every), ("stage1", 4, *far)),
            "feed1": (("stage2", 4, 0, 1), ("stage3", 3, *every), ("done", 2)),
            "feed2": (("stage2", 4, 2, 3), ("open", 5), ("done", 3)),
        },
        {
            "front0": (("stage1", 5, *far), ("stage2", 5, 0)),
            "attend0": (("stage2", 5, *far), ("stage3", 4, *every)),
            "attend1": (("done", 4),),
            "feed1": (("stage3", 5, *every), ("done", 5)),
        },
    )

    def ticker(layer, name):
        count = [0]

        def tick():
            for method, group, *args in after[layer].get(name + str(count[0]), ()):
                if method == "done":
                    finish_group(group)
                else:
                    event(method, group, *args)
            count[0] += 1

        return tick

    r = SimpleNamespace(bias=bias, lengths=lengths, vec=vec, act=act)
    event("stage2", 0, 0)
    for t in far:
        event("stage1", 0, t)
        event("stage2", 0, t)
        if t == 2:
            event("open", 1)
    event("stage3", 0, *every)
    event("stage1", 1, *far)
    event("open", 2)
    mask_setup(r, False)
    event("stage2", 1, 0)
    finish_group(0)
    move_x.finish()
    vec_block = sets[0][VEC_UNIT].reshape(WIDTH, WIDTH)[:, :BLOCK]
    vec[...] = jnp.transpose(vec_block.astype(F32))[0:8, :]
    save(x0, x0_out)

    exchanges = []
    x = x0
    for layer in range(LAYERS):
        s = SimpleNamespace(**arrays[layer])
        w = Gathered(sets[layer * len(SETS) : (layer + 1) * len(SETS)])
        def exchange(s=s, layer=layer):
            for k, (src, dst) in enumerate(((s.k, s.k1), (s.v, s.v1))):
                copy = remote(src, dst, kv_send.at[layer, k], kv_recv.at[layer, k], place.sibling())
                copy.start()
                exchanges.append(copy)

        tick = ticker(layer, "front")
        layer_front(r, w, layer, x, s.h, s.q, s.k, s.v, s.gate, tick, exchange)
        if layer == 0:
            move_cot.start()
        s.h_t[...] = jnp.transpose(s.h[...])
        for name in ("h_t", "q", "k", "v", "gate"):
            save(arrays[layer][name], saved_outs[layer][name])
        exchanges[-2].wait_recv()
        exchanges[-1].wait_recv()
        attention(r, s.q, (s.k, s.k1), (s.v, s.v1), s.attn, s.lse, ticker(layer, "attend"))
        s.attn_t[...] = jnp.transpose(s.attn[...])
        for name in ("k1", "v1", "attn_t", "lse"):
            save(arrays[layer][name], saved_outs[layer][name])
        layer_back_half(
            r,
            w,
            layer,
            x,
            s.attn,
            s.gate,
            s.a,
            s.x2,
            s.y,
            s.gf,
            s.x3,
            ticker(layer, "feed"),
            s,
        )
        for name in ("a", "x2", "y", "gf", "x3", "hid_t", "act_t", "slope"):
            if layer < LAYERS - 1 or name != "x3":
                save(arrays[layer][name], saved_outs[layer][name])
        x = s.x3

    last[...] = x[...].astype(BF)
    save(last, result)
    move_cot.finish()
    save(cot, cot_out)
    for copy in exchanges:
        copy.wait_send()
    for one in gathers:
        one.finish_sends()
    for copy in outgoing:
        copy.wait()


def forward(dims, inputs, cotangent, weights, vectors, lengths):
    rows = weights[0].shape[1]
    num_seqs, positions, _ = inputs.shape
    shapes = set_shapes(dims, rows)
    dma = pltpu.SemaphoreType.DMA
    layer_types = list(LAYER_ARRAYS.items()) * LAYERS
    outs = [tok(BF), tok(BF), tok(BF)]
    outs += [jax.ShapeDtypeStruct(s, BF) for s in shapes]
    for layer in range(LAYERS):
        for name in saved_names(layer):
            outs.append(jax.ShapeDtypeStruct(layer_shape(name), LAYER_ARRAYS[name]))
    num_saves = len(outs)
    scratch = [vm(*s) for s in shapes]
    scratch += [vm(*layer_shape(n), dtype=t) for n, t in layer_types]
    scratch += [vm(TOKENS, WIDTH), vm(TOKENS, WIDTH), vm(TOKENS, WIDTH), BIAS]
    scratch += [vm(8, WIDTH, dtype=F32), vm(BLOCK, BLOCK, dtype=F32), vm(CHUNKS, TOKENS, WIDTH)]
    scratch += pair_gather_sems(len(shapes), dims[0])
    scratch += [dma((OWN_COPIES,))]
    scratch += token_sems(num_seqs, positions // BLOCK)
    scratch += [dma((LAYERS, 2)), dma((LAYERS, 2)), dma((num_saves,))]
    cot, result, x0, *rest = pl.pallas_call(
        partial(forward_kernel, dims, num_seqs),
        out_shape=outs,
        in_specs=[ANY] * 10 + [VMEM] * 4 + [SMEM],
        out_specs=[ANY] * len(outs),
        scratch_shapes=scratch,
        compiler_params=pltpu.CompilerParams(
            collective_id=0, has_side_effects=True, vmem_limit_bytes=VMEM_BYTES
        ),
        name="forward",
    )(inputs, cotangent, *weights, *vectors, lengths)
    units, arrays = rest[: len(shapes)], rest[len(shapes) :]
    saved = []
    for layer in range(LAYERS):
        saved.append({name: arrays.pop(0) for name in saved_names(layer)})
    return cot, result, x0, units, saved


SAVED = ("h", "q", "k", "v", "k1", "v1", "gate", "attn", "lse", "a", "x2", "y", "gf")


def backward_outs():
    outs = {"g" + n: shape for n, shape in grad_outs().items()}
    outs["dx2"] = tok(F32)
    outs["dza"] = tok(BF)
    outs["dq"] = tok(BF)
    outs["dk"] = tok(F32)
    outs["dv"] = tok(F32)
    outs["dk_out"] = tok(BF)
    outs["dv_out"] = tok(BF)
    outs["vg"] = jax.ShapeDtypeStruct((8, WIDTH), F32)
    return outs


UNIT_PLACE = {"q": 0, "k": 1, "v": 2, "o": 3, "ga": 4, "gf": 5, "up0": 6}


class PlainGrads:
    def __init__(self, a, b=None, d=None):
        self.a, self.b, self.d = a, b, d

    def unit(self, name, value):
        if name in UNIT_PLACE:
            self.a[UNIT_PLACE[name]] = value.astype(BF)
        else:
            self.b[int(name[2:]) - 1] = value.astype(BF)

    def down(self, n, value):
        self.d[0, n * WIDTH : (n + 1) * WIDTH, :] = value.astype(BF)


def run_backward(r, layer, dx_ref):
    s = SimpleNamespace(**{n: getattr(r, "s" + n) for n in SAVED})
    s.k = (r.sk, r.sk1)
    s.v = (r.sv, r.sv1)
    out = PlainGrads(r.ga, r.gb, r.gd)
    for name in ("dx2", "dza", "dq", "dk", "dv", "dk_out", "dv_out"):
        setattr(out, name, getattr(r, name))
    mask_setup(r, True)
    ffn_backward(r, r.w[layer], layer, dx_ref, s, out)
    attention_backward(r, s, out)


def backward_call(gathered, vec_in, lengths, layer, dx, saved):
    ins = {"vec_in": vec_in, "lengths": lengths, "dx": dx}
    ins.update({"s" + n: saved[n] for n in SAVED})

    def body(r):
        r.vg[...] = jnp.zeros_like(r.vg)
        run_backward(r, layer, r.dx)

    outs = backward_outs()
    got = compute_call(
        body, "backward", [(layer, BACK)], gathered, ins, outs, BACKWARD_SCRATCH
    )
    return dict(zip(outs, got))


def front_backward_call(gathered, vec_in, layer, saved, g, vec_grads, final):
    ins = {"vec_in": vec_in, "sx": saved["x"], "sh": saved["h"], "vg_in": vec_grads}
    ins.update({"g" + n: g[n] for n in ("dq", "dk", "dv", "dk_in", "dv_in", "dza", "dx2")})
    outs = {
        "qkv": jax.ShapeDtypeStruct((3, WIDTH, WIDTH), BF),
        "dx": tok(F32),
    }
    if final:
        outs["vg_t"] = jax.ShapeDtypeStruct((1, WIDTH, BLOCK), F32)
    else:
        outs["vg"] = jax.ShapeDtypeStruct((8, WIDTH), F32)
    scratch = {
        "dk": vm(TOKENS, WIDTH),
        "dv": vm(TOKENS, WIDTH),
        "hid_t": vm(WIDTH, TOKENS),
        "sums": vm(8, WIDTH, dtype=F32),
        "dh": vm(TOKENS, WIDTH, dtype=F32),
    }
    if final:
        scratch["vg"] = vm(8, WIDTH, dtype=F32)

    def body(r):
        r.vg[...] = r.vg_in[...]
        s = SimpleNamespace(x=r.sx, h=r.sh)
        gg = SimpleNamespace(
            dq=r.gdq, dk=r.gdk, dv=r.gdv, dk_in=r.gdk_in, dv_in=r.gdv_in, dza=r.gdza, dx2=r.gdx2
        )
        layer_front_backward(r, r.w[layer], layer, s, gg, PlainGrads(r.qkv), r.dx)
        if final:
            tall = jnp.concatenate(
                [r.vg[...], jnp.zeros((BLOCK - 8, WIDTH), F32)], axis=0
            )
            r.vg_t[0] = jnp.transpose(tall)

    got = compute_call(
        body, "front_backward", [(layer, FRONT)], gathered, ins, outs, scratch
    )
    return dict(zip(outs, got))


GRAD_SETS = (
    ("up_a", ("up0", "up1"), (2, 1)),
    ("up_b", ("up2", "up3"), (2, 1)),
    ("down", ("down",), (1, 2)),
    ("mix", ("gf", "o", "ga"), (1, 2)),
    ("q", ("q",), (2, 1)),
    ("kv", ("k", "v"), (1, 2)),
)
LATE_SETS = ("q", "kv")
RESULT_UNITS = ("q", "k", "v", "o", "ga", "gf", "up0", "up1", "up2", "up3")

EARLY_ARRAYS = ("x2", "y", "gf", "gate", "a", "attn_t", "hid_t")
STREAMED = ("act_t", "slope")
ATTENTION_ARRAYS = ("q", "k", "v", "k1", "v1", "lse")


TICKS = ("gf", "c0", "c1", "c2", "c3", "norm", "mix", "p0", "p1", "p2", "p3", "kv", "end")
SCHEDULE = {
    "gf": ((1, 1, "q"), (1, 1, "kv")),
    "c0": ((1, 3, "down"),),
    "c1": ((1, 2, "mix"), (1, 3, "up_b")),
    "c2": ((0, 1, "up_a"), (1, 2, "q")),
    "norm": ((0, 1, "up_b"), (0, 1, "down"), (1, 3, "mix"), (1, 2, "kv")),
    "mix": ((1, 3, "q"),),
    "p0": ((0, 2, "up_a"), (0, 1, "mix")),
    "p1": ((1, 4, "up_a"), (1, 4, "up_b"), (1, 4, "down"), (1, 4, "mix")),
    "p2": ((0, 2, "up_b"), (1, 3, "kv"), (1, 4, "q")),
    "p3": ((0, 2, "down"), (0, 3, "up_a")),
}
LAST = (
    (0, 1, "q"),
    (0, 1, "kv"),
    (0, 3, "down"),
    (0, 1, "vec"),
    (0, 2, "mix"),
    (0, 2, "q"),
    (0, 3, "up_b"),
    (0, 2, "kv"),
    (0, 2, "vec"),
    (1, 4, "kv"),
    (0, 3, "mix"),
    (0, 3, "q"),
    (0, 4, "up_a"),
    (0, 4, "down"),
    (0, 4, "up_b"),
    (0, 3, "kv"),
    (0, 3, "vec"),
    (0, 4, "mix"),
    (0, 4, "q"),
    (0, 4, "kv"),
    (0, 4, "vec"),
)


def grad_set_list(dims, rows):
    out = []
    for layer in range(LAYERS):
        for name, units, order in GRAD_SETS:
            depth = 4 * rows if name == "down" else rows
            out.append((name, layer, units, order, (len(units), *dims, 2, depth, WIDTH), BF))
    out.append(("vec", 0, None, (1, 2), (1, *dims, 2, rows, BLOCK), F32))
    return out


class FusedGrads:
    def __init__(self, refs):
        self.refs = dict(zip((name for name, _, _ in GRAD_SETS), refs))
        self.place = {
            unit: (name, k) for name, units, _ in GRAD_SETS for k, unit in enumerate(units)
        }

    def unit(self, name, value):
        which, k = self.place[name]
        ref = self.refs[which]
        ref[k] = value.astype(BF).reshape(ref.shape[1:])

    def down(self, n, value):
        ref = self.refs["down"]
        part = ref.shape[1] // CHUNKS
        ref[0, n * part : (n + 1) * part] = value.astype(BF).reshape((part, *ref.shape[2:]))


BACKWARD_ARRAYS = {
    "x2": F32,
    "y": BF,
    "gf": F32,
    "gate": F32,
    "a": BF,
    "attn_t": BF,
    "hid_t": BF,
    "h_t": BF,
    "q": BF,
    "k": BF,
    "v": BF,
    "k1": BF,
    "v1": BF,
    "lse": F32,
}

FUSED_WORK = {
    "bias": BIAS_T,
    "dy": vm(TOKENS, WIDTH),
    "dz": vm(TOKENS, WIDTH),
    "act_t": vm(2, WIDTH, TOKENS),
    "slope": vm(2, TOKENS, WIDTH),
    "dh": vm(TOKENS, WIDTH, dtype=F32),
    "act": vm(TOKENS, WIDTH),
    "du": vm(TOKENS, WIDTH),
    "sums": vm(8, WIDTH, dtype=F32),
    "dattn": vm(TOKENS, WIDTH),
    "lse_t": vm(SLOTS, 8, BLOCK, dtype=F32),
    "dk_other": vm(TOKENS, BLOCK, dtype=F32),
    "dv_other": vm(TOKENS, BLOCK, dtype=F32),
    "vg": vm(8, WIDTH, dtype=F32),
    "vec": vm(8, WIDTH, dtype=F32),
    "dx": vm(TOKENS, WIDTH, dtype=F32),
    "dx2": vm(TOKENS, WIDTH, dtype=F32),
    "dza": vm(TOKENS, WIDTH),
    "dq": vm(TOKENS, WIDTH),
    "own_dk": vm(TOKENS, WIDTH, dtype=F32),
    "own_dv": vm(TOKENS, WIDTH, dtype=F32),
    "send_dk": vm(TOKENS, WIDTH),
    "send_dv": vm(TOKENS, WIDTH),
    "got_dk": vm(TOKENS, WIDTH),
    "got_dv": vm(TOKENS, WIDTH),
}


def backward_kernel(dims, num_seqs, *refs):
    refs = list(refs)

    def pop(count):
        out = refs[:count]
        del refs[:count]
        return out

    num_w = LAYERS * len(SETS)
    cot_in, x0_in, last_in = pop(3)
    weight_in = pop(num_w)
    saved_in = [{n: pop(1)[0] for n in saved_names(layer)} for layer in range(LAYERS)]
    (lengths,) = pop(1)
    res, res_down, res_vec, g_out, x_out = pop(5)
    weight_bufs = pop(len(SETS))
    (vec_buf,) = pop(1)
    bufs = dict(zip(BACKWARD_ARRAYS, pop(len(BACKWARD_ARRAYS))))
    r = SimpleNamespace(**dict(zip(FUSED_WORK, pop(len(FUSED_WORK)))))
    set_list = grad_set_list(dims, res_vec.shape[0])
    totals = pop(len(set_list))
    landings = pop(len(GRAD_SETS) + len(LATE_SETS) + 1)
    lines = pop(3 * len(set_list))
    sems = pop(6)
    weight_sem, array_sem, other_sem, stream_sem, dkv_send, dkv_recv = pop(6)
    back_sems = pop(3)
    r.lengths = lengths
    r.dk, r.dv, r.out = r.act, r.du, r.dattn

    place = Place(dims)
    core = place.core
    copies = {}

    def load(key, src, dst, sem):
        copy = pltpu.make_async_copy(src, dst, sem)
        copy.start()
        copies[key] = copy

    def need(*keys):
        for key in keys:
            copy = copies.pop(key, None)
            if copy is not None:
                copy.wait()

    unit_place = {
        name: (which, unit) for which, (names, _) in enumerate(SETS) for unit, name in enumerate(names)
    }
    flat_names = list(unit_place)

    def load_weights(layer, *names):
        for name in names:
            which, unit = unit_place[name]
            load(
                (layer, "w", name),
                weight_in[layer * len(SETS) + which].at[unit],
                weight_bufs[which].at[unit],
                weight_sem.at[layer, flat_names.index(name)],
            )

    array_names = list(BACKWARD_ARRAYS)

    def load_arrays(layer, *names):
        for name in names:
            src = saved_in[layer][name]
            load((layer, name), src, bufs[name], array_sem.at[layer, array_names.index(name)])

    def stream(layer, n):
        for k, name in enumerate(STREAMED):
            load(
                (layer, name, n),
                saved_in[layer][name].at[n],
                (r.act_t, r.slope)[k].at[n % 2],
                stream_sem.at[layer, k, n],
            )

    ffn_weights = ("gf", "o", "up0", "up1", "up2", "up3", "down")
    front_weights = ("q", "k", "v", "ga")
    last = LAYERS - 1
    load((last, "cot"), cot_in, r.dq, other_sem.at[0])
    load_arrays(last, "gf", "y", "x2", "hid_t")
    vec_src = weight_in[0].at[VEC_UNIT, :, :, :, :, :, pl.ds(0, BLOCK)]
    load("vec", vec_src, vec_buf, weight_sem.at[0, len(flat_names)])
    load_weights(last, *ffn_weights)
    stream(last, 0)
    stream(last, 1)
    load_arrays(last, "gate", "a", "attn_t", "h_t", *ATTENTION_ARRAYS)
    load_weights(last, *front_weights)
    load((last, "x"), saved_in[last - 1]["x3"], r.dx, other_sem.at[1])
    place.greet()

    def rows_of(ref):
        return lambda slot: ref.at[pl.ds(pl.multiple_of(slot * BLOCK, BLOCK), BLOCK)]

    back_x = TokenReturn(place, num_seqs, rows_of(last_in), x_out, back_sems, 1)
    back_x.start()

    sets = {}
    for k, (name, layer, units, order, _, _) in enumerate(set_list):

        def result(u, value, name=name, layer=layer, units=units):
            if name == "vec":
                res_vec[...] = value
            elif name == "down":
                res_down[layer] = value
            else:
                res[layer, RESULT_UNITS.index(units[u])] = value

        sets[(layer, name)] = PairReduce(
            place,
            totals[k],
            order,
            [landings[landing_index(name, layer)], *lines[3 * k : 3 * k + 3]],
            set_sems(sems, k),
            result,
        )
    stages = (None, "stage1", "stage2", "stage3", "finish")

    def act(layer, *events):
        for before, stage, name in events:
            if layer + before < LAYERS:
                getattr(sets[(layer + before, name)], stages[stage])()

    def ticker(layer):
        names = iter(TICKS)
        return lambda: act(layer, *SCHEDULE.get(next(names), ()))

    def ready_for(layer):
        def ready(*names):
            for name in names:
                sets[(layer, name)].start()

        return ready

    mask_setup(r, True)
    need("vec")
    r.vec[...] = jnp.transpose(vec_buf[...].reshape(WIDTH, BLOCK).astype(F32))[0:8, :]

    w = Gathered(weight_bufs)
    exchanges = []
    for layer in range(last, -1, -1):
        s = SimpleNamespace(**bufs)
        s.k = (bufs["k"], bufs["k1"])
        s.v = (bufs["v"], bufs["v1"])
        out = FusedGrads(totals[layer * len(GRAD_SETS) : (layer + 1) * len(GRAD_SETS)])
        out.dx2, out.dza, out.dq = r.dx2, r.dza, r.dq
        out.dk, out.dv, out.dk_out, out.dv_out = r.own_dk, r.own_dv, r.send_dk, r.send_dv
        dx_in = r.dq if layer == last else r.dx
        need((layer, "cot"), *((layer, n) for n in EARLY_ARRAYS), (layer, "h_t"))
        need(*((layer, "w", n) for n in ffn_weights))
        ready = ready_for(layer)
        tick = ticker(layer)

        def take(n, layer=layer):
            need((layer, "act_t", n), (layer, "slope", n))

        def drop(n, layer=layer):
            if n + 2 < CHUNKS:
                stream(layer, n + 2)
            elif layer:
                stream(layer - 1, n + 2 - CHUNKS)

        kept = SimpleNamespace(
            hid_t=bufs["hid_t"],
            attn_t=bufs["attn_t"],
            h_t=bufs["h_t"],
            act_t=lambda n: r.act_t.at[n % 2],
            slope=lambda n: r.slope.at[n % 2],
            take=take,
            drop=drop,
        )
        ffn_backward(r, w, layer, dx_in, s, out, tick, ready, kept)
        if layer:
            load_arrays(layer - 1, *EARLY_ARRAYS)
            load_weights(layer - 1, *ffn_weights)
        else:
            load((0, "x"), x0_in, r.dz, other_sem.at[2])
        need(*((layer, n) for n in ATTENTION_ARRAYS))
        for copy in exchanges:
            copy.wait_send()
        attention_backward(r, s, out, tick)
        if layer:
            load_arrays(layer - 1, *ATTENTION_ARRAYS)
        exchanges = []
        for k, (src, dst) in enumerate(((r.send_dk, r.got_dk), (r.send_dv, r.got_dv))):
            copy = remote(
                src,
                dst,
                dkv_send.at[layer, k],
                dkv_recv.at[layer, k],
                place.sibling(),
            )
            copy.start()
            exchanges.append(copy)
        need(*((layer, "w", n) for n in front_weights), (layer, "x"))
        g = SimpleNamespace(
            dq=r.dq,
            dk=r.own_dk,
            dv=r.own_dv,
            dk_in=r.got_dk,
            dv_in=r.got_dv,
            dza=r.dza,
            dx2=r.dx2,
        )

        def arrived(pair=tuple(exchanges)):
            for copy in pair:
                copy.wait_recv()

        s.x = r.dx if layer else r.dz
        layer_front_backward(r, w, layer, s, g, out, r.dx, arrived, tick, ready, bufs["h_t"])
        if layer:
            load_arrays(layer - 1, "h_t")
            load_weights(layer - 1, *front_weights)

    r.out[...] = r.dx[...].astype(BF)
    back = TokenReturn(place, num_seqs, rows_of(r.out), g_out, back_sems, 0)
    back.start()
    tall = jnp.concatenate([r.vg[...], jnp.zeros((BLOCK - 8, WIDTH), F32)], axis=0)
    totals[-1][0] = jnp.transpose(tall).reshape(totals[-1].shape[1:])
    ready_for(0)("vec")
    act(0, *LAST)
    for one in sets.values():
        one.finish_sends()
    for copy in exchanges:
        copy.wait_send()
    back.finish()
    back_x.finish()


def landing_index(name, layer):
    names = [one[0] for one in GRAD_SETS]
    if name == "vec":
        return len(names) + len(LATE_SETS)
    if name in LATE_SETS and layer:
        return len(names) + LATE_SETS.index(name)
    return names.index(name)


def backward(dims, rows, lengths, positions, cot, x0, result, units, saved):
    num_seqs = lengths.shape[0]
    per_dev = positions // BLOCK
    dma = pltpu.SemaphoreType.DMA
    scratch = [
        vm(len(names), *dims, 2, 4 * rows if names[0] == "down" else rows, WIDTH) for names, _ in SETS
    ]
    scratch += [vm(*dims, 2, rows, BLOCK)]
    scratch += [vm(*layer_shape(n), dtype=t) for n, t in BACKWARD_ARRAYS.items()]
    scratch += list(FUSED_WORK.values())
    set_list = grad_set_list(dims, rows)
    scratch += [vm(*s, dtype=t) for *_, s, t in set_list]
    landings, lines = {}, []
    for name, layer, _, order, (count, num_z, num_x, num_y, _, *block), dtype in set_list:
        landings[landing_index(name, layer)] = vm(count, num_z, num_x, num_y, *block, dtype=dtype)
        lines.append(vm(count, num_z, 2, *block, dtype=dtype))
        lines.append(vm(count, num_z, *block, dtype=dtype))
        lines.append(vm(num_z - 1, count, *block, dtype=dtype))
    scratch += [landings[k] for k in sorted(landings)] + lines
    scratch += pair_reduce_sems(len(set_list))
    scratch += [
        dma((LAYERS, 16)),
        dma((LAYERS, len(BACKWARD_ARRAYS))),
        dma((3,)),
        dma((LAYERS, 2, CHUNKS)),
        dma((LAYERS, 2)),
        dma((LAYERS, 2)),
    ]
    scratch += return_sems(2, num_seqs, per_dev)
    arrays = [saved[layer][n] for layer in range(LAYERS) for n in saved_names(layer)]
    return pl.pallas_call(
        partial(backward_kernel, dims, num_seqs),
        out_shape=[
            jax.ShapeDtypeStruct((LAYERS, len(RESULT_UNITS), rows, WIDTH), F32),
            jax.ShapeDtypeStruct((LAYERS, 4 * rows, WIDTH), F32),
            jax.ShapeDtypeStruct((rows, BLOCK), F32),
            jax.ShapeDtypeStruct((num_seqs, positions, WIDTH), BF),
            jax.ShapeDtypeStruct((num_seqs, positions, WIDTH), BF),
        ],
        in_specs=[ANY] * (3 + len(units) + len(arrays)) + [SMEM],
        out_specs=[VMEM] * 3 + [ANY] * 2,
        scratch_shapes=scratch,
        compiler_params=pltpu.CompilerParams(
            collective_id=1, has_side_effects=True, vmem_limit_bytes=BACKWARD_VMEM
        ),
        name="backward",
    )(cot, x0, result, *units, *arrays, lengths)


def unpack_kernel(*refs):
    res, res_down, res_vec, x_in, g_in = refs[:5]
    x_out, g_out = refs[5:7]
    ga, wq, wk, wv, wo, wga, ba, gf, wup, wdown, wgf, bf = refs[7:19]
    square = refs[19]
    x_out[...] = x_in[...]
    g_out[...] = g_in[...].astype(F32)
    plain = {"q": wq, "k": wk, "v": wv, "o": wo, "ga": wga, "gf": wgf}
    for layer in range(LAYERS):
        for k, name in enumerate(RESULT_UNITS):
            if name in plain:
                plain[name][layer] = res[layer, k]
            else:
                n = int(name[2:])
                wup[layer, :, n * WIDTH : (n + 1) * WIDTH] = res[layer, k]
        wdown[layer] = res_down[layer]
    rows = res_vec.shape[0]
    square[...] = jnp.zeros_like(square)
    square[0:rows, :] = res_vec[...]
    turned = jnp.transpose(square[...])
    for layer in range(LAYERS):
        for which, ref in enumerate((ga, ba, gf, bf)):
            row = layer * 4 + which
            ref[layer : layer + 1, :] = turned[row : row + 1, 0:rows]


def unpack(res, res_down, res_vec, x_out, g_out):
    rows = res_vec.shape[0]
    vector = jax.ShapeDtypeStruct((LAYERS, rows), F32)
    matrix = jax.ShapeDtypeStruct((LAYERS, rows, WIDTH), F32)
    outs = [
        jax.ShapeDtypeStruct(x_out.shape, x_out.dtype),
        jax.ShapeDtypeStruct(g_out.shape, F32),
        vector,
        matrix,
        matrix,
        matrix,
        matrix,
        matrix,
        vector,
        vector,
        jax.ShapeDtypeStruct((LAYERS, rows, CHUNKS * WIDTH), F32),
        jax.ShapeDtypeStruct((LAYERS, CHUNKS * rows, WIDTH), F32),
        matrix,
        vector,
    ]
    return pl.pallas_call(
        unpack_kernel,
        out_shape=outs,
        in_specs=[VMEM] * 5,
        out_specs=[VMEM] * 14,
        scratch_shapes=[vm(BLOCK, BLOCK, dtype=F32)],
        name="unpack",
    )(res, res_down, res_vec, x_out, g_out)


def plain_forward(gathered, vec_in, lengths, x_tok, exchange):
    x = x_tok.reshape(TOKENS, WIDTH)
    front = front_call(gathered, vec_in, 0, x)
    saved = []
    for layer in range(LAYERS):
        front["k1"], front["v1"] = exchange(front["k"], front["v"])
        got = middle_call(gathered, vec_in, lengths, layer, x, front)
        keep = dict(front)
        keep.update({n: got[n] for n in ("attn", "lse", "a", "x2", "y", "gf")})
        keep["x"] = x
        saved.append(keep)
        x = got["x3"]
        front = {n[1:]: got[n] for n in ("nh", "nq", "nk", "nv", "ngate") if n in got}
    return saved, x.astype(BF).reshape(SLOTS, BLOCK, WIDTH)


def per_device(num_dp, num_sp, *args):
    inputs, lengths, gain_a, wq, wk, wv, wo, wga, ba, gain_f, wup, wdown, wgf, bf, cotangent = args
    num_y = num_sp // 2
    num_x = num_y
    dims = (num_dp // num_x, num_x, num_y)
    rows = wq.shape[1]
    weights = (wq, wk, wv, wo, wga, wgf, wup, wdown)
    if rows % 16 == 0 and dims[0] % CHUNKS == 0 and num_x == num_y == 2:
        cot, last, x0, units, saved = forward(
            dims, inputs, cotangent, weights, (gain_a, ba, gain_f, bf), lengths
        )
        *summed, g_out, x_out = backward(
            dims, rows, lengths, inputs.shape[1], cot, x0, last, units, saved
        )
        return tuple(unpack(*summed, x_out, g_out))
    vectors = jnp.stack(
        [v[layer] for layer in range(LAYERS) for v in (gain_a, ba, gain_f, bf)], axis=1
    )
    vecs = jnp.pad(vectors, ((0, 0), (0, WIDTH - vectors.shape[1])))
    x_tok, cot_tok, *units = collect(dims, inputs, cotangent, weights, vecs)
    gathered = {}
    for layer in range(LAYERS):
        gathered[layer] = [
            u.reshape(u.shape[0], -1, WIDTH)
            for u in units[len(SETS) * layer : len(SETS) * (layer + 1)]
        ]
    vec_in = gathered[0][0][VEC_UNIT, :, :BLOCK]

    swap = [(i, i ^ 1) for i in range(num_sp)]

    def exchange(*arrays):
        return [lax.ppermute(a, "sp", swap) for a in arrays]

    saved, layer_out = plain_forward(gathered, vec_in, lengths, x_tok, exchange)

    dx = cot_tok.reshape(TOKENS, WIDTH)
    vec_grads = None
    grads = [None] * LAYERS
    for layer in reversed(range(LAYERS)):
        g = backward_call(gathered, vec_in, lengths, layer, dx, saved[layer])
        g["dk_in"], g["dv_in"] = exchange(g["dk_out"], g["dv_out"])
        vec_grads = g["vg"] if vec_grads is None else vec_grads + g["vg"]
        got = front_backward_call(gathered, vec_in, layer, saved[layer], g, vec_grads, layer == 0)
        dx = got["dx"]
        grads[layer] = (
            jnp.concatenate([got["qkv"], g["ga"][3:]], axis=0),
            g["gb"],
            g["gd"],
        )
        vec_grads = got["vg"] if layer else got["vg_t"]

    flat = [arr for layer in range(LAYERS) for arr in grads[layer]] + [vec_grads]
    toks = [dx.reshape(SLOTS, BLOCK, WIDTH), layer_out]
    *summed, g_out, x_out = spread(dims, inputs.shape[0], flat, toks)
    a, b, d = ([summed[3 * layer + k] for layer in range(LAYERS)] for k in range(3))

    def unit(k):
        return jnp.stack([a[layer][k] for layer in range(LAYERS)])

    def vector(which):
        return jnp.stack([summed[6][0, :, layer * 4 + which] for layer in range(LAYERS)])

    grad_up = jnp.stack(
        [
            jnp.concatenate([a[layer][6], b[layer][0], b[layer][1], b[layer][2]], axis=1)
            for layer in range(LAYERS)
        ]
    )
    grad_down = jnp.stack([d[layer][0] for layer in range(LAYERS)])
    return (
        x_out,
        g_out,
        vector(0),
        unit(0),
        unit(1),
        unit(2),
        unit(3),
        unit(4),
        vector(1),
        vector(2),
        grad_up,
        grad_down,
        unit(5),
        vector(3),
    )


def solution(mesh):
    tokens = P("dp", "sp", None)
    vector = P(None, ("dp", "sp"))
    matrix = P(None, ("dp", "sp"), None)
    return jax.shard_map(
        partial(per_device, mesh.shape["dp"], mesh.shape["sp"]),
        mesh=mesh,
        in_specs=(
            tokens,
            P("dp", None),
            vector,
            matrix,
            matrix,
            matrix,
            matrix,
            matrix,
            vector,
            vector,
            matrix,
            matrix,
            matrix,
            vector,
            tokens,
        ),
        out_specs=(
            tokens,
            tokens,
            vector,
            matrix,
            matrix,
            matrix,
            matrix,
            matrix,
            vector,
            vector,
            matrix,
            matrix,
            matrix,
            vector,
        ),
        check_vma=False,
    )
```

```python
from functools import partial
from types import SimpleNamespace

import jax
import jax.numpy as jnp
from jax import lax
from jax.experimental import pallas as pl
from jax.experimental.pallas import tpu as pltpu
from jax.sharding import PartitionSpec as P

LEN = 1024
LAYERS = 2
WIDTH = 512
HEAD_DIM = 64
BLOCK = 128
SLOTS = LEN // (2 * BLOCK)
TOKENS = SLOTS * BLOCK
HALF = TOKENS // 2
PAIRS = WIDTH // (2 * HEAD_DIM)
CHUNKS = 4
EPSILON = 1e-05
NEG_FILL = -1e30
F32 = jnp.float32
BF = jnp.bfloat16
MESH = pl.DeviceIdType.MESH
VMEM_BYTES = 56 * 1024 * 1024
BACKWARD_VMEM = 62 * 1024 * 1024

ANY = pl.BlockSpec(memory_space=pl.ANY)
VMEM = pl.BlockSpec(memory_space=pltpu.VMEM)
SMEM = pl.BlockSpec(memory_space=pltpu.SMEM)

SETS = (
    (("k", "v"), (1, 2)),
    (("q", "ga"), (2, 1)),
    (("o", "gf", "up0", "up1", "up2", "up3"), (2, 1)),
    (("down",), (1, 2)),
)
VEC_UNIT = len(SETS[0][0])
UNITS_A = 7
UNITS_B = 3


class Place:
    def __init__(self, dims):
        self.dims = dims
        num_z, num_x, num_y = dims
        self.dp = lax.axis_index("dp")
        self.sp = lax.axis_index("sp")
        self.at = (
            lax.div(self.dp, num_x),
            lax.rem(self.dp, num_x),
            lax.div(self.sp, 2),
            lax.rem(self.sp, 2),
        )
        self.z, self.x, self.y, self.core = self.at

    def device(self, axis=None, position=None):
        z, x, y, core = [position if k == axis else v for k, v in enumerate(self.at)]
        return (z * self.dims[1] + x, y * 2 + core)

    def sibling(self):
        return self.device(3, 1 - self.core)

    def greet(self):
        barrier = pltpu.get_barrier_semaphore()
        count = jnp.int32(0)
        for axis in (0, 1):
            reach = self.dims[0] - 1 if axis == 0 else 1
            for step in [s for s in range(-reach, reach + 1) if s]:
                position = self.at[axis] + step
                there = (position >= 0) & (position < self.dims[axis])

                @pl.when(there)
                def _(axis=axis, position=position):
                    pl.semaphore_signal(
                        barrier, inc=1, device_id=self.device(axis, position), device_id_type=MESH
                    )

                count = count + there.astype(jnp.int32)
        num_sp = self.dims[2] * 2
        for step in range(1, num_sp):
            other = lax.rem(self.sp + step, num_sp)
            pl.semaphore_signal(barrier, inc=1, device_id=(self.dp, other), device_id_type=MESH)
        pl.semaphore_wait(barrier, count + (num_sp - 1))


def remote(src, dst, send_sem, recv_sem, device):
    return pltpu.make_async_remote_copy(
        src_ref=src,
        dst_ref=dst,
        send_sem=send_sem,
        recv_sem=recv_sem,
        device_id=device,
        device_id_type=MESH,
    )


def when(cond, action):
    if cond is True:
        action()
    elif cond is not False:
        pl.when(cond)(action)


def both(*conds):
    out = True
    for cond in conds:
        if cond is False:
            return False
        if cond is not True:
            out = cond if out is True else out & cond
    return out


class GatherSet:
    def __init__(self, place, ref, order, sems):
        self.place, self.ref, self.order = place, ref, order
        self.z_send, self.z_recv, self.s_send, self.s_recv, self.c_send, self.c_recv = sems
        self.sends = []

    def put(self, src, send_sem, recv_sem, device, cond):
        copy = remote(src, src, send_sem, recv_sem, device)
        when(cond, copy.start)
        self.sends.append((cond, copy))

    def got(self, src, send_sem, recv_sem, cond):
        copy = remote(src, src, send_sem, recv_sem, self.place.sibling())
        when(cond, copy.wait_recv)

    def z_block(self, zb):
        return self.ref.at[:, zb, self.place.x, self.place.y, self.place.core]

    def stage_block(self, stage, zb, q):
        axis = self.order[stage]
        index = [zb, self.place.x, self.place.y, self.place.core]
        if stage == 1:
            index[self.order[0]] = slice(None)
        index[axis] = q
        return self.ref.at[(slice(None), *index)]

    def phase_z(self, t, side, zb, valid):
        num = self.place.dims[0]
        z = self.place.z
        if t > 0:
            self.got(self.z_block(zb), self.z_send.at[0, zb], self.z_recv.at[zb], valid)
        if (t == 0 or side == 0) and t <= num - 2:
            self.put(
                self.z_block(zb),
                self.z_send.at[1, zb],
                self.z_recv.at[zb],
                self.place.device(0, z + 1),
                both(valid, z < num - 1),
            )
        if (t == 0 or side == 1) and t <= num - 2:
            self.put(
                self.z_block(zb),
                self.z_send.at[0, zb],
                self.z_recv.at[zb],
                self.place.device(0, z - 1),
                both(valid, z > 0),
            )

    def stage_start(self, stage, zb, valid):
        axis = self.order[stage]
        p, num = self.place.at[axis], self.place.dims[axis]
        for way, cond in ((0, p > 0), (1, p < num - 1)):
            self.put(
                self.stage_block(stage, zb, p),
                self.s_send.at[stage, way, zb, p],
                self.s_recv.at[stage, zb, p],
                self.place.device(axis, p + 2 * way - 1),
                both(valid, cond),
            )

    def stage_finish(self, stage, zb, valid):
        axis = self.order[stage]
        p, num = self.place.at[axis], self.place.dims[axis]
        for u in range(1, num):
            for side in (0, 1):
                q = p - u if side == 0 else p + u
                there = both(valid, q >= 0 if side == 0 else q < num)
                block = self.stage_block(stage, zb, q)
                self.got(
                    block,
                    self.s_send.at[stage, side, zb, q],
                    self.s_recv.at[stage, zb, q],
                    there,
                )
                if u <= num - 2:
                    way = 1 - side
                    self.put(
                        block,
                        self.s_send.at[stage, way, zb, q],
                        self.s_recv.at[stage, zb, q],
                        self.place.device(axis, p + 2 * way - 1),
                        both(there, p < num - 1 if way == 1 else p > 0),
                    )

    def core_start(self, zb, valid):
        block = self.ref.at[:, zb, :, :, self.place.core]
        self.put(block, self.c_send.at[zb], self.c_recv.at[zb], self.place.sibling(), valid)

    def core_finish(self, zb, valid):
        block = self.ref.at[:, zb, :, :, 1 - self.place.core]
        self.got(block, self.c_send.at[zb], self.c_recv.at[zb], valid)

    def finish_sends(self):
        for cond, copy in self.sends:
            when(cond, copy.wait_send)


class PairGather:
    def __init__(self, place, ref, order, sems):
        self.place, self.ref, self.order = place, ref, order
        self.z_send, self.z_recv, self.s_send, self.s_recv, self.c_send, self.c_recv = sems
        self.sends = []

    def put(self, src, send_sem, recv_sem, device):
        copy = remote(src, src, send_sem, recv_sem, device)
        copy.start()
        self.sends.append(copy)

    def got(self, src, send_sem, recv_sem):
        remote(src, src, send_sem, recv_sem, self.place.sibling()).wait_recv()

    def own(self, zb):
        return self.ref.at[:, zb, self.place.x, self.place.y, self.place.core]

    def block(self, stage, zb, near):
        index = [zb, self.place.x, self.place.y, self.place.core]
        if stage == 1:
            index[self.order[0]] = slice(None)
        axis = self.order[stage]
        index[axis] = self.place.at[axis] if near else 1 - self.place.at[axis]
        return self.ref.at[(slice(None), *index)]

    def source(self, t):
        num = self.place.dims[0]
        return lax.rem(self.place.z + (num - t), num)

    def open(self):
        num = self.place.dims[0]
        z = self.place.z
        self.send_stage(0, 0)
        for t in range(1, num):
            target = lax.rem(z + t, num)
            self.put(
                self.own(z),
                self.z_send.at[t - 1],
                self.z_recv.at[t - 1],
                self.place.device(0, target),
            )

    def send_stage(self, stage, t):
        axis = self.order[stage]
        self.put(
            self.block(stage, self.source(t), True),
            self.s_send.at[stage, t],
            self.s_recv.at[stage, t],
            self.place.device(axis, 1 - self.place.at[axis]),
        )

    def got_stage(self, stage, t):
        block = self.block(stage, self.source(t), False)
        self.got(block, self.s_send.at[stage, t], self.s_recv.at[stage, t])

    def stage1(self, *steps):
        for t in steps:
            self.got(self.own(self.source(t)), self.z_send.at[t - 1], self.z_recv.at[t - 1])
            self.send_stage(0, t)

    def stage2(self, *steps):
        for t in steps:
            self.got_stage(0, t)
            self.send_stage(1, t)

    def stage3(self, *steps):
        for t in steps:
            self.got_stage(1, t)
            block = self.ref.at[:, self.source(t), :, :, self.place.core]
            self.put(block, self.c_send.at[t], self.c_recv.at[t], self.place.sibling())

    def finish(self):
        for t in range(self.place.dims[0]):
            block = self.ref.at[:, self.source(t), :, :, 1 - self.place.core]
            self.got(block, self.c_send.at[t], self.c_recv.at[t])

    def finish_sends(self):
        for copy in self.sends:
            copy.wait_send()


def pair_gather_sems(num_sets, num_z):
    dma = pltpu.SemaphoreType.DMA
    return [
        dma((num_sets, num_z - 1)),
        dma((num_sets, num_z - 1)),
        dma((num_sets, 2, num_z)),
        dma((num_sets, 2, num_z)),
        dma((num_sets, num_z)),
        dma((num_sets, num_z)),
    ]


class PairReduce:
    def __init__(self, place, ref, order, bufs, sems, result):
        self.place, self.ref, self.order, self.result = place, ref, order, result
        self.from_core, self.line1, self.line2, self.line_z = bufs
        self.c_send, self.c_recv, self.s_send, self.s_recv, self.z_send, self.z_recv = sems
        self.sends = []

    def put(self, src, dst, send_sem, recv_sem, device):
        copy = remote(src, dst, send_sem, recv_sem, device)
        copy.start()
        return copy

    def cut(self, core, x=slice(None), y=slice(None)):
        return self.ref.at[:, :, x, y, core]

    def axis_cut(self, stage, near):
        at = [slice(None), slice(None), slice(None)]
        if stage == 1:
            at[self.order[0]] = self.place.at[self.order[0]]
        axis = self.order[stage]
        at[axis] = self.place.at[axis] if near else 1 - self.place.at[axis]
        return self.cut(self.place.core, at[1], at[2])

    def wait(self, buf, send_sem, recv_sem):
        remote(buf, buf, send_sem, recv_sem, self.place.sibling()).wait_recv()

    def start(self):
        copy = self.put(
            self.cut(1 - self.place.core),
            self.from_core,
            self.c_send,
            self.c_recv,
            self.place.sibling(),
        )
        self.sends.append(copy)

    def send_stage(self, stage):
        axis = self.order[stage]
        copy = self.put(
            self.axis_cut(stage, False),
            (self.line1, self.line2)[stage],
            self.s_send.at[stage],
            self.s_recv.at[stage],
            self.place.device(axis, 1 - self.place.at[axis]),
        )
        self.sends.append(copy)

    def stage1(self):
        self.wait(self.from_core, self.c_send, self.c_recv)
        add_units(self.cut(self.place.core), self.from_core)
        self.send_stage(0)

    def stage2(self):
        self.wait(self.line1, self.s_send.at[0], self.s_recv.at[0])
        add_units(self.axis_cut(0, True), self.line1)
        self.send_stage(1)

    def stage3(self):
        self.wait(self.line2, self.s_send.at[1], self.s_recv.at[1])
        place = self.place
        num = place.dims[0]
        add_units(self.axis_cut(1, True), self.line2)
        for t in range(num - 1, 0, -1):
            target = lax.rem(place.z + t, num)
            self.put(
                self.ref.at[:, target, place.x, place.y, place.core],
                self.line_z.at[t - 1],
                self.z_send,
                self.z_recv,
                place.device(0, target),
            )
        self.sends.append(
            remote(self.line_z, self.line_z, self.z_send, self.z_recv, place.sibling())
        )

    def finish(self):
        place = self.place
        mine = self.ref.at[:, place.z, place.x, place.y, place.core]
        self.wait(self.line_z, self.z_send, self.z_recv)
        for u in range(mine.shape[0]):
            value = mine[u].astype(F32)
            for slot in range(place.dims[0] - 1):
                value = value + self.line_z[slot, u].astype(F32)
            self.result(u, value)

    def finish_sends(self):
        for copy in self.sends:
            copy.wait_send()


def pair_reduce_sems(num_sets):
    dma = pltpu.SemaphoreType.DMA
    return [
        dma((num_sets,)),
        dma((num_sets,)),
        dma((num_sets, 2)),
        dma((num_sets, 2)),
        dma((num_sets,)),
        dma((num_sets,)),
    ]


def z_items(place, far_first):
    num = place.dims[0]
    order = range(num - 1, -1, -1) if far_first else range(num)
    rounds = []
    for t in order:
        if t == 0:
            rounds.append([(0, 0, place.z, True)])
        else:
            rounds.append(
                [(t, 0, place.z - t, place.z - t >= 0), (t, 1, place.z + t, place.z + t < num)]
            )
    return rounds


def pipeline(rounds, phases):
    for k in range(len(rounds) + len(phases) - 1):
        for lag, phase in enumerate(phases):
            if 0 <= k - lag < len(rounds):
                for item in rounds[k - lag]:
                    phase(*item)


def gather_sems(num_sets, dims):
    num_z, num_x, num_y = dims
    line = max(num_x, num_y)
    dma = pltpu.SemaphoreType.DMA
    return [
        dma((num_sets, 2, num_z)),
        dma((num_sets, num_z)),
        dma((num_sets, 2, 2, num_z, line)),
        dma((num_sets, 2, num_z, line)),
        dma((num_sets, num_z)),
        dma((num_sets, num_z)),
    ]


def set_sems(sems, k):
    return [sem.at[k] for sem in sems]


def run_gather(place, sets):
    def each(method):
        def phase(t, side, zb, valid):
            for one in sets:
                method(one, t, side, zb, valid)

        return phase

    def phase_one(one, t, side, zb, valid):
        one.phase_z(t, side, zb, valid)
        one.stage_start(0, zb, valid)

    def phase_two(one, t, side, zb, valid):
        one.stage_finish(0, zb, valid)
        one.stage_start(1, zb, valid)

    def phase_three(one, t, side, zb, valid):
        one.stage_finish(1, zb, valid)
        one.core_start(zb, valid)

    def phase_four(one, t, side, zb, valid):
        one.core_finish(zb, valid)

    pipeline(
        z_items(place, False), [each(phase_one), each(phase_two), each(phase_three), each(phase_four)]
    )
    for one in sets:
        one.finish_sends()


def own_shards(weights, vecs, layer):
    wq, wk, wv, wo, wga, wgf, wup, wdown = weights
    plain = {"q": wq, "k": wk, "v": wv, "o": wo, "ga": wga, "gf": wgf, "down": wdown}
    out = []
    for which, (names, _) in enumerate(SETS):
        for unit, name in enumerate(names):
            if name in plain:
                out.append((which, unit, plain[name].at[layer]))
            else:
                out.append((which, unit, wup.at[layer, :, pl.ds(int(name[2:]) * WIDTH, WIDTH)]))
    if layer == 0 and vecs is not None:
        out.append((0, VEC_UNIT, vecs))
    return out


OWN_COPIES = LAYERS * sum(len(names) for names, _ in SETS) + 1


def set_shapes(dims, rows):
    shapes = []
    for layer in range(LAYERS):
        for which, (names, _) in enumerate(SETS):
            count = len(names) + (layer == 0 and which == 0)
            depth = 4 * rows if names[0] == "down" else rows
            shapes.append((count, *dims, 2, depth, WIDTH))
    return shapes


def start_own(place, weights, vecs, refs, sem, layers=range(LAYERS), first=0):
    copies = []
    for layer in layers:
        for which, unit, src in own_shards(weights, vecs, layer):
            dst = refs[layer * len(SETS) + which].at[(unit, *place.at)]
            copy = pltpu.make_async_copy(src, dst, sem.at[first + len(copies)])
            copy.start()
            copies.append(copy)
    return copies


def gather_sets(place, refs, sems):
    return [
        GatherSet(place, ref, SETS[k % len(SETS)][1], set_sems(sems, k)) for k, ref in enumerate(refs)
    ]


class TokenMove:
    def __init__(self, place, num_seqs, src, dst_slot, sems, which):
        self.place, self.num_seqs, self.src, self.dst_slot = place, num_seqs, src, dst_slot
        self.send_sem, self.recv_sem, self.local_sem = (s.at[which] for s in sems)
        self.per_dev = LEN // (place.dims[2] * 2) // BLOCK
        self.sends = []

    def start(self):
        for seq in range(self.num_seqs):
            for i in range(self.per_dev):
                g = self.place.sp * self.per_dev + i
                target = seq * 2 + lax.rem(g, 2)
                here = target == self.place.sp
                block = self.src.at[seq, pl.ds(i * BLOCK, BLOCK)]
                slot = self.dst_slot(lax.div(g, 2))
                copy = remote(
                    block,
                    slot,
                    self.send_sem.at[seq, i],
                    self.recv_sem.at[lax.div(g, 2)],
                    (self.place.dp, target),
                )
                local = pltpu.make_async_copy(block, slot, self.local_sem.at[seq, i])
                when(jnp.logical_not(here), copy.start)
                when(here, local.start)
                self.sends.append((here, copy, local))

    def finish(self):
        for here, copy, local in self.sends:
            when(jnp.logical_not(here), copy.wait_send)
            when(here, local.wait)
        for slot in range(SLOTS):
            source = lax.div(2 * slot + self.place.core, self.per_dev)
            goal = self.dst_slot(slot)
            arrived = remote(
                goal, goal, self.send_sem.at[0, 0], self.recv_sem.at[slot], self.place.sibling()
            )
            when(source != self.place.sp, arrived.wait_recv)


def collect_kernel(dims, num_seqs, *refs):
    inputs, cotangent = refs[:2]
    weights, vecs = refs[2:10], refs[10]
    x_out, cot_out = refs[11:13]
    count = LAYERS * len(SETS)
    sets = refs[13 : 13 + count]
    sems = refs[13 + count : 19 + count]
    own_sem, *tok_sems = refs[19 + count :]
    place = Place(dims)
    own = start_own(place, weights, vecs, sets, own_sem)
    place.greet()
    moves = []
    for which, (src, dst) in enumerate(((inputs, x_out), (cotangent, cot_out))):
        moves.append(TokenMove(place, num_seqs, src, lambda s, dst=dst: dst.at[s], tok_sems, which))
        moves[-1].start()
    for copy in own:
        copy.wait()
    run_gather(place, gather_sets(place, sets, sems))
    for move in moves:
        move.finish()


def token_sems(num_seqs, per_dev):
    dma = pltpu.SemaphoreType.DMA
    return [dma((2, num_seqs, per_dev)), dma((2, SLOTS)), dma((2, num_seqs, per_dev))]


def collect(dims, inputs, cotangent, weights, vecs):
    rows = weights[0].shape[1]
    num_seqs = inputs.shape[0]
    tok = jax.ShapeDtypeStruct((SLOTS, BLOCK, WIDTH), BF)
    outs = [tok, tok] + [jax.ShapeDtypeStruct(s, BF) for s in set_shapes(dims, rows)]
    return pl.pallas_call(
        partial(collect_kernel, dims, num_seqs),
        out_shape=outs,
        in_specs=[ANY] * 11,
        out_specs=[ANY] * len(outs),
        scratch_shapes=gather_sems(len(SETS) * LAYERS, dims)
        + [pltpu.SemaphoreType.DMA((OWN_COPIES,))]
        + token_sems(num_seqs, inputs.shape[1] // BLOCK),
        compiler_params=pltpu.CompilerParams(
            collective_id=0, has_side_effects=True, vmem_limit_bytes=VMEM_BYTES
        ),
        name="collect",
    )(inputs, cotangent, *weights, vecs)


def add_units(total, part):
    count = total.shape[0]

    def body(u, carry):
        total[u] = total[u] + part[u]
        return carry

    lax.fori_loop(0, count, body, 0)


class ReduceSet:
    def __init__(self, place, total, other, mine, order, bufs, sems, result):
        self.place, self.total, self.other, self.mine, self.order = place, total, other, mine, order
        self.from_core, self.line1, self.line2, self.line_z = bufs
        self.c_send, self.c_recv, self.s_send, self.s_recv, self.z_send, self.z_recv = sems
        self.result = result
        self.sends = []

    def put(self, src, dst, send_sem, recv_sem, device, cond):
        copy = remote(src, dst, send_sem, recv_sem, device)
        when(cond, copy.start)
        self.sends.append((cond, copy))

    def core_copy(self, zb):
        return remote(
            self.other(zb),
            self.from_core.at[:, zb],
            self.c_send.at[zb],
            self.c_recv.at[zb],
            self.place.sibling(),
        )

    def start(self, zb, valid):
        copy = self.core_copy(zb)
        when(valid, copy.start)
        if self.mine is not None:
            when(valid, self.mine(zb).start)
        self.sends.append((valid, copy))

    def core_finish(self, zb, valid):
        def go():
            if self.mine is not None:
                self.mine(zb).wait()
            self.core_copy(zb).wait_recv()
            add_units(self.total(zb, slice(None), slice(None)), self.from_core.at[:, zb])

        when(valid, go)

    def block(self, stage, zb, q):
        index = [zb, self.place.x, self.place.y]
        if stage == 0:
            index[self.order[1]] = slice(None)
        index[self.order[stage]] = q
        return self.total(*index)

    def line(self, stage, way, zb, slot):
        if self.place.dims[self.order[stage]] == 2:
            way = 0
        return (self.line1, self.line2)[stage].at[way, slot, :, zb]

    def take(self, stage, way, zb, q, cond):
        slot = q - 1 if way == 0 else q
        buf = self.line(stage, way, zb, slot)
        copy = remote(
            buf,
            buf,
            self.s_send.at[stage, way, zb, slot],
            self.s_recv.at[stage, way, zb, slot],
            self.place.sibling(),
        )

        def go():
            copy.wait_recv()
            add_units(self.block(stage, zb, q), buf)

        when(cond, go)

    def stage_send(self, stage, zb, valid):
        axis = self.order[stage]
        p, num = self.place.at[axis], self.place.dims[axis]
        for u in range(num - 1, 0, -1):
            for side in (0, 1):
                q = p - u if side == 0 else p + u
                there = both(valid, q >= 0 if side == 0 else q < num)
                way = 1 - side
                if u <= num - 2:
                    self.take(stage, way, zb, q, both(there, p > 0 if side == 1 else p < num - 1))
                slot = q - 1 if side == 1 else q
                self.put(
                    self.block(stage, zb, q),
                    self.line(stage, way, zb, slot),
                    self.s_send.at[stage, way, zb, slot],
                    self.s_recv.at[stage, way, zb, slot],
                    self.place.device(axis, p + 1 if side == 1 else p - 1),
                    there,
                )

    def stage_keep(self, stage, zb, valid):
        axis = self.order[stage]
        p, num = self.place.at[axis], self.place.dims[axis]
        self.take(stage, 0, zb, p, both(valid, p > 0))
        self.take(stage, 1, zb, p, both(valid, p < num - 1))

    def z_slot(self, source, target):
        return jnp.where(source < target, source, source - 1)

    def z_step(self, t, zb, valid):
        place = self.place
        if t > 0:
            slot = self.z_slot(place.z, zb)
            self.put(
                self.total(zb, place.x, place.y),
                self.line_z.at[slot],
                self.z_send.at[self.z_slot(zb, place.z)],
                self.z_recv.at[slot],
                place.device(0, zb),
                valid,
            )

    def finish(self):
        place = self.place
        mine = self.total(place.z, place.x, place.y)
        num = place.dims[0] - 1
        for slot in range(num):
            buf = self.line_z.at[slot]
            remote(
                buf, buf, self.z_send.at[slot], self.z_recv.at[slot], place.sibling()
            ).wait_recv()
        for u in range(mine.shape[0]):
            value = mine[u].astype(F32)
            for slot in range(num):
                value = value + self.line_z[slot, u].astype(F32)
            self.result(u, value)

    def finish_sends(self):
        for cond, copy in self.sends:
            when(cond, copy.wait_send)

    def steps(self, rounds):
        def round_of(k):
            def act():
                for lag in (2, 1, 0):
                    if not 0 <= k - lag < len(rounds):
                        continue
                    for t, side, zb, valid in rounds[k - lag]:
                        if lag == 0:
                            self.core_finish(zb, valid)
                            self.stage_send(0, zb, valid)
                        elif lag == 1:
                            self.stage_keep(0, zb, valid)
                            self.stage_send(1, zb, valid)
                        else:
                            self.stage_keep(1, zb, valid)
                            self.z_step(t, zb, valid)

            return act

        return [round_of(k) for k in range(len(rounds) + 2)]


def reduce_sems(num_sets, dims):
    num_z, num_x, num_y = dims
    line = max(num_x, num_y)
    dma = pltpu.SemaphoreType.DMA
    return [
        dma((num_sets, num_z)),
        dma((num_sets, num_z)),
        dma((num_sets, 2, 2, num_z, line - 1)),
        dma((num_sets, 2, 2, num_z, line - 1)),
        dma((num_sets, num_z - 1)),
        dma((num_sets, num_z - 1)),
    ]


def reduce_bufs(count, depth, columns, dims, order, dtype):
    one, two = dims[order[0]], dims[order[1]]

    def ways(num):
        return 1 if num == 2 else 2

    return [
        pltpu.VMEM((count, *dims, depth, columns), dtype),
        pltpu.VMEM((ways(one), one - 1, count, dims[0], two, depth, columns), dtype),
        pltpu.VMEM((ways(two), two - 1, count, dims[0], depth, columns), dtype),
        pltpu.VMEM((dims[0] - 1, count, depth, columns), dtype),
    ]


ORDER_A = (2, 1)
ORDER_B = (1, 2)


class TokenReturn:
    def __init__(self, place, num_seqs, src_slot, dst, sems, which):
        self.place, self.num_seqs, self.src_slot, self.dst = place, num_seqs, src_slot, dst
        self.send_sem, self.recv_sem, self.local_sem = (s.at[which] for s in sems)
        self.per_dev = LEN // (place.dims[2] * 2) // BLOCK
        self.sends = []

    def start(self, slots=range(SLOTS)):
        for slot in slots:
            g = 2 * slot + self.place.core
            target = lax.div(g, self.per_dev)
            row = lax.rem(g, self.per_dev)
            here = target == self.place.sp
            block = self.src_slot(slot)
            goal = self.dst.at[self.place.y, pl.ds(pl.multiple_of(row * BLOCK, BLOCK), BLOCK)]
            copy = remote(
                block,
                goal,
                self.send_sem.at[slot],
                self.recv_sem.at[self.place.y, row],
                (self.place.dp, target),
            )
            local = pltpu.make_async_copy(block, goal, self.local_sem.at[slot])
            when(jnp.logical_not(here), copy.start)
            when(here, local.start)
            self.sends.append((here, copy, local))

    def finish(self):
        for here, copy, local in self.sends:
            when(jnp.logical_not(here), copy.wait_send)
            when(here, local.wait)
        for seq in range(self.num_seqs):
            for i in range(self.per_dev):
                g = self.place.sp * self.per_dev + i
                source = seq * 2 + lax.rem(g, 2)
                goal = self.dst.at[seq, pl.ds(i * BLOCK, BLOCK)]
                arrived = remote(
                    goal, goal, self.send_sem.at[0], self.recv_sem.at[seq, i], self.place.sibling()
                )
                when(source != self.place.sp, arrived.wait_recv)


def return_sems(num, num_seqs, per_dev):
    dma = pltpu.SemaphoreType.DMA
    return [dma((num, SLOTS)), dma((num, num_seqs, per_dev)), dma((num, SLOTS))]


def spread_kernel(dims, num_seqs, num_tok, *refs):
    refs = list(refs)

    def pop(count):
        out = refs[:count]
        del refs[:count]
        return out

    grads, toks, outs, tok_outs = pop(7), pop(num_tok), pop(7), pop(num_tok)
    totals, bufs, sems, own, tok_sems = pop(7), pop(28), pop(6), pop(1)[0], pop(3)
    place = Place(dims)
    core = place.core
    place.greet()
    sets = []
    for k in range(7):
        grad, total = grads[k], totals[k]

        def result(u, value, k=k):
            outs[k][u] = value

        sets.append(
            ReduceSet(
                place,
                lambda z, x, y, total=total: total.at[:, z, x, y],
                lambda z, grad=grad: grad.at[:, z, :, :, 1 - core],
                lambda z, grad=grad, total=total, k=k: pltpu.make_async_copy(
                    grad.at[:, z, :, :, core], total.at[:, z], own.at[k, z]
                ),
                ORDER_A if k in (0, 3, 6) else ORDER_B,
                bufs[4 * k : 4 * k + 4],
                set_sems(sems, k),
                result,
            )
        )
    rounds = z_items(place, True)
    for items in rounds:
        for t, side, zb, valid in items:
            for one in sets:
                one.start(zb, valid)
    moves = []
    for which, (src, dst) in enumerate(zip(toks, tok_outs)):
        moves.append(
            TokenReturn(place, num_seqs, lambda s, src=src: src.at[s], dst, tok_sems, which)
        )
        moves[-1].start()
    lists = [one.steps(rounds) for one in sets]
    for acts in zip(*lists):
        for act in acts:
            act()
    for one in sets:
        one.finish()
        one.finish_sends()
    for move in moves:
        move.finish()


def spread(dims, num_seqs, grads, toks):
    num_z, num_x, num_y = dims
    per_dev = LEN // (num_y * 2) // BLOCK
    rows = WIDTH // (num_z * num_x * num_y * 2)
    dma = pltpu.SemaphoreType.DMA
    set_sizes = [(UNITS_A, rows), (UNITS_B, rows), (1, 4 * rows)] * LAYERS + [(1, rows)]
    outs, bufs, totals = [], [], []
    for k, (count, depth) in enumerate(set_sizes):
        columns = WIDTH if k < 6 else BLOCK
        dtype = BF if k < 6 else F32
        outs.append(jax.ShapeDtypeStruct((count, depth, columns), F32))
        order = ORDER_A if k in (0, 3, 6) else ORDER_B
        totals.append(pltpu.VMEM((count, *dims, depth, columns), dtype))
        bufs += reduce_bufs(count, depth, columns, dims, order, dtype)
    outs += [jax.ShapeDtypeStruct((num_seqs, per_dev * BLOCK, WIDTH), t.dtype) for t in toks]
    shaped = [
        g.reshape(count, num_z, num_x, num_y, 2, depth, g.shape[-1])
        for g, (count, depth) in zip(grads, set_sizes)
    ]
    return pl.pallas_call(
        partial(spread_kernel, dims, num_seqs, len(toks)),
        out_shape=outs,
        in_specs=[ANY] * (7 + len(toks)),
        out_specs=[VMEM] * 7 + [ANY] * len(toks),
        scratch_shapes=totals
        + bufs
        + reduce_sems(7, dims)
        + [dma((7, num_z))]
        + return_sems(len(toks), num_seqs, per_dev),
        compiler_params=pltpu.CompilerParams(
            collective_id=1, has_side_effects=True, vmem_limit_bytes=VMEM_BYTES
        ),
        name="spread",
    )(*shaped, *toks)


def dot(left, right):
    return lax.dot_general(left, right, (((1,), (0,)), ((), ())), preferred_element_type=F32)


def dot_nt(left, right):
    return lax.dot_general(left, right, (((1,), (1,)), ((), ())), preferred_element_type=F32)


def dot_tn(left, right):
    return lax.dot_general(left, right, (((0,), (0,)), ((), ())), preferred_element_type=F32)


def normalize(values):
    centre = jnp.mean(values, axis=-1, keepdims=True)
    shifted = values - centre
    inv_std = lax.rsqrt(jnp.mean(shifted * shifted, axis=-1, keepdims=True) + EPSILON)
    return shifted * inv_std, inv_std


def norm_back(grad_normed, normed, inv_std, gain):
    grad_hat = grad_normed * gain
    mean_one = jnp.mean(grad_hat, axis=-1, keepdims=True)
    mean_two = jnp.mean(grad_hat * normed, axis=-1, keepdims=True)
    return inv_std * (grad_hat - mean_one - normed * mean_two)


def halves(body, tick=None):
    if tick is not None:
        for i in range(2):
            body(pl.ds(i * HALF, HALF))
            tick()
        return

    def step(i, carry):
        body(pl.ds(pl.multiple_of(i * HALF, HALF), HALF))
        return carry

    lax.fori_loop(0, 2, step, 0)


def column_sums(values):
    return jnp.sum(values, axis=0, keepdims=True)


GELU_A = 0.7978845608028654
GELU_B = 0.044715


def gelu(t):
    return 0.5 * t * (1.0 + jnp.tanh(GELU_A * (t + GELU_B * t * t * t)))


def gelu_both(t):
    square = t * t
    wave = jnp.tanh(GELU_A * (t + GELU_B * t * square))
    up = 0.5 * (1.0 + wave)
    slope = up + 0.5 * t * (1.0 - wave * wave) * (GELU_A * (1.0 + 3.0 * GELU_B * square))
    return t * up, slope


class Weights:
    def __init__(self, r, layer, names):
        self.r, self.layer = r, layer
        self.copies = {}
        sets = r.g[layer]
        place_of = {}
        for which, (units, _) in enumerate(SETS):
            for unit, name in enumerate(units):
                src = sets[which].at[unit]
                if name == "down":
                    place_of["down"] = [
                        (src.at[pl.ds(k * WIDTH, WIDTH)], r.w_scratch, ("down", k))
                        for k in range(CHUNKS)
                    ]
                elif name[:2] == "up":
                    place_of.setdefault("up", []).append((src, r.w_scratch, ("up", int(name[2:]))))
                else:
                    place_of[name] = [(src, r.w_scratch, name)]
        for name in names:
            group = []
            for src, pool, key in place_of[name]:
                index = r.w_index[(layer, key)]
                copy = pltpu.make_async_copy(src, pool.at[index], r.w_sem.at[index])
                copy.start()
                group.append(copy)
            self.copies[name] = group
        self.waited = set()

    def need(self, *names):
        for name in names:
            if name in self.copies and name not in self.waited:
                self.waited.add(name)
                for copy in self.copies[name]:
                    copy.wait()

    def get(self, name):
        return self.r.w_scratch[self.r.w_index[(self.layer, name)]]

    def chunk(self, name, n):
        return self.r.w_scratch[self.r.w_index[(self.layer, (name, 0))] + n]


def vec_row(r, layer, which):
    row = layer * 4 + which
    return r.vec[row : row + 1, :]


def load_vectors(r):
    r.vec[...] = jnp.transpose(r.vec_in[...].astype(F32))[0:8, :]


def mask_setup(r, flipped):
    core = lax.rem(lax.axis_index("sp"), 2)
    seq = lax.div(lax.axis_index("sp"), 2)
    ends = []
    total = jnp.int32(0)
    for d in range(4):
        total = total + r.lengths[seq, d]
        ends.append(total)

    def segment(position):
        out = jnp.zeros(position.shape, jnp.int32)
        for end in ends:
            out = out + (position >= end).astype(jnp.int32)
        return out

    for j in range(SLOTS):
        for which in range(2):
            count = (j + 1) * BLOCK
            other = core if which == 0 else 1 - core
            q_shape, k_shape = ((1, BLOCK), (count, 1)) if flipped else ((BLOCK, 1), (1, count))
            q_in = lax.broadcasted_iota(jnp.int32, q_shape, 1 if flipped else 0)
            k_in = lax.broadcasted_iota(jnp.int32, k_shape, 0 if flipped else 1)
            q_pos = (2 * j + core) * BLOCK + q_in
            k_pos = k_in + BLOCK * lax.div(k_in, BLOCK) + other * BLOCK
            q_seg = segment(q_pos)
            k_seg = segment(k_pos)
            k_seg = jnp.where(k_seg >= 4, -1, k_seg)
            allowed = ((q_seg == k_seg) & (k_pos <= q_pos)) | (q_pos == k_pos)
            bias = jnp.where(allowed, 0.0, NEG_FILL).astype(F32)
            if flipped:
                r.bias[j, which * TOKENS : which * TOKENS + count, :] = bias
            else:
                r.bias[j, :, which * TOKENS : which * TOKENS + count] = bias


def two_heads(block):
    lane = lax.broadcasted_iota(jnp.int32, block.shape, 1)
    zero = jnp.zeros_like(block)
    first = jnp.where(lane < HEAD_DIM, block, zero)
    second = jnp.where(lane < HEAD_DIM, zero, block)
    return jnp.concatenate([first, second], axis=0)


def join_heads(stacked):
    first, second = stacked[:BLOCK], stacked[BLOCK:]
    lane = lax.broadcasted_iota(jnp.int32, first.shape, 1)
    return jnp.where(lane < HEAD_DIM, first, second)


def layer_front(
    r, w, layer, x_ref, h_ref, q_ref, k_ref, v_ref, gate_ref, tick=None, exchange=lambda: None
):
    w.need("q", "k", "v", "ga")

    def first(rows):
        normed, _ = normalize(x_ref[rows, :].astype(F32))
        hidden = (normed * vec_row(r, layer, 0)).astype(BF)
        h_ref[rows, :] = hidden
        k_ref[rows, :] = dot(hidden, w.get("k")).astype(BF)
        v_ref[rows, :] = dot(hidden, w.get("v")).astype(BF)

    halves(first)
    exchange()
    if tick is not None:
        tick()

    def second(rows):
        hidden = h_ref[rows, :]
        q_ref[rows, :] = (dot(hidden, w.get("q")) * (HEAD_DIM**-0.5)).astype(BF)
        gate_ref[rows, :] = jax.nn.sigmoid(dot(hidden, w.get("ga")) + vec_row(r, layer, 1))

    halves(second)
    if tick is not None:
        tick()


def attention(r, q_ref, k_refs, v_refs, out_ref, lse_ref, tick=None):
    lse_ref[...] = jnp.zeros_like(lse_ref)

    def pair_step(pair, carry):
        cols = pl.ds(pl.multiple_of(pair * BLOCK, BLOCK), BLOCK)
        for j in range(SLOTS):
            rows = slice(j * BLOCK, (j + 1) * BLOCK)
            count = (j + 1) * BLOCK
            queries = two_heads(q_ref[rows, cols])
            scores = []
            for which in range(2):
                bias = r.bias[j, :, which * TOKENS : which * TOKENS + count]
                score = dot_nt(queries, k_refs[which][0:count, cols])
                scores.append(score + jnp.concatenate([bias, bias], axis=0))
            top = jnp.maximum(
                jnp.max(scores[0], axis=1, keepdims=True), jnp.max(scores[1], axis=1, keepdims=True)
            )
            expo = [jnp.exp(score - top) for score in scores]
            total = jnp.sum(expo[0], axis=1, keepdims=True) + jnp.sum(expo[1], axis=1, keepdims=True)
            mixed = dot(expo[0].astype(BF), v_refs[0][0:count, cols])
            mixed = mixed + dot(expo[1].astype(BF), v_refs[1][0:count, cols])
            out_ref[rows, cols] = join_heads(mixed / total).astype(BF)
            lse = top + jnp.log(total)
            lane = lax.broadcasted_iota(jnp.int32, (BLOCK, BLOCK), 1)
            kept = lse_ref[rows, :]
            kept = jnp.where(lane == 2 * pair, lse[:BLOCK], kept)
            lse_ref[rows, :] = jnp.where(lane == 2 * pair + 1, lse[BLOCK:], kept)
        return carry

    if tick is None:
        lax.fori_loop(0, PAIRS, pair_step, 0)
        return
    for part in range(2):
        lax.fori_loop(part * PAIRS // 2, (part + 1) * PAIRS // 2, pair_step, 0)
        tick()


def layer_back_half(
    r, w, layer, x_ref, attn_ref, gate_ref, a_ref, x2_ref, y_ref, gf_ref, x3_ref, tick=None, more=None
):
    w.need("o", "gf", "up", "down")

    def body(rows):
        branch = dot(attn_ref[rows, :], w.get("o"))
        a_ref[rows, :] = branch.astype(a_ref.dtype)
        after = x_ref[rows, :].astype(F32) + gate_ref[rows, :] * branch
        x2_ref[rows, :] = after
        normed, _ = normalize(after)
        hidden = (normed * vec_row(r, layer, 2)).astype(BF)
        if more is not None:
            more.hid_t[:, rows] = jnp.transpose(hidden)
        out = None
        for n in range(CHUNKS):
            up = dot(hidden, w.chunk("up", n))
            if more is None:
                active = gelu(up).astype(BF)
            else:
                value, slope = gelu_both(up)
                active = value.astype(BF)
                more.slope[n, rows, :] = slope.astype(BF)
                more.act_t[n, :, rows] = jnp.transpose(active)
            part = dot(active, w.chunk("down", n))
            out = part if out is None else out + part
        y_ref[rows, :] = out.astype(y_ref.dtype)
        gate = jax.nn.sigmoid(dot(hidden, w.get("gf")) + vec_row(r, layer, 3))
        gf_ref[rows, :] = gate
        x3_ref[rows, :] = after + gate * out

    halves(body, tick)


def nothing(*args):
    pass


def ffn_backward(r, w, layer, dx_ref, s, out, tick=nothing, ready=nothing, kept=None):
    w.need("o", "gf", "up", "down")
    hid_t = r.hid_t if kept is None else kept.hid_t

    def start(rows):
        grad = dx_ref[rows, :].astype(F32)
        gate = s.gf[rows, :]
        r.dy[rows, :] = (grad * gate).astype(BF)
        dz = (grad * s.y[rows, :].astype(F32) * gate * (1.0 - gate)).astype(BF)
        r.dz[rows, :] = dz
        if kept is None:
            normed, _ = normalize(s.x2[rows, :])
            r.hid[rows, :] = (normed * vec_row(r, layer, 2)).astype(BF)
        r.dh[rows, :] = dot_nt(dz, w.get("gf"))

    halves(start)
    if kept is None:
        r.hid_t[...] = jnp.transpose(r.hid[...])
    out.unit("gf", dot(hid_t[...], r.dz[...]))
    r.vg[layer * 4 + 3 : layer * 4 + 4, :] = column_sums(r.dz[...].astype(F32))
    tick()

    for n in range(CHUNKS):
        if kept is not None:
            kept.take(n)

        def body(rows, n=n):
            if kept is None:
                act, slope = gelu_both(dot(r.hid[rows, :], w.chunk("up", n)))
                r.act[rows, :] = act.astype(BF)
            else:
                slope = kept.slope(n)[rows, :].astype(F32)
            du = (dot_nt(r.dy[rows, :], w.chunk("down", n)) * slope).astype(BF)
            r.du[rows, :] = du
            r.dh[rows, :] += dot_nt(du, w.chunk("up", n))

        halves(body)
        if kept is None:
            out.down(n, dot_tn(r.act[...], r.dy[...]))
        else:
            out.down(n, dot(kept.act_t(n)[...], r.dy[...]))
        out.unit("up" + str(n), dot(hid_t[...], r.du[...]))
        if kept is not None:
            kept.drop(n)
        if n == 1:
            ready("up_a")
        elif n == 3:
            ready("up_b", "down")
        tick()

    r.sums[...] = jnp.zeros_like(r.sums)

    def finish(rows):
        normed, inv_std = normalize(s.x2[rows, :])
        grad_hidden = r.dh[rows, :]
        r.sums[0:1, :] += column_sums(grad_hidden * normed)
        mid = dx_ref[rows, :].astype(F32) + norm_back(
            grad_hidden, normed, inv_std, vec_row(r, layer, 2)
        )
        out.dx2[rows, :] = mid
        gate = s.gate[rows, :]
        da = (mid * gate).astype(BF)
        r.dy[rows, :] = da
        dza = (mid * s.a[rows, :].astype(F32) * gate * (1.0 - gate)).astype(BF)
        out.dza[rows, :] = dza
        r.sums[1:2, :] += column_sums(dza.astype(F32))
        r.dattn[rows, :] = dot_nt(da, w.get("o")).astype(BF)

    halves(finish)
    tick()
    r.vg[layer * 4 + 2 : layer * 4 + 3, :] = r.sums[0:1, :]
    r.vg[layer * 4 + 1 : layer * 4 + 2, :] = r.sums[1:2, :]
    if kept is None:
        out.unit("o", dot_tn(s.attn[...], r.dy[...]))
        out.unit("ga", dot_tn(s.h[...], out.dza[...]))
    else:
        out.unit("o", dot(kept.attn_t[...], r.dy[...]))
        out.unit("ga", dot(kept.h_t[...], out.dza[...]))
    ready("mix")
    tick()


def attention_backward(r, s, out, tick=None):
    for j in range(SLOTS):
        r.lse_t[j] = jnp.transpose(s.lse[j * BLOCK : (j + 1) * BLOCK, :])[0:8, :]

    def slot_step(pair, cols, j):
        rows = slice(j * BLOCK, (j + 1) * BLOCK)
        count = (j + 1) * BLOCK
        queries = two_heads(s.q[rows, cols])
        grads = two_heads(r.dattn[rows, cols])
        lse = jnp.concatenate(
            [r.lse_t[j, pl.ds(2 * pair, 1), :], r.lse_t[j, pl.ds(2 * pair + 1, 1), :]], axis=1
        )
        probs, slopes = [], []
        delta = None
        for which in range(2):
            bias = r.bias[j, which * TOKENS : which * TOKENS + count, :]
            score = dot_nt(s.k[which][0:count, cols], queries)
            prob = jnp.exp(score + jnp.concatenate([bias, bias], axis=1) - lse)
            slope = dot_nt(s.v[which][0:count, cols], grads)
            part = column_sums(prob * slope)
            delta = part if delta is None else delta + part
            probs.append(prob)
            slopes.append(slope)
        grad_q = None
        for which in range(2):
            ds = (probs[which] * (slopes[which] - delta)).astype(BF)
            dv = dot(probs[which].astype(BF), grads)
            dk = dot(ds, queries)
            dk_ref, dv_ref = (out.dk, out.dv) if which == 0 else (r.dk_other, r.dv_other)
            where = cols if which == 0 else slice(None)
            if j == SLOTS - 1:
                dk_ref[:, where] = dk
                dv_ref[:, where] = dv
            else:
                dk_ref[0:count, where] += dk
                dv_ref[0:count, where] += dv
            part = dot_tn(s.k[which][0:count, cols], ds)
            grad_q = part if grad_q is None else grad_q + part
        grad_q = join_heads(jnp.transpose(grad_q)) * (HEAD_DIM**-0.5)
        out.dq[rows, cols] = grad_q.astype(BF)

    def pair_step(pair, carry):
        cols = pl.ds(pl.multiple_of(pair * BLOCK, BLOCK), BLOCK)
        for j in range(SLOTS - 1, -1, -1):
            slot_step(pair, cols, j)
        if tick is not None:
            tick()
        out.dk_out[:, cols] = r.dk_other[...].astype(BF)
        out.dv_out[:, cols] = r.dv_other[...].astype(BF)
        return carry

    if tick is None:
        lax.fori_loop(0, PAIRS, pair_step, 0)
    else:
        for pair in range(PAIRS):
            pair_step(pair, 0)


def layer_front_backward(
    r, w, layer, s, g, out, dx_ref, arrived=nothing, tick=nothing, ready=nothing, h_t=None
):
    w.need("q", "k", "v", "ga")
    if h_t is None:
        h_t = r.hid_t
        h_t[...] = jnp.transpose(s.h[...])
    out.unit("q", dot(h_t[...], g.dq[...]))
    ready("q")

    def before(rows):
        grad_hidden = dot_nt(g.dq[rows, :], w.get("q"))
        r.dh[rows, :] = grad_hidden + dot_nt(g.dza[rows, :], w.get("ga"))

    halves(before)
    arrived()

    def start(rows):
        r.dk[rows, :] = (g.dk[rows, :] + g.dk_in[rows, :].astype(F32)).astype(BF)
        r.dv[rows, :] = (g.dv[rows, :] + g.dv_in[rows, :].astype(F32)).astype(BF)

    halves(start)
    out.unit("k", dot(h_t[...], r.dk[...]))
    out.unit("v", dot(h_t[...], r.dv[...]))
    ready("kv")
    tick()
    r.sums[...] = jnp.zeros_like(r.sums)

    def body(rows):
        grad_hidden = r.dh[rows, :] + dot_nt(r.dk[rows, :], w.get("k"))
        grad_hidden += dot_nt(r.dv[rows, :], w.get("v"))
        normed, inv_std = normalize(s.x[rows, :].astype(F32))
        r.sums[0:1, :] += column_sums(grad_hidden * normed)
        dx_ref[rows, :] = g.dx2[rows, :] + norm_back(
            grad_hidden, normed, inv_std, vec_row(r, layer, 0)
        )

    halves(body)
    tick()
    r.vg[layer * 4 : layer * 4 + 1, :] = r.sums[0:1, :]


FRONT = ("q", "k", "v", "ga")
BACK = ("o", "gf", "up", "down")


def weight_index(wanted):
    index, count = {}, 0
    for layer, names in wanted:
        for name in names:
            if name in ("up", "down"):
                for k in range(CHUNKS):
                    index[(layer, (name, k))] = count
                    count += 1
            else:
                index[(layer, name)] = count
                count += 1
    return index, count


def compute_call(body, name, wanted, gathered, ins, outs, scratch):
    in_names, out_names, scratch_names = list(ins), list(outs), list(scratch)
    layers = sorted({layer for layer, _ in wanted})
    index, count = weight_index(wanted)
    weight_refs = [arr for layer in layers for arr in gathered[layer]]

    def kernel(*refs):
        refs = list(refs)
        r = SimpleNamespace()
        r.g = {}
        for layer in layers:
            r.g[layer] = [refs.pop(0) for _ in SETS]
        for field in in_names + out_names + scratch_names:
            setattr(r, field, refs.pop(0))
        r.w_scratch, r.w_sem, r.vec = refs
        r.w_index = index
        r.w = {}
        for layer, names in wanted:
            r.w[layer] = Weights(r, layer, names)
        load_vectors(r)
        body(r)

    return pl.pallas_call(
        kernel,
        out_shape=[outs[n] for n in out_names],
        in_specs=[ANY] * len(weight_refs) + [SMEM if n == "lengths" else VMEM for n in in_names],
        out_specs=[VMEM] * len(out_names),
        scratch_shapes=[scratch[n] for n in scratch_names]
        + [
            pltpu.VMEM((count, WIDTH, WIDTH), BF),
            pltpu.SemaphoreType.DMA((count,)),
            pltpu.VMEM((8, WIDTH), F32),
        ],
        compiler_params=pltpu.CompilerParams(vmem_limit_bytes=VMEM_BYTES),
        name=name,
    )(*weight_refs, *[ins[n] for n in in_names])


def tok(dtype):
    return jax.ShapeDtypeStruct((TOKENS, WIDTH), dtype)


def vm(*shape, dtype=BF):
    return pltpu.VMEM(shape, dtype)


def front_outs(prefix):
    return {
        prefix + "h": tok(BF),
        prefix + "q": tok(BF),
        prefix + "k": tok(BF),
        prefix + "v": tok(BF),
        prefix + "gate": tok(F32),
    }


def back_outs():
    return {
        "attn": tok(BF),
        "lse": jax.ShapeDtypeStruct((TOKENS, BLOCK), F32),
        "a": tok(F32),
        "x2": tok(F32),
        "y": tok(F32),
        "gf": tok(F32),
        "x3": tok(F32),
    }


BIAS = vm(SLOTS, BLOCK, 2 * TOKENS, dtype=F32)
BIAS_T = vm(SLOTS, 2 * TOKENS, BLOCK, dtype=F32)


def grad_outs():
    return {
        "a": jax.ShapeDtypeStruct((UNITS_A, WIDTH, WIDTH), BF),
        "b": jax.ShapeDtypeStruct((UNITS_B, WIDTH, WIDTH), BF),
        "d": jax.ShapeDtypeStruct((1, CHUNKS * WIDTH, WIDTH), BF),
    }


BACKWARD_SCRATCH = {
    "bias": BIAS_T,
    "dy": vm(TOKENS, WIDTH),
    "dz": vm(TOKENS, WIDTH),
    "hid": vm(TOKENS, WIDTH),
    "hid_t": vm(WIDTH, TOKENS),
    "dh": vm(TOKENS, WIDTH, dtype=F32),
    "act": vm(TOKENS, WIDTH),
    "du": vm(TOKENS, WIDTH),
    "sums": vm(8, WIDTH, dtype=F32),
    "dattn": vm(TOKENS, WIDTH),
    "lse_t": vm(SLOTS, 8, BLOCK, dtype=F32),
    "dk_other": vm(TOKENS, BLOCK, dtype=F32),
    "dv_other": vm(TOKENS, BLOCK, dtype=F32),
}


def front_call(gathered, vec_in, layer, x):
    def body(r):
        layer_front(r, r.w[layer], layer, r.x, r.h, r.q, r.k, r.v, r.gate)

    outs = front_outs("")
    got = compute_call(
        body, "front", [(layer, FRONT)], gathered, {"vec_in": vec_in, "x": x}, outs, {}
    )
    return dict(zip(outs, got))


def middle_call(gathered, vec_in, lengths, layer, x, s):
    ins = {
        "vec_in": vec_in,
        "lengths": lengths,
        "x": x,
        "q": s["q"],
        "k0": s["k"],
        "v0": s["v"],
        "k1": s["k1"],
        "v1": s["v1"],
        "gate": s["gate"],
    }
    last = layer == LAYERS - 1
    outs = back_outs()
    wanted = [(layer, BACK)]
    if not last:
        outs.update(front_outs("n"))
        wanted.append((layer + 1, FRONT))

    def body(r):
        mask_setup(r, False)
        attention(r, r.q, (r.k0, r.k1), (r.v0, r.v1), r.attn, r.lse)
        layer_back_half(
            r, r.w[layer], layer, r.x, r.attn, r.gate, r.a, r.x2, r.y, r.gf, r.x3
        )
        if not last:
            layer_front(
                r, r.w[layer + 1], layer + 1, r.x3, r.nh, r.nq, r.nk, r.nv, r.ngate
            )

    got = compute_call(body, "middle", wanted, gathered, ins, outs, {"bias": BIAS})
    return dict(zip(outs, got))


class Gathered:
    def __init__(self, refs):
        self.place = {
            name: refs[which].at[unit]
            for which, (names, _) in enumerate(SETS)
            for unit, name in enumerate(names)
        }

    def need(self, *names):
        pass

    def get(self, name):
        return self.place[name][...].reshape(WIDTH, WIDTH)

    def chunk(self, name, n):
        if name == "up":
            return self.get("up" + str(n))
        ref = self.place["down"]
        part = ref.shape[0] // CHUNKS
        return ref[n * part : (n + 1) * part].reshape(WIDTH, WIDTH)


LAYER_ARRAYS = {
    "h": BF,
    "q": BF,
    "k": BF,
    "v": BF,
    "k1": BF,
    "v1": BF,
    "gate": F32,
    "attn": BF,
    "lse": F32,
    "a": BF,
    "x2": F32,
    "y": BF,
    "gf": F32,
    "x3": F32,
    "h_t": BF,
    "attn_t": BF,
    "hid_t": BF,
    "act_t": BF,
    "slope": BF,
}
NOT_SAVED = ("h", "attn")


def layer_shape(name):
    if name in ("act_t", "slope"):
        return (CHUNKS, WIDTH, TOKENS)
    return (TOKENS, BLOCK if name == "lse" else WIDTH)


def saved_names(layer):
    return [n for n in LAYER_ARRAYS if n not in NOT_SAVED and (n != "x3" or layer < LAYERS - 1)]


def forward_kernel(dims, num_seqs, *refs):
    refs = list(refs)

    def pop(count):
        out = refs[:count]
        del refs[:count]
        return out

    num_sets = LAYERS * len(SETS)
    inputs, cotangent = pop(2)
    weights = pop(8)
    vectors = pop(4)
    (lengths,) = pop(1)
    cot_out, result, x0_out = pop(3)
    set_outs = pop(num_sets)
    saved_outs = [{n: pop(1)[0] for n in saved_names(layer)} for layer in range(LAYERS)]
    sets = pop(num_sets)
    arrays = [dict(zip(LAYER_ARRAYS, pop(len(LAYER_ARRAYS)))) for _ in range(LAYERS)]
    x0, cot, last, bias, vec, square = pop(6)
    sems = pop(6)
    (own_sem,) = pop(1)
    tok_sems = pop(3)
    kv_send, kv_recv, out_sem = pop(3)

    place = Place(dims)
    own = [start_own(place, weights, None, sets, own_sem, (0,))]
    own.append(start_own(place, weights, None, sets, own_sem, (1,), len(own[0])))
    rows = vectors[0].shape[1]
    square[...] = jnp.zeros_like(square)
    for layer in range(LAYERS):
        for which, ref in enumerate(vectors):
            row = layer * 4 + which
            square[row : row + 1, 0:rows] = ref[layer : layer + 1, :].astype(F32)
    vec_unit = sets[0].at[VEC_UNIT, place.z, place.x, place.y, place.core]
    vec_unit[...] = jnp.zeros(vec_unit.shape, BF)
    vec_unit[:, 0:BLOCK] = jnp.transpose(square[...])[0:rows, :].astype(BF)
    place.greet()

    def rows_of(ref):
        return lambda slot: ref.at[pl.ds(pl.multiple_of(slot * BLOCK, BLOCK), BLOCK)]

    move_x = TokenMove(place, num_seqs, inputs, rows_of(x0), tok_sems, 0)
    move_cot = TokenMove(place, num_seqs, cotangent, rows_of(cot), tok_sems, 1)
    outgoing = []

    def save(src, dst):
        copy = pltpu.make_async_copy(src, dst, out_sem.at[len(outgoing)])
        copy.start()
        outgoing.append(copy)

    gathers = [
        PairGather(place, ref, SETS[k % len(SETS)][1], set_sems(sems, k))
        for k, ref in enumerate(sets)
    ]
    far = range(1, dims[0])

    every = range(dims[0])

    def event(method, group, *args):
        two = gathers[2 * group : 2 * group + 2]
        if not args:
            for one in two:
                getattr(one, method)()
        for t in args:
            for one in two:
                getattr(one, method)(t)

    for copy in own[0]:
        copy.wait()
    event("open", 0)
    move_x.start()
    for copy in own[1]:
        copy.wait()

    def finish_group(group):
        event("finish", group)
        for which in (2 * group, 2 * group + 1):
            save(sets[which], set_outs[which])

    after = (
        {
            "front0": (("stage2", 1, 1),),
            "front1": (("stage2", 1, 2, 3), ("stage1", 2, *far), ("stage2", 2, 0)),
            "attend1": (
                ("stage2", 2, *far),
                ("stage3", 1, *every),
                ("stage1", 3, *far),
                ("done", 1),
            ),
            "feed0": (("stage2", 3, 0, 1), ("stage3", 2, *every)),
            "feed1": (("stage2", 3, 2, 3), ("done", 2)),
        },
        {"attend1": (("stage3", 3, *every), ("done", 3))},
    )

    def ticker(layer, name):
        count = [0]

        def tick():
            for method, group, *args in after[layer].get(name + str(count[0]), ()):
                if method == "done":
                    finish_group(group)
                else:
                    event(method, group, *args)
            count[0] += 1

        return tick

    r = SimpleNamespace(bias=bias, lengths=lengths, vec=vec)
    event("open", 1)
    event("stage2", 0, 0)
    for t in far:
        event("stage1", 0, t)
        event("stage2", 0, t)
    event("open", 2)
    event("stage1", 1, *far)
    event("stage3", 0, *every)
    event("open", 3)
    event("stage2", 1, 0)
    mask_setup(r, False)
    finish_group(0)
    move_x.finish()
    vec_block = sets[0][VEC_UNIT].reshape(WIDTH, WIDTH)[:, :BLOCK]
    vec[...] = jnp.transpose(vec_block.astype(F32))[0:8, :]
    save(x0, x0_out)

    exchanges = []
    x = x0
    for layer in range(LAYERS):
        s = SimpleNamespace(**arrays[layer])
        w = Gathered(sets[layer * len(SETS) : (layer + 1) * len(SETS)])
        def exchange(s=s, layer=layer):
            for k, (src, dst) in enumerate(((s.k, s.k1), (s.v, s.v1))):
                copy = remote(src, dst, kv_send.at[layer, k], kv_recv.at[layer, k], place.sibling())
                copy.start()
                exchanges.append(copy)

        tick = ticker(layer, "front")
        layer_front(r, w, layer, x, s.h, s.q, s.k, s.v, s.gate, tick, exchange)
        if layer == 0:
            move_cot.start()
        s.h_t[...] = jnp.transpose(s.h[...])
        for name in ("h_t", "q", "k", "v", "gate"):
            save(arrays[layer][name], saved_outs[layer][name])
        exchanges[-2].wait_recv()
        exchanges[-1].wait_recv()
        attention(r, s.q, (s.k, s.k1), (s.v, s.v1), s.attn, s.lse, ticker(layer, "attend"))
        s.attn_t[...] = jnp.transpose(s.attn[...])
        for name in ("k1", "v1", "attn_t", "lse"):
            save(arrays[layer][name], saved_outs[layer][name])
        layer_back_half(
            r,
            w,
            layer,
            x,
            s.attn,
            s.gate,
            s.a,
            s.x2,
            s.y,
            s.gf,
            s.x3,
            ticker(layer, "feed"),
            s,
        )
        for name in ("a", "x2", "y", "gf", "x3", "hid_t", "act_t", "slope"):
            if layer < LAYERS - 1 or name != "x3":
                save(arrays[layer][name], saved_outs[layer][name])
        x = s.x3

    last[...] = x[...].astype(BF)
    save(last, result)
    move_cot.finish()
    save(cot, cot_out)
    for copy in exchanges:
        copy.wait_send()
    for one in gathers:
        one.finish_sends()
    for copy in outgoing:
        copy.wait()


def forward(dims, inputs, cotangent, weights, vectors, lengths):
    rows = weights[0].shape[1]
    num_seqs, positions, _ = inputs.shape
    shapes = set_shapes(dims, rows)
    dma = pltpu.SemaphoreType.DMA
    layer_types = list(LAYER_ARRAYS.items()) * LAYERS
    outs = [tok(BF), tok(BF), tok(BF)]
    outs += [jax.ShapeDtypeStruct(s, BF) for s in shapes]
    for layer in range(LAYERS):
        for name in saved_names(layer):
            outs.append(jax.ShapeDtypeStruct(layer_shape(name), LAYER_ARRAYS[name]))
    num_saves = len(outs)
    scratch = [vm(*s) for s in shapes]
    scratch += [vm(*layer_shape(n), dtype=t) for n, t in layer_types]
    scratch += [vm(TOKENS, WIDTH), vm(TOKENS, WIDTH), vm(TOKENS, WIDTH), BIAS]
    scratch += [vm(8, WIDTH, dtype=F32), vm(BLOCK, BLOCK, dtype=F32)]
    scratch += pair_gather_sems(len(shapes), dims[0])
    scratch += [dma((OWN_COPIES,))]
    scratch += token_sems(num_seqs, positions // BLOCK)
    scratch += [dma((LAYERS, 2)), dma((LAYERS, 2)), dma((num_saves,))]
    cot, result, x0, *rest = pl.pallas_call(
        partial(forward_kernel, dims, num_seqs),
        out_shape=outs,
        in_specs=[ANY] * 10 + [VMEM] * 4 + [SMEM],
        out_specs=[ANY] * len(outs),
        scratch_shapes=scratch,
        compiler_params=pltpu.CompilerParams(
            collective_id=0, has_side_effects=True, vmem_limit_bytes=VMEM_BYTES
        ),
        name="forward",
    )(inputs, cotangent, *weights, *vectors, lengths)
    units, arrays = rest[: len(shapes)], rest[len(shapes) :]
    saved = []
    for layer in range(LAYERS):
        saved.append({name: arrays.pop(0) for name in saved_names(layer)})
    return cot, result, x0, units, saved


SAVED = ("h", "q", "k", "v", "k1", "v1", "gate", "attn", "lse", "a", "x2", "y", "gf")


def backward_outs():
    outs = {"g" + n: shape for n, shape in grad_outs().items()}
    outs["dx2"] = tok(F32)
    outs["dza"] = tok(BF)
    outs["dq"] = tok(BF)
    outs["dk"] = tok(F32)
    outs["dv"] = tok(F32)
    outs["dk_out"] = tok(BF)
    outs["dv_out"] = tok(BF)
    outs["vg"] = jax.ShapeDtypeStruct((8, WIDTH), F32)
    return outs


UNIT_PLACE = {"q": 0, "k": 1, "v": 2, "o": 3, "ga": 4, "gf": 5, "up0": 6}


class PlainGrads:
    def __init__(self, a, b=None, d=None):
        self.a, self.b, self.d = a, b, d

    def unit(self, name, value):
        if name in UNIT_PLACE:
            self.a[UNIT_PLACE[name]] = value.astype(BF)
        else:
            self.b[int(name[2:]) - 1] = value.astype(BF)

    def down(self, n, value):
        self.d[0, n * WIDTH : (n + 1) * WIDTH, :] = value.astype(BF)


def run_backward(r, layer, dx_ref):
    s = SimpleNamespace(**{n: getattr(r, "s" + n) for n in SAVED})
    s.k = (r.sk, r.sk1)
    s.v = (r.sv, r.sv1)
    out = PlainGrads(r.ga, r.gb, r.gd)
    for name in ("dx2", "dza", "dq", "dk", "dv", "dk_out", "dv_out"):
        setattr(out, name, getattr(r, name))
    mask_setup(r, True)
    ffn_backward(r, r.w[layer], layer, dx_ref, s, out)
    attention_backward(r, s, out)


def backward_call(gathered, vec_in, lengths, layer, dx, saved):
    ins = {"vec_in": vec_in, "lengths": lengths, "dx": dx}
    ins.update({"s" + n: saved[n] for n in SAVED})

    def body(r):
        r.vg[...] = jnp.zeros_like(r.vg)
        run_backward(r, layer, r.dx)

    outs = backward_outs()
    got = compute_call(
        body, "backward", [(layer, BACK)], gathered, ins, outs, BACKWARD_SCRATCH
    )
    return dict(zip(outs, got))


def front_backward_call(gathered, vec_in, layer, saved, g, vec_grads, final):
    ins = {"vec_in": vec_in, "sx": saved["x"], "sh": saved["h"], "vg_in": vec_grads}
    ins.update({"g" + n: g[n] for n in ("dq", "dk", "dv", "dk_in", "dv_in", "dza", "dx2")})
    outs = {
        "qkv": jax.ShapeDtypeStruct((3, WIDTH, WIDTH), BF),
        "dx": tok(F32),
    }
    if final:
        outs["vg_t"] = jax.ShapeDtypeStruct((1, WIDTH, BLOCK), F32)
    else:
        outs["vg"] = jax.ShapeDtypeStruct((8, WIDTH), F32)
    scratch = {
        "dk": vm(TOKENS, WIDTH),
        "dv": vm(TOKENS, WIDTH),
        "hid_t": vm(WIDTH, TOKENS),
        "sums": vm(8, WIDTH, dtype=F32),
        "dh": vm(TOKENS, WIDTH, dtype=F32),
    }
    if final:
        scratch["vg"] = vm(8, WIDTH, dtype=F32)

    def body(r):
        r.vg[...] = r.vg_in[...]
        s = SimpleNamespace(x=r.sx, h=r.sh)
        gg = SimpleNamespace(
            dq=r.gdq, dk=r.gdk, dv=r.gdv, dk_in=r.gdk_in, dv_in=r.gdv_in, dza=r.gdza, dx2=r.gdx2
        )
        layer_front_backward(r, r.w[layer], layer, s, gg, PlainGrads(r.qkv), r.dx)
        if final:
            tall = jnp.concatenate(
                [r.vg[...], jnp.zeros((BLOCK - 8, WIDTH), F32)], axis=0
            )
            r.vg_t[0] = jnp.transpose(tall)

    got = compute_call(
        body, "front_backward", [(layer, FRONT)], gathered, ins, outs, scratch
    )
    return dict(zip(outs, got))


GRAD_SETS = (
    ("up_a", ("up0", "up1"), (2, 1)),
    ("up_b", ("up2", "up3"), (2, 1)),
    ("down", ("down",), (1, 2)),
    ("mix", ("gf", "o", "ga"), (1, 2)),
    ("q", ("q",), (2, 1)),
    ("kv", ("k", "v"), (1, 2)),
)
LATE_SETS = ("q", "kv")
RESULT_UNITS = ("q", "k", "v", "o", "ga", "gf", "up0", "up1", "up2", "up3")

EARLY_ARRAYS = ("x2", "y", "gf", "gate", "a", "attn_t", "hid_t")
STREAMED = ("act_t", "slope")
ATTENTION_ARRAYS = ("q", "k", "v", "k1", "v1", "lse")


TICKS = ("gf", "c0", "c1", "c2", "c3", "norm", "mix", "p0", "p1", "p2", "p3", "kv", "end")
SCHEDULE = {
    "c0": ((1, 3, "down"),),
    "c1": ((1, 2, "mix"), (1, 3, "up_b")),
    "c2": ((0, 1, "up_a"), (1, 2, "q")),
    "norm": ((0, 1, "up_b"), (0, 1, "down"), (1, 3, "mix"), (1, 2, "kv")),
    "mix": ((1, 3, "q"),),
    "p0": ((0, 2, "up_a"), (0, 1, "mix")),
    "p1": ((1, 4, "up_a"), (1, 4, "up_b"), (1, 4, "down"), (1, 4, "mix")),
    "p2": ((0, 2, "up_b"), (1, 3, "kv"), (1, 4, "q")),
    "p3": ((0, 2, "down"), (0, 3, "up_a")),
    "kv": ((0, 1, "q"),),
    "end": ((0, 1, "kv"),),
}
LAST = (
    (0, 3, "down"),
    (0, 1, "vec"),
    (0, 2, "mix"),
    (0, 2, "q"),
    (0, 3, "up_b"),
    (0, 2, "kv"),
    (0, 2, "vec"),
    (1, 4, "kv"),
    (0, 3, "mix"),
    (0, 3, "q"),
    (0, 4, "up_a"),
    (0, 4, "down"),
    (0, 4, "up_b"),
    (0, 3, "kv"),
    (0, 3, "vec"),
    (0, 4, "mix"),
    (0, 4, "q"),
    (0, 4, "kv"),
    (0, 4, "vec"),
)


def grad_set_list(dims, rows):
    out = []
    for layer in range(LAYERS):
        for name, units, order in GRAD_SETS:
            depth = 4 * rows if name == "down" else rows
            out.append((name, layer, units, order, (len(units), *dims, 2, depth, WIDTH), BF))
    out.append(("vec", 0, None, (1, 2), (1, *dims, 2, rows, BLOCK), F32))
    return out


class FusedGrads:
    def __init__(self, refs):
        self.refs = dict(zip((name for name, _, _ in GRAD_SETS), refs))
        self.place = {
            unit: (name, k) for name, units, _ in GRAD_SETS for k, unit in enumerate(units)
        }

    def unit(self, name, value):
        which, k = self.place[name]
        ref = self.refs[which]
        ref[k] = value.astype(BF).reshape(ref.shape[1:])

    def down(self, n, value):
        ref = self.refs["down"]
        part = ref.shape[1] // CHUNKS
        ref[0, n * part : (n + 1) * part] = value.astype(BF).reshape((part, *ref.shape[2:]))


BACKWARD_ARRAYS = {
    "x2": F32,
    "y": BF,
    "gf": F32,
    "gate": F32,
    "a": BF,
    "attn_t": BF,
    "hid_t": BF,
    "h_t": BF,
    "q": BF,
    "k": BF,
    "v": BF,
    "k1": BF,
    "v1": BF,
    "lse": F32,
}

FUSED_WORK = {
    "bias": BIAS_T,
    "dy": vm(TOKENS, WIDTH),
    "dz": vm(TOKENS, WIDTH),
    "act_t": vm(2, WIDTH, TOKENS),
    "slope": vm(2, TOKENS, WIDTH),
    "dh": vm(TOKENS, WIDTH, dtype=F32),
    "act": vm(TOKENS, WIDTH),
    "du": vm(TOKENS, WIDTH),
    "sums": vm(8, WIDTH, dtype=F32),
    "dattn": vm(TOKENS, WIDTH),
    "lse_t": vm(SLOTS, 8, BLOCK, dtype=F32),
    "dk_other": vm(TOKENS, BLOCK, dtype=F32),
    "dv_other": vm(TOKENS, BLOCK, dtype=F32),
    "vg": vm(8, WIDTH, dtype=F32),
    "vec": vm(8, WIDTH, dtype=F32),
    "dx": vm(TOKENS, WIDTH, dtype=F32),
    "dx2": vm(TOKENS, WIDTH, dtype=F32),
    "dza": vm(TOKENS, WIDTH),
    "dq": vm(TOKENS, WIDTH),
    "own_dk": vm(TOKENS, WIDTH, dtype=F32),
    "own_dv": vm(TOKENS, WIDTH, dtype=F32),
    "send_dk": vm(TOKENS, WIDTH),
    "send_dv": vm(TOKENS, WIDTH),
    "got_dk": vm(TOKENS, WIDTH),
    "got_dv": vm(TOKENS, WIDTH),
}


def backward_kernel(dims, num_seqs, *refs):
    refs = list(refs)

    def pop(count):
        out = refs[:count]
        del refs[:count]
        return out

    num_w = LAYERS * len(SETS)
    cot_in, x0_in, last_in = pop(3)
    weight_in = pop(num_w)
    saved_in = [{n: pop(1)[0] for n in saved_names(layer)} for layer in range(LAYERS)]
    (lengths,) = pop(1)
    res, res_down, res_vec, g_out, x_out = pop(5)
    weight_bufs = pop(len(SETS))
    (vec_buf,) = pop(1)
    bufs = dict(zip(BACKWARD_ARRAYS, pop(len(BACKWARD_ARRAYS))))
    r = SimpleNamespace(**dict(zip(FUSED_WORK, pop(len(FUSED_WORK)))))
    set_list = grad_set_list(dims, res_vec.shape[0])
    totals = pop(len(set_list))
    landings = pop(len(GRAD_SETS) + len(LATE_SETS) + 1)
    lines = pop(3 * len(set_list))
    sems = pop(6)
    weight_sem, array_sem, other_sem, stream_sem, dkv_send, dkv_recv = pop(6)
    back_sems = pop(3)
    r.lengths = lengths
    r.dk, r.dv, r.out = r.act, r.du, r.dattn

    place = Place(dims)
    core = place.core
    copies = {}

    def load(key, src, dst, sem):
        copy = pltpu.make_async_copy(src, dst, sem)
        copy.start()
        copies[key] = copy

    def need(*keys):
        for key in keys:
            copy = copies.pop(key, None)
            if copy is not None:
                copy.wait()

    unit_place = {
        name: (which, unit) for which, (names, _) in enumerate(SETS) for unit, name in enumerate(names)
    }
    flat_names = list(unit_place)

    def load_weights(layer, *names):
        for name in names:
            which, unit = unit_place[name]
            load(
                (layer, "w", name),
                weight_in[layer * len(SETS) + which].at[unit],
                weight_bufs[which].at[unit],
                weight_sem.at[layer, flat_names.index(name)],
            )

    array_names = list(BACKWARD_ARRAYS)

    def load_arrays(layer, *names):
        for name in names:
            src = saved_in[layer][name]
            load((layer, name), src, bufs[name], array_sem.at[layer, array_names.index(name)])

    def stream(layer, n):
        for k, name in enumerate(STREAMED):
            load(
                (layer, name, n),
                saved_in[layer][name].at[n],
                (r.act_t, r.slope)[k].at[n % 2],
                stream_sem.at[layer, k, n],
            )

    ffn_weights = ("gf", "o", "up0", "up1", "up2", "up3", "down")
    front_weights = ("q", "k", "v", "ga")
    last = LAYERS - 1
    load((last, "cot"), cot_in, r.dq, other_sem.at[0])
    load_arrays(last, "gf", "y", "x2", "hid_t")
    vec_src = weight_in[0].at[VEC_UNIT, :, :, :, :, :, pl.ds(0, BLOCK)]
    load("vec", vec_src, vec_buf, weight_sem.at[0, len(flat_names)])
    load_weights(last, *ffn_weights)
    stream(last, 0)
    stream(last, 1)
    load_arrays(last, "gate", "a", "attn_t", "h_t", *ATTENTION_ARRAYS)
    load_weights(last, *front_weights)
    load((last, "x"), saved_in[last - 1]["x3"], r.dx, other_sem.at[1])
    place.greet()

    def rows_of(ref):
        return lambda slot: ref.at[pl.ds(pl.multiple_of(slot * BLOCK, BLOCK), BLOCK)]

    back_x = TokenReturn(place, num_seqs, rows_of(last_in), x_out, back_sems, 1)
    back_x.start()

    sets = {}
    for k, (name, layer, units, order, _, _) in enumerate(set_list):

        def result(u, value, name=name, layer=layer, units=units):
            if name == "vec":
                res_vec[...] = value
            elif name == "down":
                res_down[layer] = value
            else:
                res[layer, RESULT_UNITS.index(units[u])] = value

        sets[(layer, name)] = PairReduce(
            place,
            totals[k],
            order,
            [landings[landing_index(name, layer)], *lines[3 * k : 3 * k + 3]],
            set_sems(sems, k),
            result,
        )
    stages = (None, "stage1", "stage2", "stage3", "finish")

    def act(layer, *events):
        for before, stage, name in events:
            if layer + before < LAYERS:
                getattr(sets[(layer + before, name)], stages[stage])()

    def ticker(layer):
        names = iter(TICKS)
        return lambda: act(layer, *SCHEDULE.get(next(names), ()))

    def ready_for(layer):
        def ready(*names):
            for name in names:
                sets[(layer, name)].start()

        return ready

    mask_setup(r, True)
    need("vec")
    r.vec[...] = jnp.transpose(vec_buf[...].reshape(WIDTH, BLOCK).astype(F32))[0:8, :]

    w = Gathered(weight_bufs)
    exchanges = []
    for layer in range(last, -1, -1):
        s = SimpleNamespace(**bufs)
        s.k = (bufs["k"], bufs["k1"])
        s.v = (bufs["v"], bufs["v1"])
        out = FusedGrads(totals[layer * len(GRAD_SETS) : (layer + 1) * len(GRAD_SETS)])
        out.dx2, out.dza, out.dq = r.dx2, r.dza, r.dq
        out.dk, out.dv, out.dk_out, out.dv_out = r.own_dk, r.own_dv, r.send_dk, r.send_dv
        dx_in = r.dq if layer == last else r.dx
        need((layer, "cot"), *((layer, n) for n in EARLY_ARRAYS), (layer, "h_t"))
        need(*((layer, "w", n) for n in ffn_weights))
        ready = ready_for(layer)
        tick = ticker(layer)

        def take(n, layer=layer):
            need((layer, "act_t", n), (layer, "slope", n))

        def drop(n, layer=layer):
            if n + 2 < CHUNKS:
                stream(layer, n + 2)
            elif layer:
                stream(layer - 1, n + 2 - CHUNKS)

        kept = SimpleNamespace(
            hid_t=bufs["hid_t"],
            attn_t=bufs["attn_t"],
            h_t=bufs["h_t"],
            act_t=lambda n: r.act_t.at[n % 2],
            slope=lambda n: r.slope.at[n % 2],
            take=take,
            drop=drop,
        )
        ffn_backward(r, w, layer, dx_in, s, out, tick, ready, kept)
        if layer:
            load_arrays(layer - 1, *EARLY_ARRAYS)
            load_weights(layer - 1, *ffn_weights)
        else:
            load((0, "x"), x0_in, r.dz, other_sem.at[2])
        need(*((layer, n) for n in ATTENTION_ARRAYS))
        for copy in exchanges:
            copy.wait_send()
        attention_backward(r, s, out, tick)
        if layer:
            load_arrays(layer - 1, *ATTENTION_ARRAYS)
        exchanges = []
        for k, (src, dst) in enumerate(((r.send_dk, r.got_dk), (r.send_dv, r.got_dv))):
            copy = remote(
                src,
                dst,
                dkv_send.at[layer, k],
                dkv_recv.at[layer, k],
                place.sibling(),
            )
            copy.start()
            exchanges.append(copy)
        need(*((layer, "w", n) for n in front_weights), (layer, "x"))
        g = SimpleNamespace(
            dq=r.dq,
            dk=r.own_dk,
            dv=r.own_dv,
            dk_in=r.got_dk,
            dv_in=r.got_dv,
            dza=r.dza,
            dx2=r.dx2,
        )

        def arrived(pair=tuple(exchanges)):
            for copy in pair:
                copy.wait_recv()

        s.x = r.dx if layer else r.dz
        layer_front_backward(r, w, layer, s, g, out, r.dx, arrived, tick, ready, bufs["h_t"])
        if layer:
            load_arrays(layer - 1, "h_t")
            load_weights(layer - 1, *front_weights)

    r.out[...] = r.dx[...].astype(BF)
    back = TokenReturn(place, num_seqs, rows_of(r.out), g_out, back_sems, 0)
    back.start()
    tall = jnp.concatenate([r.vg[...], jnp.zeros((BLOCK - 8, WIDTH), F32)], axis=0)
    totals[-1][0] = jnp.transpose(tall).reshape(totals[-1].shape[1:])
    ready_for(0)("vec")
    act(0, *LAST)
    for one in sets.values():
        one.finish_sends()
    for copy in exchanges:
        copy.wait_send()
    back.finish()
    back_x.finish()


def landing_index(name, layer):
    names = [one[0] for one in GRAD_SETS]
    if name == "vec":
        return len(names) + len(LATE_SETS)
    if name in LATE_SETS and layer:
        return len(names) + LATE_SETS.index(name)
    return names.index(name)


def backward(dims, rows, lengths, positions, cot, x0, result, units, saved):
    num_seqs = lengths.shape[0]
    per_dev = positions // BLOCK
    dma = pltpu.SemaphoreType.DMA
    scratch = [
        vm(len(names), *dims, 2, 4 * rows if names[0] == "down" else rows, WIDTH) for names, _ in SETS
    ]
    scratch += [vm(*dims, 2, rows, BLOCK)]
    scratch += [vm(*layer_shape(n), dtype=t) for n, t in BACKWARD_ARRAYS.items()]
    scratch += list(FUSED_WORK.values())
    set_list = grad_set_list(dims, rows)
    scratch += [vm(*s, dtype=t) for *_, s, t in set_list]
    landings, lines = {}, []
    for name, layer, _, order, (count, num_z, num_x, num_y, _, *block), dtype in set_list:
        landings[landing_index(name, layer)] = vm(count, num_z, num_x, num_y, *block, dtype=dtype)
        lines.append(vm(count, num_z, 2, *block, dtype=dtype))
        lines.append(vm(count, num_z, *block, dtype=dtype))
        lines.append(vm(num_z - 1, count, *block, dtype=dtype))
    scratch += [landings[k] for k in sorted(landings)] + lines
    scratch += pair_reduce_sems(len(set_list))
    scratch += [
        dma((LAYERS, 16)),
        dma((LAYERS, len(BACKWARD_ARRAYS))),
        dma((3,)),
        dma((LAYERS, 2, CHUNKS)),
        dma((LAYERS, 2)),
        dma((LAYERS, 2)),
    ]
    scratch += return_sems(2, num_seqs, per_dev)
    arrays = [saved[layer][n] for layer in range(LAYERS) for n in saved_names(layer)]
    return pl.pallas_call(
        partial(backward_kernel, dims, num_seqs),
        out_shape=[
            jax.ShapeDtypeStruct((LAYERS, len(RESULT_UNITS), rows, WIDTH), F32),
            jax.ShapeDtypeStruct((LAYERS, 4 * rows, WIDTH), F32),
            jax.ShapeDtypeStruct((rows, BLOCK), F32),
            jax.ShapeDtypeStruct((num_seqs, positions, WIDTH), BF),
            jax.ShapeDtypeStruct((num_seqs, positions, WIDTH), BF),
        ],
        in_specs=[ANY] * (3 + len(units) + len(arrays)) + [SMEM],
        out_specs=[VMEM] * 3 + [ANY] * 2,
        scratch_shapes=scratch,
        compiler_params=pltpu.CompilerParams(
            collective_id=1, has_side_effects=True, vmem_limit_bytes=BACKWARD_VMEM
        ),
        name="backward",
    )(cot, x0, result, *units, *arrays, lengths)


def unpack_kernel(*refs):
    res, res_down, res_vec, x_in, g_in = refs[:5]
    x_out, g_out = refs[5:7]
    ga, wq, wk, wv, wo, wga, ba, gf, wup, wdown, wgf, bf = refs[7:19]
    square = refs[19]
    x_out[...] = x_in[...]
    g_out[...] = g_in[...].astype(F32)
    plain = {"q": wq, "k": wk, "v": wv, "o": wo, "ga": wga, "gf": wgf}
    for layer in range(LAYERS):
        for k, name in enumerate(RESULT_UNITS):
            if name in plain:
                plain[name][layer] = res[layer, k]
            else:
                n = int(name[2:])
                wup[layer, :, n * WIDTH : (n + 1) * WIDTH] = res[layer, k]
        wdown[layer] = res_down[layer]
    rows = res_vec.shape[0]
    square[...] = jnp.zeros_like(square)
    square[0:rows, :] = res_vec[...]
    turned = jnp.transpose(square[...])
    for layer in range(LAYERS):
        for which, ref in enumerate((ga, ba, gf, bf)):
            row = layer * 4 + which
            ref[layer : layer + 1, :] = turned[row : row + 1, 0:rows]


def unpack(res, res_down, res_vec, x_out, g_out):
    rows = res_vec.shape[0]
    vector = jax.ShapeDtypeStruct((LAYERS, rows), F32)
    matrix = jax.ShapeDtypeStruct((LAYERS, rows, WIDTH), F32)
    outs = [
        jax.ShapeDtypeStruct(x_out.shape, x_out.dtype),
        jax.ShapeDtypeStruct(g_out.shape, F32),
        vector,
        matrix,
        matrix,
        matrix,
        matrix,
        matrix,
        vector,
        vector,
        jax.ShapeDtypeStruct((LAYERS, rows, CHUNKS * WIDTH), F32),
        jax.ShapeDtypeStruct((LAYERS, CHUNKS * rows, WIDTH), F32),
        matrix,
        vector,
    ]
    return pl.pallas_call(
        unpack_kernel,
        out_shape=outs,
        in_specs=[VMEM] * 5,
        out_specs=[VMEM] * 14,
        scratch_shapes=[vm(BLOCK, BLOCK, dtype=F32)],
        name="unpack",
    )(res, res_down, res_vec, x_out, g_out)


def plain_forward(gathered, vec_in, lengths, x_tok, exchange):
    x = x_tok.reshape(TOKENS, WIDTH)
    front = front_call(gathered, vec_in, 0, x)
    saved = []
    for layer in range(LAYERS):
        front["k1"], front["v1"] = exchange(front["k"], front["v"])
        got = middle_call(gathered, vec_in, lengths, layer, x, front)
        keep = dict(front)
        keep.update({n: got[n] for n in ("attn", "lse", "a", "x2", "y", "gf")})
        keep["x"] = x
        saved.append(keep)
        x = got["x3"]
        front = {n[1:]: got[n] for n in ("nh", "nq", "nk", "nv", "ngate") if n in got}
    return saved, x.astype(BF).reshape(SLOTS, BLOCK, WIDTH)


def per_device(num_dp, num_sp, *args):
    inputs, lengths, gain_a, wq, wk, wv, wo, wga, ba, gain_f, wup, wdown, wgf, bf, cotangent = args
    num_y = num_sp // 2
    num_x = num_y
    dims = (num_dp // num_x, num_x, num_y)
    rows = wq.shape[1]
    weights = (wq, wk, wv, wo, wga, wgf, wup, wdown)
    if rows % 16 == 0 and dims[0] % CHUNKS == 0 and num_x == num_y == 2:
        cot, last, x0, units, saved = forward(
            dims, inputs, cotangent, weights, (gain_a, ba, gain_f, bf), lengths
        )
        *summed, g_out, x_out = backward(
            dims, rows, lengths, inputs.shape[1], cot, x0, last, units, saved
        )
        return tuple(unpack(*summed, x_out, g_out))
    vectors = jnp.stack(
        [v[layer] for layer in range(LAYERS) for v in (gain_a, ba, gain_f, bf)], axis=1
    )
    vecs = jnp.pad(vectors, ((0, 0), (0, WIDTH - vectors.shape[1])))
    x_tok, cot_tok, *units = collect(dims, inputs, cotangent, weights, vecs)
    gathered = {}
    for layer in range(LAYERS):
        gathered[layer] = [
            u.reshape(u.shape[0], -1, WIDTH)
            for u in units[len(SETS) * layer : len(SETS) * (layer + 1)]
        ]
    vec_in = gathered[0][0][VEC_UNIT, :, :BLOCK]

    swap = [(i, i ^ 1) for i in range(num_sp)]

    def exchange(*arrays):
        return [lax.ppermute(a, "sp", swap) for a in arrays]

    saved, layer_out = plain_forward(gathered, vec_in, lengths, x_tok, exchange)

    dx = cot_tok.reshape(TOKENS, WIDTH)
    vec_grads = None
    grads = [None] * LAYERS
    for layer in reversed(range(LAYERS)):
        g = backward_call(gathered, vec_in, lengths, layer, dx, saved[layer])
        g["dk_in"], g["dv_in"] = exchange(g["dk_out"], g["dv_out"])
        vec_grads = g["vg"] if vec_grads is None else vec_grads + g["vg"]
        got = front_backward_call(gathered, vec_in, layer, saved[layer], g, vec_grads, layer == 0)
        dx = got["dx"]
        grads[layer] = (
            jnp.concatenate([got["qkv"], g["ga"][3:]], axis=0),
            g["gb"],
            g["gd"],
        )
        vec_grads = got["vg"] if layer else got["vg_t"]

    flat = [arr for layer in range(LAYERS) for arr in grads[layer]] + [vec_grads]
    toks = [dx.reshape(SLOTS, BLOCK, WIDTH), layer_out]
    *summed, g_out, x_out = spread(dims, inputs.shape[0], flat, toks)
    a, b, d = ([summed[3 * layer + k] for layer in range(LAYERS)] for k in range(3))

    def unit(k):
        return jnp.stack([a[layer][k] for layer in range(LAYERS)])

    def vector(which):
        return jnp.stack([summed[6][0, :, layer * 4 + which] for layer in range(LAYERS)])

    grad_up = jnp.stack(
        [
            jnp.concatenate([a[layer][6], b[layer][0], b[layer][1], b[layer][2]], axis=1)
            for layer in range(LAYERS)
        ]
    )
    grad_down = jnp.stack([d[layer][0] for layer in range(LAYERS)])
    return (
        x_out,
        g_out,
        vector(0),
        unit(0),
        unit(1),
        unit(2),
        unit(3),
        unit(4),
        vector(1),
        vector(2),
        grad_up,
        grad_down,
        unit(5),
        vector(3),
    )


def solution(mesh):
    tokens = P("dp", "sp", None)
    vector = P(None, ("dp", "sp"))
    matrix = P(None, ("dp", "sp"), None)
    return jax.shard_map(
        partial(per_device, mesh.shape["dp"], mesh.shape["sp"]),
        mesh=mesh,
        in_specs=(
            tokens,
            P("dp", None),
            vector,
            matrix,
            matrix,
            matrix,
            matrix,
            matrix,
            vector,
            vector,
            matrix,
            matrix,
            matrix,
            vector,
            tokens,
        ),
        out_specs=(
            tokens,
            tokens,
            vector,
            matrix,
            matrix,
            matrix,
            matrix,
            matrix,
            vector,
            vector,
            matrix,
            matrix,
            matrix,
            vector,
        ),
        check_vma=False,
    )
```
